512 devices in a mesh: dp: 128 (over z, y, core), fsdp: 4 (over x).
Axes of the slice: x: 4, y: 4, z: 16, core: 2. Of those that a mesh axis runs over, the one named last changes fastest.
Arguments:
- tiles: bfloat16 [768, 65536], P('fsdp', 'dp'), may hold values from -6 to 6
- kernel: bfloat16 [49, 768], P(None, 'fsdp'), may hold values from -0.875 to 0.875
- norm_gain: bfloat16 [768], P('fsdp'), may hold values from 0.099609375 to 1.8984375
- w_up: bfloat16 [768, 1536], P('dp', 'fsdp'), may hold values from -0.21875 to 0.21875
- w_down: bfloat16 [768, 1536], P('dp', 'fsdp'), may hold values from -0.15625 to 0.15625
- layer_scale: bfloat16 [768], P('fsdp'), may hold values from 0.5 to 2
- neighbors: int32 [1024, 4, 2], P('dp'), may hold values from -1 to 1023, as said below
- shifts: int32 [1024, 4, 2], P('dp'), may hold values from -8 to 7, as said below
- halo_widths: int32 [1024, 4], P('dp'), may hold values from 1 to 3
- land: int32 [1024, 8, 8], P('dp'), may hold values 0 or 1
- cotangent: bfloat16 [768, 65536], P('fsdp', 'dp'), may hold values from -6 to 6
Outputs:
- block_out: bfloat16 [768, 65536], P('fsdp', 'dp')
- tile_grad: bfloat16 [768, 65536], P('fsdp', 'dp')
- up_grad: float32 [768, 1536], P('dp', 'fsdp')
- down_grad: float32 [768, 1536], P('dp', 'fsdp')
The draws below stay inside these ranges and needn't reach their ends.
Inputs may be any that keep to these rules, and one draw needn't show every extreme that they name: `neighbors`: faces are north, south, west, east. Tile t is held by index t // 8 of dp. A named north or south neighbour is held by the same index of dp as the tile, a west one by the index before, an east one by the index after. Adjacency is symmetric: a cell taken from a neighbour's edge belongs to the tile that takes the facing cell of it. Entry 0 of a face holds shifts 0 to 7, entry 1 shifts -8 to -1; an entry that names no tile has shift 0, and north and south shifts are 0.
All inputs are finite; a program needn't handle non-finite values. No bound on the sum of `land` on one device may be relied on, other than what follows from the above.
Results may differ from the reference program's by a relative error of at most 0.0095.
Values may be sent and summed in bfloat16 or wider, within the bound.
A program may use at most 64 MiB of HBM per device.

```python
import math
import jax
import jax.numpy as jnp
from jax import lax

WIDTH = 768
HIDDEN_SIZE = 1536
KSIZE = 7
SIDE = 8
TILE_DEV = 8
TILES = 1024
N_FSDP = 4


def tile_layout(key):
    columns = TILES // TILE_DEV
    scores = jax.random.randint(jax.random.fold_in(key, 11), (columns, TILE_DEV), 0, 1 << 20) * TILE_DEV + jnp.arange(TILE_DEV, dtype=jnp.int32)[None, :]
    row_of_slot = jnp.argsort(scores, axis=1).astype(jnp.int32)
    slot_of_row = jnp.argsort(row_of_slot, axis=1).astype(jnp.int32)
    base_row = jax.random.randint(jax.random.fold_in(key, 7), (columns,), 0, SIDE).astype(jnp.int32)
    tile_index = jnp.arange(TILES, dtype=jnp.int32)
    column = tile_index // TILE_DEV
    tile_row = row_of_slot[column, tile_index % TILE_DEV]
    none_tile = jnp.full((TILES,), -1, jnp.int32)
    zero_shift = jnp.zeros((TILES,), jnp.int32)
    owner_list = []
    shift_list = []
    for step_row in (-1, 1):
        other_row = tile_row + step_row
        inside = (other_row >= 0) & (other_row < TILE_DEV)
        named = column * TILE_DEV + slot_of_row[column, jnp.clip(other_row, 0, TILE_DEV - 1)]
        owner_list.append(jnp.stack([jnp.where(inside, named, -1), none_tile], axis=1))
        shift_list.append(jnp.stack([zero_shift, zero_shift], axis=1))
    for step_col in (-1, 1):
        other_col = column + step_col
        col_inside = (other_col >= 0) & (other_col < columns)
        safe_col = jnp.clip(other_col, 0, columns - 1)
        start_row = base_row[column] - base_row[safe_col] + SIDE * tile_row
        first_row = start_row // SIDE
        first_shift = start_row - SIDE * first_row
        entries = []
        moves = []
        for which_entry in range(2):
            near_row = first_row + which_entry
            inside = col_inside & (near_row >= 0) & (near_row < TILE_DEV)
            named = safe_col * TILE_DEV + slot_of_row[safe_col, jnp.clip(near_row, 0, TILE_DEV - 1)]
            entries.append(jnp.where(inside, named, -1))
            moves.append(jnp.where(inside, first_shift - SIDE * which_entry, 0))
        owner_list.append(jnp.stack(entries, axis=1))
        shift_list.append(jnp.stack(moves, axis=1))
    return (jnp.stack(owner_list, axis=1).astype(jnp.int32), jnp.stack(shift_list, axis=1).astype(jnp.int32))


def draw_neighbors(key, part):
    return tile_layout(key)[0]


def draw_shifts(key, part):
    return tile_layout(key)[1]


def touch_ends(drawn, own_key, smallest, largest):
    longest = drawn.shape.index(max(drawn.shape))
    spots = []
    for shift in (0, 1):
        where = [jax.random.randint(jax.random.fold_in(own_key, axis), (), 0, length) for axis, length in enumerate(drawn.shape)]
        where[longest] = (where[longest] + shift) % drawn.shape[longest]
        spots.append(tuple(where))
    return drawn.at[spots[0]].set(smallest).at[spots[1]].set(largest)


def block_levels(key, shape, pieces, smallest, top_value):
    def one(axis_at, shards_of):
        heights = jax.random.uniform(jax.random.fold_in(jax.random.fold_in(key, 6), axis_at), (shards_of,), jnp.float32, smallest / len(pieces), top_value / len(pieces))
        return jnp.repeat(jnp.exp(heights), shape[axis_at] // shards_of).reshape((-1,) + (1,) * (len(shape) - axis_at - 1))

    loudness = one(*pieces[0])
    for cut in pieces[1:]:
        loudness = loudness * one(*cut)
    return loudness


def gaussian(own_key, dims, deviation, limit, shards=(), held_as=jnp.bfloat16):
    values = jax.random.normal(own_key, dims, jnp.float32) * deviation
    if len(shards) > 0:
        values = block_levels(own_key, dims, shards, -0.22, 0.18) * values
    return jnp.clip(values, min=-limit, max=limit).astype(held_as)


def setup_inputs(seed: int = 0) -> dict:
    streams_of = jax.random.split(jax.random.key(seed), 12)
    tiles = gaussian(streams_of[0], (WIDTH, TILES * SIDE * SIDE), 1.0, 6.0, ((0, 4), (1, 128)))
    kernel = gaussian(streams_of[1], (KSIZE * KSIZE, WIDTH), (KSIZE * KSIZE) ** -0.5, 0.875, ((1, 4),))
    norm_gain = jnp.clip(1.0 + 0.18 * jax.random.normal(streams_of[2], (WIDTH,), jnp.float32), 0.099609375, 1.8984375).astype(jnp.bfloat16)
    w_up = gaussian(streams_of[3], (WIDTH, HIDDEN_SIZE), WIDTH ** -0.5, 0.21875, ((0, 128), (1, 4)))
    w_down = gaussian(streams_of[4], (WIDTH, HIDDEN_SIZE), HIDDEN_SIZE ** -0.5, 0.15625, ((0, 128), (1, 4)))
    layer_scale = jnp.clip(jnp.exp(math.log(2.0) - 1.3862944 * jax.random.uniform(streams_of[5], (WIDTH,), jnp.float32) ** block_levels(streams_of[5], (WIDTH,), ((0, 4),), -0.2, 0.2)), 0.5, 2.0).astype(jnp.bfloat16)
    neighbors = draw_neighbors(jax.random.fold_in(streams_of[11], 71), 0)
    shifts = draw_shifts(jax.random.fold_in(streams_of[11], 71), 0)
    halo_widths = touch_ends(jax.random.randint(streams_of[8], (TILES, 4), 1, 4), jax.random.fold_in(streams_of[8], 1), 1, 3).astype(jnp.int32)
    land = touch_ends((jax.random.randint(streams_of[9], (TILES, SIDE, SIDE), 0, 4) < 3).astype(jnp.int32), jax.random.fold_in(streams_of[9], 1), 0, 1)
    cotangent = gaussian(streams_of[10], (WIDTH, TILES * SIDE * SIDE), 1.0, 6.0, ((0, 4), (1, 128)))
    return {"tiles": tiles, "kernel": kernel, "norm_gain": norm_gain, "w_up": w_up, "w_down": w_down, "layer_scale": layer_scale, "neighbors": neighbors, "shifts": shifts, "halo_widths": halo_widths, "land": land, "cotangent": cotangent}


root_half = 1.0 / math.sqrt(2.0)
root_tau = 1.0 / math.sqrt(2.0 * math.pi)

def gelu_value(hidden):
    return 0.5 * hidden * (1.0 + jax.scipy.special.erf(hidden * root_half))

def gelu_slope(hidden):
    return 0.5 * (1.0 + jax.scipy.special.erf(hidden * root_half)) + hidden * jnp.exp(-0.5 * hidden * hidden) * root_tau

def depth_keep(widths_face, far_first):
    layer_index = jnp.arange(3, dtype=jnp.int32)
    if far_first:
        depth_value = 3 - layer_index
    else:
        depth_value = layer_index + 1
    return depth_value[None, :] <= widths_face[:, None]

def face_sources(tiles):
    side_len = tiles.shape[1]
    return (jnp.transpose(tiles[:, side_len - 3:], (0, 2, 1, 3)), jnp.transpose(tiles[:, :3], (0, 2, 1, 3)), tiles[:, :, side_len - 3:], tiles[:, :, :3])

def assemble(tiles, halos):
    tile_count = tiles.shape[0]
    channels = tiles.shape[3]
    corner = jnp.zeros((tile_count, 3, 3, channels), tiles.dtype)
    upper = jnp.concatenate([corner, jnp.transpose(halos[0], (0, 2, 1, 3)), corner], axis=2)
    lower = jnp.concatenate([corner, jnp.transpose(halos[1], (0, 2, 1, 3)), corner], axis=2)
    middle = jnp.concatenate([halos[2], tiles, halos[3]], axis=2)
    return jnp.concatenate([upper, middle, lower], axis=1)

def depthwise(padded, kernel):
    side_len = padded.shape[1] - 6
    taps = kernel.astype(jnp.float32)
    summed = jnp.zeros((padded.shape[0], side_len, side_len, padded.shape[3]), jnp.float32)
    for row_tap in range(7):
        for col_tap in range(7):
            window = padded[:, row_tap:row_tap + side_len, col_tap:col_tap + side_len, :].astype(jnp.float32)
            summed = summed + window * taps[row_tap * 7 + col_tap]
    return summed

def depthwise_back(grad_conv, kernel):
    side_len = grad_conv.shape[1]
    taps = kernel.astype(jnp.float32)
    spread = jnp.pad(grad_conv.astype(jnp.float32), ((0, 0), (6, 6), (6, 6), (0, 0)))
    summed = jnp.zeros((grad_conv.shape[0], side_len + 6, side_len + 6, grad_conv.shape[3]), jnp.float32)
    for row_tap in range(7):
        for col_tap in range(7):
            window = spread[:, 6 - row_tap:12 - row_tap + side_len, 6 - col_tap:12 - col_tap + side_len, :]
            summed = summed + window * taps[row_tap * 7 + col_tap]
    return summed

def pick_halo(source, neighbor_ids, shift_values):
    side_len = source.shape[1]
    position = jnp.arange(side_len, dtype=jnp.int32)
    summed = jnp.zeros(source.shape, jnp.float32)
    for which_entry in range(2):
        owner_tile = neighbor_ids[:, which_entry]
        along_edge = position[None, :] + shift_values[:, which_entry][:, None]
        is_valid = (owner_tile[:, None] >= 0) & (along_edge >= 0) & (along_edge < side_len)
        gathered = source[jnp.maximum(owner_tile, 0)]
        picked = jnp.take_along_axis(gathered, jnp.clip(along_edge, 0, side_len - 1)[:, :, None, None], axis=1)
        summed = summed + jnp.where(is_valid[:, :, None, None], picked.astype(jnp.float32), 0.0)
    return summed

def return_halo(grad_face, neighbor_ids, shift_values):
    side_len = grad_face.shape[1]
    position = jnp.arange(side_len, dtype=jnp.int32)
    summed = jnp.zeros(grad_face.shape, jnp.float32)
    for which_entry in range(2):
        owner_tile = neighbor_ids[:, which_entry]
        along_edge = position[None, :] + shift_values[:, which_entry][:, None]
        is_valid = (owner_tile[:, None] >= 0) & (along_edge >= 0) & (along_edge < side_len)
        moving = jnp.where(is_valid[:, :, None, None], grad_face, 0.0)
        summed = summed.at[jnp.maximum(owner_tile, 0)[:, None], jnp.clip(along_edge, 0, side_len - 1)].add(moving)
    return summed

def reference(tiles, kernel, norm_gain, w_up, w_down, layer_scale, neighbors, shifts, halo_widths, land, cotangent):
    channels = tiles.shape[0]
    tile_count, side_len = (land.shape[0], land.shape[1])
    tiles_grid = jnp.transpose(tiles.reshape(channels, tile_count, side_len, side_len), (1, 2, 3, 0))
    cotangent_grid = jnp.transpose(cotangent.reshape(channels, tile_count, side_len, side_len), (1, 2, 3, 0))
    row_count = tile_count * side_len * side_len
    sources = face_sources(tiles_grid)
    halos = []
    masks = []
    for face_index in range(4):
        keep_mask = depth_keep(halo_widths[:, face_index], face_index in (0, 2))[:, None, :, None]
        masks.append(keep_mask)
        picked = pick_halo(sources[face_index], neighbors[:, face_index], shifts[:, face_index])
        halos.append(jnp.where(keep_mask, picked, 0.0).astype(jnp.bfloat16))
    conv = depthwise(assemble(tiles_grid, halos), kernel)
    conv_rows = conv.reshape(row_count, channels).astype(jnp.bfloat16)
    values = lax.optimization_barrier(conv_rows).astype(jnp.float32)
    row_mean = lax.optimization_barrier(jnp.sum(values, axis=1)) / channels
    row_square = lax.optimization_barrier(jnp.sum(values * values, axis=1)) / channels
    inv_scale = lax.rsqrt(row_square - row_mean * row_mean + 1e-06)
    centered = (values - row_mean[:, None]) * inv_scale[:, None]
    gain_f = norm_gain.astype(jnp.float32)
    normed = (centered * gain_f).astype(jnp.bfloat16)
    pre_act = jnp.dot(normed, w_up, preferred_element_type=jnp.float32)
    hidden = gelu_value(pre_act).astype(jnp.bfloat16)
    block_size = w_up.shape[1] // N_FSDP
    mixed = jnp.zeros((row_count, channels), jnp.float32)
    for block_index in range(N_FSDP):
        lower_edge = block_index * block_size
        partial_out = jnp.dot(hidden[:, lower_edge:lower_edge + block_size], w_down[:, lower_edge:lower_edge + block_size].T, preferred_element_type=jnp.float32)
        mixed = mixed + lax.optimization_barrier(partial_out.astype(jnp.bfloat16)).astype(jnp.float32)
    scale_f = layer_scale.astype(jnp.float32)
    block_out = (tiles_grid.reshape(row_count, channels).astype(jnp.float32) + scale_f * mixed).astype(jnp.bfloat16).reshape(tiles_grid.shape)
    grad_out = cotangent_grid * land[:, :, :, None].astype(jnp.bfloat16)
    grad_mixed = (scale_f * grad_out.reshape(row_count, channels).astype(jnp.float32)).astype(jnp.bfloat16)
    down_grad = jnp.dot(grad_mixed.T, hidden, preferred_element_type=jnp.float32)
    grad_hidden = jnp.dot(grad_mixed, w_down, preferred_element_type=jnp.float32)
    grad_pre = (grad_hidden * gelu_slope(pre_act)).astype(jnp.bfloat16)
    up_grad = jnp.dot(normed.T, grad_pre, preferred_element_type=jnp.float32)
    grad_normed = jnp.zeros((row_count, channels), jnp.float32)
    for block_index in range(N_FSDP):
        lower_edge = block_index * block_size
        partial_grad = jnp.dot(grad_pre[:, lower_edge:lower_edge + block_size], w_up[:, lower_edge:lower_edge + block_size].T, preferred_element_type=jnp.float32)
        grad_normed = grad_normed + lax.optimization_barrier(partial_grad.astype(jnp.bfloat16)).astype(jnp.float32)
    grad_centered = grad_normed * gain_f
    first_mean = lax.optimization_barrier(jnp.sum(grad_centered, axis=1)) / channels
    second_mean = lax.optimization_barrier(jnp.sum(grad_centered * centered, axis=1)) / channels
    grad_conv = (inv_scale[:, None] * (grad_centered - first_mean[:, None] - centered * second_mean[:, None])).astype(jnp.bfloat16)
    grad_pad = depthwise_back(grad_conv.reshape(conv.shape), kernel)
    inner = slice(3, 3 + side_len)
    tile_grad = grad_out.astype(jnp.float32) + grad_pad[:, inner, inner]
    edge_north = return_halo(jnp.where(masks[0], jnp.transpose(grad_pad[:, 0:3, inner], (0, 2, 1, 3)), 0.0), neighbors[:, 0], shifts[:, 0])
    tile_grad = tile_grad + jnp.pad(jnp.transpose(edge_north, (0, 2, 1, 3)), ((0, 0), (side_len - 3, 0), (0, 0), (0, 0)))
    edge_south = return_halo(jnp.where(masks[1], jnp.transpose(grad_pad[:, side_len + 3:, inner], (0, 2, 1, 3)), 0.0), neighbors[:, 1], shifts[:, 1])
    tile_grad = tile_grad + jnp.pad(jnp.transpose(edge_south, (0, 2, 1, 3)), ((0, 0), (0, side_len - 3), (0, 0), (0, 0)))
    edge_west = return_halo(jnp.where(masks[2], grad_pad[:, inner, 0:3], 0.0), neighbors[:, 2], shifts[:, 2])
    tile_grad = tile_grad + jnp.pad(edge_west, ((0, 0), (0, 0), (side_len - 3, 0), (0, 0)))
    edge_east = return_halo(jnp.where(masks[3], grad_pad[:, inner, side_len + 3:], 0.0), neighbors[:, 3], shifts[:, 3])
    tile_grad = tile_grad + jnp.pad(edge_east, ((0, 0), (0, 0), (0, side_len - 3), (0, 0)))
    block_flat = jnp.transpose(block_out, (3, 0, 1, 2)).reshape(channels, row_count)
    grad_flat = jnp.transpose(tile_grad.astype(jnp.bfloat16), (3, 0, 1, 2)).reshape(channels, row_count)
    return (block_flat, grad_flat, up_grad, down_grad)
```

```python
import functools
import math

import jax
import jax.numpy as jnp
from jax import lax
from jax.experimental import pallas as pl
from jax.experimental.pallas import tpu as pltpu
from jax.sharding import PartitionSpec as P

root_half = 1.0 / math.sqrt(2.0)
root_tau = 1.0 / math.sqrt(2.0 * math.pi)


N_Z, N_Y, N_CORE = 16, 4, 2
GROUP = N_Y * N_CORE
MESH = pl.DeviceIdType.MESH
RIGHT_STEPS = N_Z // 2
LEFT_STEPS = N_Z - 1 - RIGHT_STEPS


def dp_index(z, y, core):
    return (z * N_Y + y) * N_CORE + core


def own_place():
    me = lax.axis_index("dp")
    return me // GROUP, (me // N_CORE) % N_Y, me % N_CORE


def remote(src, dst, send_sem, recv_sem, dp, fs):
    return pltpu.make_async_remote_copy(
        src_ref=src,
        dst_ref=dst,
        send_sem=send_sem,
        recv_sem=recv_sem,
        device_id=(dp, fs),
        device_id_type=MESH,
    )


def weights_kernel(
    rows, shard_ref, up_ref, down_ref, units, full,
    unit_send, unit_recv, right_send, right_recv, left_send, left_recv, sib_send, sib_recv,
):
    z, y, core = own_place()
    fs = lax.axis_index("fsdp")
    group = y * N_CORE + core
    right = dp_index((z + 1) % N_Z, y, core)
    left = dp_index((z + N_Z - 1) % N_Z, y, core)
    sibling = dp_index(z, y, 1 - core)

    def mate(k):
        other = (group + k) % GROUP
        return dp_index(z, other // N_CORE, other % N_CORE)

    barrier = pltpu.get_barrier_semaphore()
    for k in range(1, GROUP):
        pl.semaphore_signal(barrier, inc=1, device_id=(mate(k), fs), device_id_type=MESH)
    for other in (right, left):
        pl.semaphore_signal(barrier, inc=1, device_id=(other, fs), device_id_type=MESH)
    pl.semaphore_wait(barrier, GROUP + 1)

    def unit_copy(k):
        return remote(
            shard_ref, units.at[group], unit_send.at[k - 1], unit_recv.at[k - 1], mate(k), fs
        )

    for k in range(1, GROUP):
        unit_copy(k).start()
    units[group] = shard_ref[...]
    for k in range(1, GROUP):
        unit_copy(k).wait_recv()
    flat = units[...].reshape(GROUP * 16, units.shape[2])
    dense = GROUP * rows
    row = lax.broadcasted_iota(jnp.int32, (dense, GROUP * 16), 0)
    column = lax.broadcasted_iota(jnp.int32, (dense, GROUP * 16), 1)
    for m in range(2):
        pick = jnp.zeros((dense, GROUP * 16), jnp.float32)
        for q in range(GROUP):
            hit = (row >= q * rows) & (row < (q + 1) * rows) & (column - q * 16 - 8 * m == row - q * rows)
            pick = jnp.where(hit, 1.0, pick)
        full[m, z] = jnp.dot(
            pick.astype(jnp.bfloat16), flat, preferred_element_type=jnp.float32
        ).astype(jnp.bfloat16)

    def right_copy(s):
        block = full.at[core, (z - s + N_Z) % N_Z]
        return remote(block, block, right_send.at[s], right_recv.at[s], right, fs)

    def left_copy(s):
        block = full.at[core, (z + s) % N_Z]
        return remote(block, block, left_send.at[s], left_recv.at[s], left, fs)

    def share(k, offset):
        block = full.at[core, (z + offset + N_Z) % N_Z]
        return remote(block, block, sib_send.at[k], sib_recv.at[k], sibling, fs)

    def step(s, carry):
        right_copy(s).start()
        left_copy(s).start()
        right_copy(s).wait_recv()
        share(2 * s, -1 - s).start()
        left_copy(s).wait_recv()
        share(2 * s + 1, 1 + s).start()
        return carry

    lax.fori_loop(0, LEFT_STEPS, step, 0)
    right_copy(LEFT_STEPS).start()
    right_copy(LEFT_STEPS).wait_recv()
    share(N_Z - 2, -RIGHT_STEPS).start()

    for k in range(1, GROUP):
        unit_copy(k).wait_send()

    def drain(s, carry):
        right_copy(s).wait_send()
        left_copy(s).wait_send()
        share(2 * s, -1 - s).wait()
        share(2 * s + 1, 1 + s).wait()
        return carry

    lax.fori_loop(0, LEFT_STEPS, drain, 0)
    right_copy(LEFT_STEPS).wait_send()
    share(N_Z - 2, -RIGHT_STEPS).wait()

    def emit(b, carry):
        span = pl.ds(pl.multiple_of(b * dense, 16), dense)
        up_ref[span, :] = full[0, b]
        down_ref[span, :] = full[1, b]
        return carry

    lax.fori_loop(0, N_Z, emit, 0)


def gather_weights(w_up, w_down):
    rows, hidden = w_up.shape
    gap = jnp.zeros((8 - rows, hidden), w_up.dtype)
    shard = jnp.concatenate([w_up, gap, w_down, gap], axis=0)
    total = rows * N_Z * GROUP
    vmem = pl.BlockSpec(memory_space=pltpu.VMEM)
    dma = pltpu.SemaphoreType.DMA
    return pl.pallas_call(
        functools.partial(weights_kernel, rows),
        out_shape=[jax.ShapeDtypeStruct((total, hidden), w_up.dtype)] * 2,
        in_specs=[vmem],
        out_specs=[vmem, vmem],
        scratch_shapes=[
            pltpu.VMEM((GROUP, 16, hidden), w_up.dtype),
            pltpu.VMEM((2, N_Z, GROUP * rows, hidden), w_up.dtype),
            dma((GROUP - 1,)), dma((GROUP - 1,)),
            dma((RIGHT_STEPS,)), dma((RIGHT_STEPS,)),
            dma((LEFT_STEPS,)), dma((LEFT_STEPS,)),
            dma((N_Z - 1,)), dma((N_Z - 1,)),
        ],
        compiler_params=pltpu.CompilerParams(
            collective_id=0, has_side_effects=True, vmem_limit_bytes=48 * 1024 * 1024
        ),
    )(shard)


def sums_kernel(
    rows, up_ref, down_ref, out_ref, mats, mine, theirs, right_out, right_in, left_out, left_in,
    block_sum, strips, strips_in, last, last_in,
    sib_send, sib_recv, right_send, right_recv, left_send, left_recv, y_send, y_recv, end_send, end_recv,
):
    z, y, core = own_place()
    fs = lax.axis_index("fsdp")
    right = dp_index((z + 1) % N_Z, y, core)
    left = dp_index((z + N_Z - 1) % N_Z, y, core)
    sibling = dp_index(z, y, 1 - core)
    dense = GROUP * rows

    def column_mate(k):
        return dp_index(z, (y + k) % N_Y, core)

    barrier = pltpu.get_barrier_semaphore()
    for other in [sibling, right, left] + [column_mate(k) for k in range(1, N_Y)]:
        pl.semaphore_signal(barrier, inc=1, device_id=(other, fs), device_id_type=MESH)
    pl.semaphore_wait(barrier, 2 + N_Y)

    def sib_copy(k, block):
        return remote(
            mine.at[block], theirs.at[block], sib_send.at[k], sib_recv.at[k], sibling, fs
        )

    def span(block):
        return pl.ds(pl.multiple_of(block * dense, 16), dense)

    def pack(k, block):
        mats[0, block] = up_ref[span(block), :]
        mats[1, block] = down_ref[span(block), :]
        mine[block] = mats[1 - core, block].astype(jnp.bfloat16)
        sib_copy(k, block).start()

    def right_dest(s):
        return (z + RIGHT_STEPS - s) % N_Z

    def left_dest(s):
        return (z - LEFT_STEPS + s + N_Z) % N_Z

    def pack_step(s, carry):
        pack(2 * s, right_dest(s))
        pack(2 * s + 1, left_dest(s))
        return carry

    lax.fori_loop(0, LEFT_STEPS, pack_step, 0)
    pack(N_Z - 2, right_dest(LEFT_STEPS))
    pack(N_Z - 1, z)

    def own(k, block):
        sib_copy(k, block).wait_recv()
        return mats[core, block] + theirs[block].astype(jnp.float32)

    def right_copy(s):
        return remote(
            right_out.at[s], right_in.at[s], right_send.at[s], right_recv.at[s], right, fs
        )

    def left_copy(s):
        return remote(left_out.at[s], left_in.at[s], left_send.at[s], left_recv.at[s], left, fs)

    right_out[0] = own(0, right_dest(0)).astype(jnp.bfloat16)
    right_copy(0).start()
    left_out[0] = own(1, left_dest(0)).astype(jnp.bfloat16)
    left_copy(0).start()

    def step(s, carry):
        mixed = own(2 * s, right_dest(s))
        right_copy(s - 1).wait_recv()
        right_out[s] = (mixed + right_in[s - 1].astype(jnp.float32)).astype(jnp.bfloat16)
        right_copy(s).start()
        mixed = own(2 * s + 1, left_dest(s))
        left_copy(s - 1).wait_recv()
        left_out[s] = (mixed + left_in[s - 1].astype(jnp.float32)).astype(jnp.bfloat16)
        left_copy(s).start()
        return carry

    lax.fori_loop(1, LEFT_STEPS, step, 0)
    s = LEFT_STEPS
    mixed = own(2 * s, right_dest(s))
    right_copy(s - 1).wait_recv()
    right_out[s] = (mixed + right_in[s - 1].astype(jnp.float32)).astype(jnp.bfloat16)
    right_copy(s).start()
    mixed = own(N_Z - 1, z)
    left_copy(s - 1).wait_recv()
    mixed = mixed + left_in[s - 1].astype(jnp.float32)
    right_copy(s).wait_recv()
    block_sum[...] = mixed + right_in[s].astype(jnp.float32)

    for k in range(N_Y):
        strips[k, 0 : N_CORE * rows] = block_sum[k * N_CORE * rows : (k + 1) * N_CORE * rows]

    def strip_copy(k):
        return remote(
            strips.at[(y + k) % N_Y], strips_in.at[k - 1], y_send.at[k - 1], y_recv.at[k - 1],
            column_mate(k), fs,
        )

    for k in range(1, N_Y):
        strip_copy(k).start()
    for k in range(1, N_Y):
        strip_copy(k).wait_recv()
    total = strips[y, 0 : N_CORE * rows]
    for k in range(1, N_Y):
        total = total + strips_in[k - 1, 0 : N_CORE * rows]
    block_sum[0 : N_CORE * rows] = total
    for k in range(N_CORE):
        last[k, 0:rows] = block_sum[k * rows : (k + 1) * rows]
    end = remote(last.at[1 - core], last_in, end_send, end_recv, sibling, fs)
    end.start()
    out_ref[core, 0:rows] = last[core, 0:rows]
    end.wait_recv()
    out_ref[1 - core, 0:rows] = last_in[0:rows]

    end.wait_send()
    for k in range(1, N_Y):
        strip_copy(k).wait_send()

    def drain(s, carry):
        right_copy(s).wait_send()
        left_copy(s).wait_send()
        sib_copy(2 * s, right_dest(s)).wait_send()
        sib_copy(2 * s + 1, left_dest(s)).wait_send()
        return carry

    lax.fori_loop(0, LEFT_STEPS, drain, 0)
    right_copy(LEFT_STEPS).wait_send()
    sib_copy(N_Z - 2, right_dest(LEFT_STEPS)).wait_send()
    sib_copy(N_Z - 1, z).wait_send()


def sum_weights(up_local, down_local):
    total, hidden = up_local.shape
    dense = total // N_Z
    rows = dense // GROUP
    vmem = pl.BlockSpec(memory_space=pltpu.VMEM)
    dma = pltpu.SemaphoreType.DMA
    f32, b16 = jnp.float32, jnp.bfloat16
    both = pl.pallas_call(
        functools.partial(sums_kernel, rows),
        out_shape=jax.ShapeDtypeStruct((2, 8, hidden), f32),
        in_specs=[vmem, vmem],
        out_specs=vmem,
        scratch_shapes=[
            pltpu.VMEM((2, N_Z, dense, hidden), f32),
            pltpu.VMEM((N_Z, dense, hidden), b16),
            pltpu.VMEM((N_Z, dense, hidden), b16),
            pltpu.VMEM((RIGHT_STEPS, dense, hidden), b16),
            pltpu.VMEM((RIGHT_STEPS, dense, hidden), b16),
            pltpu.VMEM((LEFT_STEPS, dense, hidden), b16),
            pltpu.VMEM((LEFT_STEPS, dense, hidden), b16),
            pltpu.VMEM((dense, hidden), f32),
            pltpu.VMEM((N_Y, 16, hidden), f32),
            pltpu.VMEM((N_Y - 1, 16, hidden), f32),
            pltpu.VMEM((N_CORE, 8, hidden), f32),
            pltpu.VMEM((8, hidden), f32),
            dma((N_Z,)), dma((N_Z,)),
            dma((RIGHT_STEPS,)), dma((RIGHT_STEPS,)),
            dma((LEFT_STEPS,)), dma((LEFT_STEPS,)),
            dma((N_Y - 1,)), dma((N_Y - 1,)),
            dma, dma,
        ],
        compiler_params=pltpu.CompilerParams(
            collective_id=1, has_side_effects=True, vmem_limit_bytes=48 * 1024 * 1024
        ),
    )(up_local, down_local)
    return both[0, :rows], both[1, :rows]


def padded_2(block, sides, width):
    for axis, dim in sides:
        count = lax.axis_size(axis)
        forward = [(i, i + 1) for i in range(count - 1)]
        backward = [(target, source) for source, target in forward]
        low = lax.ppermute(
            lax.slice_in_dim(block, block.shape[dim] - width, None, axis=dim), axis, forward
        )
        high = lax.ppermute(lax.slice_in_dim(block, 0, width, axis=dim), axis, backward)
        block = jnp.concatenate([low, block, high], axis=dim)
    return block


def gelu_value(hidden):
    return 0.5 * hidden * (1.0 + jax.scipy.special.erf(hidden * root_half))


def gelu_slope(hidden):
    return (
        0.5 * (1.0 + jax.scipy.special.erf(hidden * root_half))
        + hidden * jnp.exp(-0.5 * hidden * hidden) * root_tau
    )


def depth_keep(widths_face, far_first):
    layer_index = jnp.arange(3, dtype=jnp.int32)
    if far_first:
        depth_value = 3 - layer_index
    else:
        depth_value = layer_index + 1
    return depth_value[None, :] <= widths_face[:, None]


def depthwise_flat(padded, kernel):
    channels, tile_count, wide, _ = padded.shape
    total = tile_count * wide * wide
    flat = jnp.pad(padded.reshape(channels, total), ((0, 0), (0, 6 * wide + 6)))
    taps = kernel.astype(jnp.float32)
    summed = jnp.zeros((channels, total), jnp.float32)
    for row_tap in range(7):
        for col_tap in range(7):
            offset = row_tap * wide + col_tap
            summed = (
                summed
                + flat[:, offset : offset + total].astype(jnp.float32)
                * taps[row_tap * 7 + col_tap][:, None]
            )
    side_len = wide - 6
    return summed.reshape(channels, tile_count, wide, wide)[:, :, :side_len, :side_len]


def depthwise_back_flat(grad_grid, kernel):
    channels, tile_count, side_len, _ = grad_grid.shape
    wide = side_len + 6
    total = tile_count * wide * wide
    lead = 6 * wide + 6
    placed = jnp.pad(grad_grid.astype(jnp.float32), ((0, 0), (0, 0), (0, 6), (0, 6))).reshape(
        channels, total
    )
    placed = jnp.pad(placed, ((0, 0), (lead, 0)))
    taps = kernel.astype(jnp.float32)
    summed = jnp.zeros((channels, total), jnp.float32)
    for row_tap in range(7):
        for col_tap in range(7):
            offset = row_tap * wide + col_tap
            summed = (
                summed
                + placed[:, lead - offset : lead - offset + total]
                * taps[row_tap * 7 + col_tap][:, None]
            )
    return summed.reshape(channels, tile_count, wide, wide)


def selection(neighbor_ids, shift_values, tile_count, side_len):
    position = jnp.arange(side_len, dtype=jnp.int32)
    source_tile = jnp.arange(tile_count, dtype=jnp.int32)
    summed = jnp.zeros((tile_count, side_len, tile_count, side_len), jnp.float32)
    for which_entry in range(2):
        owner_tile = neighbor_ids[:, which_entry]
        slot_index = jnp.where(owner_tile >= 0, owner_tile % tile_count, -1)
        along_edge = position[None, :] + shift_values[:, which_entry][:, None]
        tile_hit = slot_index[:, None] == source_tile[None, :]
        row_hit = along_edge[:, :, None] == position[None, None, :]
        summed = summed + (tile_hit[:, None, :, None] & row_hit[:, :, None, :]).astype(jnp.float32)
    return summed.reshape(tile_count * side_len, tile_count * side_len)


def per_device(
    tiles,
    kernel,
    norm_gain,
    w_up,
    w_down,
    layer_scale,
    neighbors,
    shifts,
    halo_widths,
    land,
    cotangent,
):
    channels = tiles.shape[0]
    tile_count, side_len = (land.shape[0], land.shape[1])
    row_count = tile_count * side_len * side_len
    face_cols = tile_count * side_len
    full_width = channels * lax.axis_size("fsdp")
    grid_in = tiles.reshape(channels, tile_count, side_len, side_len)
    north_src = jnp.transpose(grid_in[:, :, side_len - 3 :, :], (2, 0, 1, 3))
    south_src = jnp.transpose(grid_in[:, :, :3, :], (2, 0, 1, 3))
    west_src = jnp.transpose(grid_in[:, :, :, side_len - 3 :], (3, 0, 1, 2))
    east_src = jnp.transpose(grid_in[:, :, :, :3], (3, 0, 1, 2))
    edges = padded_2(jnp.stack([east_src, west_src]), (("dp", 0),), 1)
    faces = (north_src, south_src, edges[0], edges[3])
    selectors = []
    masks = []
    halos = []
    for face_index in range(4):
        selector = selection(neighbors[:, face_index], shifts[:, face_index], tile_count, side_len)
        keep = depth_keep(halo_widths[:, face_index], face_index in (0, 2))
        keep_mask = jnp.transpose(keep)[:, None, :, None]
        picked = jnp.dot(
            faces[face_index].reshape(3 * channels, face_cols),
            selector.T.astype(jnp.bfloat16),
            preferred_element_type=jnp.float32,
        )
        halos.append(
            jnp.where(keep_mask, picked.reshape(3, channels, tile_count, side_len), 0.0).astype(
                jnp.bfloat16
            )
        )
        selectors.append(selector)
        masks.append(keep_mask)
    up_full, down_full = gather_weights(w_up, w_down)
    corner = jnp.zeros((channels, tile_count, 3, 3), jnp.bfloat16)
    upper = jnp.concatenate([corner, jnp.transpose(halos[0], (1, 2, 0, 3)), corner], axis=3)
    lower = jnp.concatenate([corner, jnp.transpose(halos[1], (1, 2, 0, 3)), corner], axis=3)
    middle = jnp.concatenate(
        [jnp.transpose(halos[2], (1, 2, 3, 0)), grid_in, jnp.transpose(halos[3], (1, 2, 3, 0))],
        axis=3,
    )
    padded = jnp.concatenate([upper, middle, lower], axis=2)
    conv = depthwise_flat(padded, kernel)
    conv_rows = conv.reshape(channels, row_count).astype(jnp.bfloat16)
    gain_f = norm_gain.astype(jnp.float32)[:, None]
    values = lax.optimization_barrier(conv_rows).astype(jnp.float32)
    row_total, row_squares = lax.psum(
        (jnp.sum(values, axis=0), jnp.sum(values * values, axis=0)), "fsdp"
    )
    row_mean = row_total / full_width
    inv_scale = lax.rsqrt(row_squares / full_width - row_mean * row_mean + 1e-06)
    centered = (values - row_mean[None, :]) * inv_scale[None, :]
    normed = lax.all_gather((centered * gain_f).astype(jnp.bfloat16), "fsdp", axis=0, tiled=True)
    pre_act = lax.dot_general(
        normed, up_full, (((0,), (0,)), ((), ())), preferred_element_type=jnp.float32
    )
    hidden = gelu_value(pre_act).astype(jnp.bfloat16)
    partial_out = lax.dot_general(
        down_full, hidden, (((1,), (1,)), ((), ())), preferred_element_type=jnp.float32
    )
    mixed = lax.psum_scatter(
        partial_out.astype(jnp.bfloat16), "fsdp", scatter_dimension=0, tiled=True
    ).astype(jnp.float32)
    scale_f = layer_scale.astype(jnp.float32)[:, None]
    block_out = (tiles.astype(jnp.float32) + scale_f * mixed).astype(jnp.bfloat16)
    grad_out = cotangent * land.reshape(row_count)[None, :].astype(jnp.bfloat16)
    grad_mixed = (scale_f * grad_out.astype(jnp.float32)).astype(jnp.bfloat16)
    grad_mixed_all = lax.all_gather(grad_mixed, "fsdp", axis=0, tiled=True)
    down_local = jnp.dot(grad_mixed_all, hidden, preferred_element_type=jnp.float32)
    grad_hidden = lax.dot_general(
        grad_mixed_all, down_full, (((0,), (0,)), ((), ())), preferred_element_type=jnp.float32
    )
    grad_pre = (grad_hidden * gelu_slope(pre_act)).astype(jnp.bfloat16)
    partial_grad = lax.dot_general(
        up_full, grad_pre, (((1,), (1,)), ((), ())), preferred_element_type=jnp.float32
    )
    grad_normed = lax.psum_scatter(
        partial_grad.astype(jnp.bfloat16), "fsdp", scatter_dimension=0, tiled=True
    ).astype(jnp.float32)
    up_local = jnp.dot(normed, grad_pre, preferred_element_type=jnp.float32)
    grad_centered = grad_normed * gain_f
    first_sum, second_sum = lax.psum(
        (jnp.sum(grad_centered, axis=0), jnp.sum(grad_centered * centered, axis=0)), "fsdp"
    )
    grad_conv = (
        inv_scale[None, :]
        * (
            grad_centered
            - first_sum[None, :] / full_width
            - centered * (second_sum[None, :] / full_width)
        )
    ).astype(jnp.bfloat16)
    grad_pad = depthwise_back_flat(
        grad_conv.reshape(channels, tile_count, side_len, side_len), kernel
    )
    inner = slice(3, 3 + side_len)

    def returned(face_index, grad_face):
        masked = jnp.where(masks[face_index], grad_face, 0.0).reshape(3 * channels, face_cols)
        moved = jnp.dot(
            masked,
            selectors[face_index],
            precision=lax.Precision.HIGHEST,
            preferred_element_type=jnp.float32,
        )
        return moved.reshape(3, channels, tile_count, side_len)

    tile_grad = (
        grad_out.astype(jnp.float32).reshape(channels, tile_count, side_len, side_len)
        + grad_pad[:, :, inner, inner]
    )
    edge_north = returned(0, jnp.transpose(grad_pad[:, :, 0:3, inner], (2, 0, 1, 3)))
    tile_grad = tile_grad + jnp.pad(
        jnp.transpose(edge_north, (1, 2, 0, 3)), ((0, 0), (0, 0), (side_len - 3, 0), (0, 0))
    )
    edge_south = returned(1, jnp.transpose(grad_pad[:, :, side_len + 3 :, inner], (2, 0, 1, 3)))
    tile_grad = tile_grad + jnp.pad(
        jnp.transpose(edge_south, (1, 2, 0, 3)), ((0, 0), (0, 0), (0, side_len - 3), (0, 0))
    )
    edge_west = returned(2, jnp.transpose(grad_pad[:, :, inner, 0:3], (3, 0, 1, 2)))
    edge_east = returned(3, jnp.transpose(grad_pad[:, :, inner, side_len + 3 :], (3, 0, 1, 2)))
    coming = padded_2(
        jnp.stack([edge_west, edge_east]).astype(jnp.bfloat16), (("dp", 0),), 1
    ).astype(jnp.float32)
    tile_grad = tile_grad + jnp.pad(
        jnp.transpose(coming[0], (1, 2, 3, 0)), ((0, 0), (0, 0), (0, 0), (0, side_len - 3))
    )
    tile_grad = tile_grad + jnp.pad(
        jnp.transpose(coming[3], (1, 2, 3, 0)), ((0, 0), (0, 0), (0, 0), (side_len - 3, 0))
    )
    up_grad, down_grad = sum_weights(up_local, down_local)
    return (
        block_out,
        tile_grad.reshape(channels, row_count).astype(jnp.bfloat16),
        up_grad,
        down_grad,
    )


def solution(mesh):
    return jax.shard_map(
        per_device,
        mesh=mesh,
        in_specs=(
            P("fsdp", "dp"),
            P(None, "fsdp"),
            P("fsdp"),
            P("dp", "fsdp"),
            P("dp", "fsdp"),
            P("fsdp"),
            P("dp", None, None),
            P("dp", None, None),
            P("dp", None),
            P("dp", None, None),
            P("fsdp", "dp"),
        ),
        out_specs=(P("fsdp", "dp"), P("fsdp", "dp"), P("dp", "fsdp"), P("dp", "fsdp")),
        check_vma=False,
    )
```

```python
import functools
import math

import jax
import jax.numpy as jnp
from jax import lax
from jax.experimental import pallas as pl
from jax.experimental.pallas import tpu as pltpu
from jax.sharding import PartitionSpec as P

root_half = 1.0 / math.sqrt(2.0)
root_tau = 1.0 / math.sqrt(2.0 * math.pi)

N_Z, N_Y, N_CORE, N_X = 16, 4, 2, 4
N_FAR, N_NEAR = 4, 4
N_DP = N_Z * N_Y * N_CORE
MESH = pl.DeviceIdType.MESH
F32, B16 = jnp.float32, jnp.bfloat16
SIDE, TILE, TAPS = 8, 8, 7
HALF_ROWS = 256


def dp_index(z, y, core):
    return (z * N_Y + y) * N_CORE + core


def dot(a, b):
    return jnp.dot(a, b, preferred_element_type=F32)


def dot_nt(a, b):
    return lax.dot_general(a, b, (((1,), (1,)), ((), ())), preferred_element_type=F32)


def dot_tn(a, b):
    return lax.dot_general(a, b, (((0,), (0,)), ((), ())), preferred_element_type=F32)


def block_kernel(
    rows, width,
    x_ref, cot_ref, land_ref, taps_ref, gain_ref, scale_ref, links_ref, shard_ref,
    block_ref, grad_ref, wgrad_ref,
    perm, widen, picks, taps, xt, go, east_in, west_in, pad, gains,
    gma, gmb, cva, cvb, cen, inv, nrm, gmx, hid, gpre,
    pga, pgb, pgin_a, pgin_b, mxa, mxb, mxin_a, mxin_b, sums, sums_in, sum_cols,
    gcv, gpad, ret_w, ret_e, ret_w_in, ret_e_in, tg,
    unit, unit_in, full, dense,
    st, st_in, ysum, y_in, nsum, n_in, fsum, f_in, last, last_in,
    halo_s, halo_r, gain_s, gain_r, gm_s, gm_r, cv_s, cv_r, pg_s, pg_r, mx_s, mx_r, sum_s, sum_r,
    ret_s, ret_r, wsib_s, wsib_r, wfar_s, wfar_r, wnear_s, wnear_r, wy_s, wy_r, wsh_s, wsh_r,
    gsib_s, gsib_r, gy_s, gy_r, gnear_s, gnear_r, gfar_s, gfar_r, gend_s, gend_r,
):
    channels = x_ref.shape[0]
    low, high = 128, channels - 128
    cells = x_ref.shape[1]
    me = lax.axis_index("dp")
    x = lax.axis_index("fsdp")
    z, y, core = me // (N_Y * N_CORE), (me // N_CORE) % N_Y, me % N_CORE
    far, near = z // N_NEAR, z % N_NEAR
    east, west = (me + 1) % N_DP, (me + N_DP - 1) % N_DP
    sibling = dp_index(z, y, 1 - core)

    def at_z(step):
        return dp_index((z + step + N_Z) % N_Z, y, core)

    def at_y(k):
        return dp_index(z, (y + k) % N_Y, core)

    def copy(src, dst, send, recv, dp, fs=None):
        return pltpu.make_async_remote_copy(
            src_ref=src, dst_ref=dst, send_sem=send, recv_sem=recv,
            device_id=(dp, x if fs is None else fs), device_id_type=MESH,
        )

    barrier = pltpu.get_barrier_semaphore()
    greeted = [(east, x), (west, x), (sibling, x)]
    greeted += [(me, (x + k) % N_X) for k in range(1, N_X)]
    greeted += [(at_z(s), x) for s in (4, 8, 12, 1, -1, 2, -2)]
    greeted += [(at_y(k), x) for k in range(1, N_Y)]
    for other in greeted:
        pl.semaphore_signal(barrier, inc=1, device_id=other, device_id_type=MESH)

    out_cell = lax.broadcasted_iota(jnp.int32, (cells, cells), 0)
    in_cell = lax.broadcasted_iota(jnp.int32, (cells, cells), 1)
    wanted = (out_cell % 8) * 64 + ((out_cell // 8) % 8) * 8 + out_cell // 64
    perm[...] = jnp.where(in_cell == wanted, 1.0, 0.0).astype(B16)
    xt[...] = dot_nt(perm[...], x_ref[...]).astype(B16)
    go[...] = dot_nt(perm[...], cot_ref[...] * land_ref[...]).astype(B16)
    grad_mixed = (go[...].astype(F32) * scale_ref[...]).astype(B16)
    gma[x] = grad_mixed[:, :low]
    gmb[x] = jnp.concatenate([grad_mixed[:HALF_ROWS, low:], grad_mixed[HALF_ROWS:, low:]], axis=1)
    gains[x] = gain_ref[...]

    pl.semaphore_wait(barrier, len(greeted))

    halo_west = copy(xt.at[pl.ds(0, 192)], east_in, halo_s.at[0], halo_r.at[0], west)
    halo_east = copy(xt.at[pl.ds(cells - 192, 192)], west_in, halo_s.at[1], halo_r.at[1], east)
    halo_west.start()
    halo_east.start()
    unit_in[core] = shard_ref[...]
    wsib = copy(shard_ref, unit_in.at[core], wsib_s, wsib_r, sibling)
    wsib.start()

    def x_copies(src, dst, send, recv, scatter):
        made = []
        for k in range(1, N_X):
            other = (x + k) % N_X
            if scatter:
                pair = (src.at[other], dst.at[k - 1])
            else:
                pair = (src.at[x], dst.at[x])
            made.append(copy(*pair, send.at[k - 1], recv.at[k - 1], me, other))
        return made

    gain_copies = x_copies(gains, gains, gain_s, gain_r, False)
    gm_copies = x_copies(gma, gma, gm_s.at[0], gm_r.at[0], False)
    gm_copies += x_copies(gmb, gmb, gm_s.at[1], gm_r.at[1], False)
    for c in gain_copies + gm_copies:
        c.start()

    edge_row = lax.broadcasted_iota(jnp.int32, (64, 64), 0)
    edge_col = lax.broadcasted_iota(jnp.int32, (64, 64), 1)
    links = jnp.concatenate([links_ref[...]] * 8, axis=0)
    for face in range(4):
        chosen = jnp.zeros((64, 64), F32)
        for entry in range(2):
            c = face * 2 + entry
            owner = links[:, c : c + 1]
            shift = links[:, 8 + c : 9 + c]
            target = jnp.where(owner >= 0, owner % TILE + TILE * shift, -4096)
            target = target + (edge_row // 8) * 8
            chosen = chosen + jnp.where(target == edge_col, 1.0, 0.0)
        for layer in range(3):
            depth = 3 - layer if face in (0, 2) else layer + 1
            keep = links[:, 16 + face : 17 + face] >= depth
            picks[face * 3 + layer] = jnp.where(keep, chosen, 0.0).astype(B16)

    kernel_taps = taps_ref[...].astype(F32)
    for a in range(TAPS):
        for b in range(TAPS):
            k = a * TAPS + b
            taps[b, a] = jnp.broadcast_to(kernel_taps[k : k + 1], (8, channels))

    pad[...] = jnp.zeros_like(pad)
    cells_f = xt[...].astype(F32).reshape(SIDE, SIDE, TILE, channels)
    pad[3 : 3 + SIDE, 3 : 3 + SIDE] = cells_f
    for layer in range(3):
        north = cells_f[:, 5 + layer].reshape(64, channels).astype(B16)
        south = cells_f[:, layer].reshape(64, channels).astype(B16)
        pad[3 : 3 + SIDE, layer] = dot(picks[layer], north).astype(B16).astype(F32).reshape(SIDE, TILE, channels)
        pad[3 : 3 + SIDE, 11 + layer] = (
            dot(picks[3 + layer], south).astype(B16).astype(F32).reshape(SIDE, TILE, channels)
        )

    wsib.wait_recv()
    both = unit_in[...].reshape(N_CORE * 16, width)
    u_row = lax.broadcasted_iota(jnp.int32, (16, N_CORE * 16), 0)
    u_col = lax.broadcasted_iota(jnp.int32, (16, N_CORE * 16), 1)
    first = (u_row < rows) & (u_col == u_row + 8 * core)
    second = (u_row >= rows) & (u_row < 2 * rows) & (u_col == 16 + u_row - rows + 8 * core)
    joined = dot(jnp.where(first | second, 1.0, 0.0).astype(B16), both).astype(B16)
    full[core, y, near, far] = joined

    def far_copy(k):
        place = full.at[core, y, near, far]
        return copy(place, place, wfar_s.at[k - 1], wfar_r.at[k - 1], at_z(4 * k))

    for k in range(1, N_FAR):
        far_copy(k).start()

    halo_west.wait_recv()
    halo_east.wait_recv()
    for layer in range(3):
        part = pl.ds(layer * 64, 64)
        pad[layer, 3 : 3 + SIDE] = (
            dot(picks[6 + layer], west_in[part]).astype(B16).astype(F32).reshape(SIDE, TILE, channels)
        )
        pad[11 + layer, 3 : 3 + SIDE] = (
            dot(picks[9 + layer], east_in[part]).astype(B16).astype(F32).reshape(SIDE, TILE, channels)
        )

    def conv_column(j, start, size):
        total = jnp.zeros((SIDE, TILE, size), F32)
        for b in range(TAPS):
            source = pad[j + b, :, :, start : start + size]
            for a in range(TAPS):
                total = total + source[a : a + SIDE] * taps[b, a, :, start : start + size][None]
        return total.reshape(64, size).astype(B16)

    def conv_low(j, carry):
        cva[x, pl.ds(pl.multiple_of(j * 64, 64), 64)] = conv_column(j, 0, low)
        return carry

    def conv_high(j, carry):
        cvb[x, pl.ds(pl.multiple_of(j * 64, 64), 64)] = jnp.concatenate(
            [conv_column(j, low, high), conv_column(j + 4, low, high)], axis=1
        )
        return carry

    lax.fori_loop(0, SIDE, conv_low, 0)
    cv_copies = x_copies(cva, cva, cv_s.at[0], cv_r.at[0], False)
    for c in cv_copies:
        c.start()

    for k in range(1, N_FAR):
        far_copy(k).wait_recv()

    near_steps = (1, -1, -2)

    def near_copy(k):
        place = full.at[core, y, near]
        return copy(place, place, wnear_s.at[k], wnear_r.at[k], at_z(near_steps[k]))

    for k in range(3):
        near_copy(k).start()

    lax.fori_loop(0, 4, conv_high, 0)
    high_copies = x_copies(cvb, cvb, cv_s.at[1], cv_r.at[1], False)
    for c in high_copies:
        c.start()

    w_row = lax.broadcasted_iota(jnp.int32, (256, 256), 0)
    w_col = lax.broadcasted_iota(jnp.int32, (256, 256), 1)
    span = N_CORE * rows
    w_from = ((w_row // span) % N_Y) * 64 + (w_row // (span * N_Y)) * 16 + w_row % span
    widen[...] = jnp.where((w_col == w_from) & (w_row < channels), 1.0, 0.0).astype(B16)

    for k in range(3):
        near_copy(k).wait_recv()

    def y_copy(k):
        place = full.at[core, y]
        return copy(place, place, wy_s.at[k - 1], wy_r.at[k - 1], at_y(k))

    def share(k):
        place = full.at[core, (y + N_Y - k) % N_Y]
        return copy(place, place, wsh_s.at[k], wsh_r.at[k], sibling)

    for k in range(1, N_Y):
        y_copy(k).start()
    share(0).start()

    for c in gain_copies + gm_copies:
        c.wait_recv()
    nrm[...] = jnp.zeros_like(nrm)
    gmx[...] = jnp.zeros_like(gmx)
    for b in range(N_X):
        gmx[:, b * 256 : b * 256 + low] = gma[b]
        packed = gmb[b]
        gmx[:HALF_ROWS, b * 256 + low : b * 256 + channels] = packed[:, :high]
        gmx[HALF_ROWS:, b * 256 + low : b * 256 + channels] = packed[:, high:]

    for c in cv_copies + high_copies:
        c.wait_recv()

    wide = float(channels * N_X)
    for half in range(2):

        def norm_rows(i, carry, half=half):
            part = pl.ds(pl.multiple_of(i * 64, 64), 64)
            here = pl.ds(pl.multiple_of(half * HALF_ROWS + i * 64, 64), 64)
            lows = [cva[b, here].astype(F32) for b in range(N_X)]
            highs = [cvb[b, part, half * high : (half + 1) * high].astype(F32) for b in range(N_X)]
            total = jnp.sum(sum(lows), axis=1, keepdims=True) + jnp.sum(sum(highs), axis=1, keepdims=True)
            square = jnp.sum(sum(v * v for v in lows), axis=1, keepdims=True) + jnp.sum(
                sum(v * v for v in highs), axis=1, keepdims=True
            )
            mean = total / wide
            scale = lax.rsqrt(square / wide - mean * mean + 1e-06)
            inv[here] = jnp.broadcast_to(scale, (64, 128))
            for b in range(N_X):
                centered = (lows[b] - mean) * scale
                cen[b, here, 0:low] = centered
                nrm[here, b * 256 : b * 256 + low] = (centered * gains[b, 0:1, 0:low]).astype(B16)
                centered = (highs[b] - mean) * scale
                cen[b, here, low:channels] = centered
                nrm[here, b * 256 + low : b * 256 + channels] = (
                    centered * gains[b, 0:1, low:channels]
                ).astype(B16)
            return carry

        lax.fori_loop(0, 4, norm_rows, 0)

    for k in range(1, N_Y):
        y_copy(k).wait_recv()
        share(k).start()

    def unit_rows(m, b):
        return jnp.concatenate(
            [full[m, yy, nn, b] for yy in range(N_Y) for nn in range(N_NEAR)], axis=0
        )

    for k in range(N_Y):
        share(k).wait_recv()
    for m in range(2):
        for b in range(N_X):
            dense[m, b * 256 : (b + 1) * 256] = dot(widen[...], unit_rows(m, b)).astype(B16)

    for half in range(2):

        def mlp_rows(i, carry, half=half):
            part = pl.ds(pl.multiple_of(i * 128, 128), 128)
            here = pl.ds(pl.multiple_of(half * HALF_ROWS + i * 128, 128), 128)
            pre = dot(nrm[here], dense[0])
            edge = 0.5 * (1.0 + lax.erf(pre * root_half))
            hidden = (pre * edge).astype(B16)
            hid[here] = hidden
            slope = edge + pre * jnp.exp(-0.5 * pre * pre) * root_tau
            grad_pre = (dot_nt_rows(gmx[here], dense[1]) * slope).astype(B16)
            gpre[here] = grad_pre
            back = dot_nt(grad_pre, dense[0]).astype(B16)
            first_sum = jnp.zeros((128, 128), F32)
            second_sum = jnp.zeros((128, 128), F32)
            first_high = jnp.zeros((128, high), F32)
            second_high = jnp.zeros((128, high), F32)
            for b in range(N_X):
                low_part = back[:, b * 256 : b * 256 + low]
                high_part = back[:, b * 256 + low : b * 256 + channels]
                pga[b, here] = low_part
                pgb[b, part, half * high : (half + 1) * high] = high_part
                g = low_part.astype(F32) * gains[b, 0:1, 0:low]
                first_sum += g
                second_sum += g * cen[b, here, 0:low]
                g = high_part.astype(F32) * gains[b, 0:1, low:channels]
                first_high += g
                second_high += g * cen[b, here, low:channels]
            one = jnp.sum(first_sum, axis=1, keepdims=True) + jnp.sum(first_high, axis=1, keepdims=True)
            two = jnp.sum(second_sum, axis=1, keepdims=True) + jnp.sum(second_high, axis=1, keepdims=True)
            lane = lax.broadcasted_iota(jnp.int32, (128, 128), 1)
            columns = jnp.where(lane == 0, one, jnp.where(lane == 1, two, 0.0))
            sums[i + 2 * half] = jnp.transpose(columns)[0:8]
            return carry

        def dot_nt_rows(a, b):
            return dot(a, b)

        lax.fori_loop(0, 2, mlp_rows, 0)

    pg_copies = x_copies(pga, pgin_a, pg_s.at[0], pg_r.at[0], True)
    pg_copies += x_copies(pgb, pgin_b, pg_s.at[1], pg_r.at[1], True)
    sum_copies = []
    for k in range(1, N_X):
        sum_copies.append(
            copy(sums, sums_in.at[k - 1], sum_s.at[k - 1], sum_r.at[k - 1], me, (x + k) % N_X)
        )
    for c in sum_copies + pg_copies:
        c.start()

    for b in range(N_X):
        for m, left, right in ((0, nrm, gpre), (1, gmx, hid)):
            local = dot_tn(left[:, b * 256 : (b + 1) * 256], right[...]).astype(B16)
            units = dot_tn(widen[...], local).astype(B16)
            for yy in range(N_Y):
                for nn in range(N_NEAR):
                    r = (yy * N_NEAR + nn) * 16
                    st[m, yy, nn, b] = units[r : r + 16]

    def gsib_copy(k):
        yy = (y + k) % N_Y
        return copy(st.at[1 - core, yy], st_in.at[yy], gsib_s.at[k], gsib_r.at[k], sibling)

    for k in (1, 2, 3, 0):
        gsib_copy(k).start()

    for half in range(2):

        def out_rows(i, carry, half=half):
            part = pl.ds(pl.multiple_of(i * 128, 128), 128)
            here = pl.ds(pl.multiple_of(half * HALF_ROWS + i * 128, 128), 128)
            mixed = dot_nt(hid[here], dense[1]).astype(B16)
            for b in range(N_X):
                mxa[b, here] = mixed[:, b * 256 : b * 256 + low]
                mxb[b, part, half * high : (half + 1) * high] = mixed[:, b * 256 + low : b * 256 + channels]
            return carry

        lax.fori_loop(0, 2, out_rows, 0)

    mx_copies = x_copies(mxa, mxin_a, mx_s.at[0], mx_r.at[0], True)
    mx_copies += x_copies(mxb, mxin_b, mx_s.at[1], mx_r.at[1], True)
    for c in mx_copies:
        c.start()

    def gy_copy(k):
        return copy(ysum.at[k], y_in.at[k - 1], gy_s.at[k - 1], gy_r.at[k - 1], at_y(k))

    for k in (1, 2, 3, 0):
        gsib_copy(k).wait_recv()
        yy = (y + k) % N_Y
        ysum[k] = (st[core, yy].astype(F32) + st_in[yy].astype(F32)).astype(B16)
        if k > 0:
            gy_copy(k).start()

    for c in sum_copies + pg_copies:
        c.wait_recv()
    for q in range(4):
        total = sums[q]
        for k in range(1, N_X):
            total = total + sums_in[k - 1, q]
        spread = jnp.concatenate([total / wide, jnp.zeros((120, 128), F32)], axis=0)
        sum_cols[q * 128 : (q + 1) * 128] = jnp.transpose(spread)

    gcv[...] = jnp.zeros_like(gcv)
    for half in range(2):

        def back_rows(i, carry, half=half):
            part = pl.ds(pl.multiple_of(i * 64, 64), 64)
            here = pl.ds(pl.multiple_of(half * HALF_ROWS + i * 64, 64), 64)
            lanes = slice(half * high, (half + 1) * high)
            low_part = pga[x, here].astype(F32)
            high_part = pgb[x, part, lanes].astype(F32)
            for k in range(N_X - 1):
                low_part = low_part + pgin_a[k, here].astype(F32)
                high_part = high_part + pgin_b[k, part, lanes].astype(F32)
            e1 = sum_cols[here, 0:1]
            e2 = sum_cols[here, 1:2]
            scale = inv[here]
            g = low_part * gains[x, 0:1, 0:low]
            g = scale * (g - e1 - cen[x, here, 0:low] * e2)
            gcv[half * 4 + i, :, :, 0:low] = g.astype(B16).astype(F32).reshape(SIDE, TILE, low)
            g = high_part * gains[x, 0:1, low:channels]
            g = scale[:, :high] * (g - e1 - cen[x, here, low:channels] * e2)
            gcv[half * 4 + i, :, :, low:channels] = g.astype(B16).astype(F32).reshape(SIDE, TILE, high)
            return carry

        lax.fori_loop(0, 4, back_rows, 0)

    def spread_column(j, start, size):
        def add_tap(b, totals):
            totals = list(totals)
            source = gcv[j - b, :, :, start : start + size]
            for a in range(TAPS):
                tap = taps[b, a, :, start : start + size]
                for i in range(SIDE):
                    totals[i + a] = totals[i + a] + source[i] * tap
            return tuple(totals)

        empty = tuple(jnp.zeros((TILE, size), F32) for _ in range(SIDE + 6))
        first_tap = jnp.maximum(0, j - (SIDE - 1))
        end_tap = jnp.minimum(TAPS, j + 1)
        totals = lax.fori_loop(first_tap, end_tap, add_tap, empty)
        for i in range(SIDE + 6):
            gpad[j, i, :, start : start + size] = totals[i]

    def spread_edge(j, carry):
        for k in (j, j + 11):
            spread_column(k, 0, low)
            spread_column(k, low, high)
        return carry

    def spread_inner(j, carry):
        spread_column(j, 0, low)
        spread_column(j, low, high)
        return carry

    lax.fori_loop(0, 3, spread_edge, 0)
    for layer in range(3):
        part = pl.ds(layer * 64, 64)
        for face, column, held in ((2, layer, ret_w), (3, 11 + layer, ret_e)):
            edge = gpad[column, 3 : 3 + SIDE].reshape(64, channels).astype(B16)
            held[part] = dot_tn(picks[face * 3 + layer], edge).astype(B16)
    ret_west = copy(ret_w, ret_w_in, ret_s.at[0], ret_r.at[0], west)
    ret_east = copy(ret_e, ret_e_in, ret_s.at[1], ret_r.at[1], east)
    ret_west.start()
    ret_east.start()

    for k in range(1, N_Y):
        gy_copy(k).wait_recv()
    for nn in range(N_NEAR):
        total = ysum[0, nn].astype(F32)
        for k in range(1, N_Y):
            total = total + y_in[k - 1, nn].astype(F32)
        nsum[nn] = total.astype(B16)

    back_steps = (-1, 1, 2)

    def gnear_copy(k):
        target = (near + back_steps[k] + N_NEAR) % N_NEAR
        return copy(nsum.at[target], n_in.at[k], gnear_s.at[k], gnear_r.at[k], at_z(back_steps[k]))

    for k in range(3):
        gnear_copy(k).start()

    lax.fori_loop(3, 11, spread_inner, 0)

    for k in range(3):
        gnear_copy(k).wait_recv()
    total = nsum[near].astype(F32)
    for k in range(3):
        total = total + n_in[k].astype(F32)
    fsum[...] = total

    def gfar_copy(k):
        return copy(
            fsum.at[(far + k) % N_FAR], f_in.at[k - 1], gfar_s.at[k - 1], gfar_r.at[k - 1], at_z(4 * k)
        )

    for k in range(1, N_FAR):
        gfar_copy(k).start()

    tg[...] = go[...].astype(F32).reshape(SIDE, SIDE, TILE, channels) + gpad[3 : 3 + SIDE, 3 : 3 + SIDE]
    for layer in range(3):
        for face, row, target in ((0, layer, 5 + layer), (1, 11 + layer, layer)):
            edge = gpad[3 : 3 + SIDE, row].reshape(64, channels).astype(B16)
            back = dot_tn(picks[face * 3 + layer], edge)
            tg[:, target] = tg[:, target] + back.reshape(SIDE, TILE, channels)

    for c in mx_copies:
        c.wait_recv()
    low_part = mxa[x].astype(F32)
    packed = mxb[x].astype(F32)
    for k in range(N_X - 1):
        low_part = low_part + mxin_a[k].astype(F32)
        packed = packed + mxin_b[k].astype(F32)
    high_part = jnp.concatenate([packed[:, :high], packed[:, high:]], axis=0)
    mixed = jnp.concatenate([low_part, high_part], axis=1)
    out = (xt[...].astype(F32) + scale_ref[...] * mixed).astype(B16)
    block_ref[...] = dot_tn(out, perm[...]).astype(B16)

    for k in range(1, N_FAR):
        gfar_copy(k).wait_recv()
    total = fsum[far]
    for k in range(1, N_FAR):
        total = total + f_in[k - 1]
    last[0, 0:8] = total[0:8]
    last[1, 0:8] = total[rows : rows + 8]
    gend = copy(last.at[1 - core], last_in, gend_s, gend_r, sibling)
    gend.start()
    wgrad_ref[core] = last[core]

    ret_west.wait_recv()
    ret_east.wait_recv()
    for layer in range(3):
        part = pl.ds(layer * 64, 64)
        tg[5 + layer] = tg[5 + layer] + ret_w_in[part].astype(F32).reshape(SIDE, TILE, channels)
        tg[layer] = tg[layer] + ret_e_in[part].astype(F32).reshape(SIDE, TILE, channels)
    grad_ref[...] = dot_tn(tg[...].reshape(cells, channels).astype(B16), perm[...]).astype(B16)

    gend.wait_recv()
    wgrad_ref[1 - core] = last_in[...]

    sent = [halo_west, halo_east, wsib, ret_west, ret_east, gend]
    sent += gain_copies + gm_copies + cv_copies + high_copies + pg_copies + sum_copies + mx_copies
    sent += [far_copy(k) for k in range(1, N_FAR)] + [near_copy(k) for k in range(3)]
    sent += [y_copy(k) for k in range(1, N_Y)] + [share(k) for k in range(N_Y)]
    sent += [gsib_copy(k) for k in range(N_Y)] + [gy_copy(k) for k in range(1, N_Y)]
    sent += [gnear_copy(k) for k in range(3)] + [gfar_copy(k) for k in range(1, N_FAR)]
    for c in sent:
        c.wait_send()


def per_device(
    tiles, kernel, norm_gain, w_up, w_down, layer_scale, neighbors, shifts, halo_widths, land, cotangent
):
    channels, cells = tiles.shape
    rows, width = w_up.shape
    gap = jnp.zeros((8 - rows, width), w_up.dtype)
    shard = jnp.concatenate([w_up, gap, w_down, gap], axis=0)
    links = jnp.concatenate(
        [neighbors.reshape(TILE, 8), shifts.reshape(TILE, 8), halo_widths], axis=1
    )
    land_row = land.reshape(1, cells).astype(B16)
    gain = jnp.broadcast_to(norm_gain.astype(F32)[None], (8, channels))
    scale = layer_scale.astype(F32)[None]
    high = channels - 128
    vmem = pl.BlockSpec(memory_space=pltpu.VMEM)
    dma = pltpu.SemaphoreType.DMA

    def v(dtype, *shape):
        return pltpu.VMEM(shape, dtype)

    quarter = (N_NEAR, N_FAR, 16, width)
    scratch = [
        v(B16, cells, cells), v(B16, 256, 256), v(B16, 12, 64, 64), v(F32, TAPS, TAPS, 8, channels),
        v(B16, cells, channels), v(B16, cells, channels), v(B16, 192, channels), v(B16, 192, channels),
        v(F32, SIDE + 6, SIDE + 6, TILE, channels), v(F32, N_X, 8, channels),
        v(B16, N_X, cells, 128), v(B16, N_X, HALF_ROWS, 128), v(B16, N_X, cells, 128), v(B16, N_X, HALF_ROWS, 128),
        v(F32, N_X, cells, channels), v(F32, cells, 128), v(B16, cells, N_X * 256), v(B16, cells, N_X * 256),
        v(B16, cells, width), v(B16, cells, width),
        v(B16, N_X, cells, 128), v(B16, N_X, HALF_ROWS, 128), v(B16, 3, cells, 128), v(B16, 3, HALF_ROWS, 128),
        v(B16, N_X, cells, 128), v(B16, N_X, HALF_ROWS, 128), v(B16, 3, cells, 128), v(B16, 3, HALF_ROWS, 128),
        v(F32, 4, 8, 128), v(F32, 3, 4, 8, 128), v(F32, cells, 128),
        v(F32, SIDE, SIDE, TILE, channels), v(F32, SIDE + 6, SIDE + 6, TILE, channels),
        v(B16, 192, channels), v(B16, 192, channels), v(B16, 192, channels), v(B16, 192, channels),
        v(F32, SIDE, SIDE, TILE, channels),
        v(B16, 16, width), v(B16, 2, 16, width), v(B16, 2, N_Y, *quarter), v(B16, 2, N_X * 256, width),
        v(B16, 2, N_Y, *quarter), v(B16, N_Y, *quarter), v(B16, N_Y, *quarter), v(B16, 3, *quarter),
        v(B16, *quarter), v(B16, 3, N_FAR, 16, width), v(F32, N_FAR, 16, width), v(F32, 3, 16, width),
        v(F32, 2, 8, width), v(F32, 8, width),
    ]
    pairs = [(2,), (3,), (2, 3), (2, 3), (2, 3), (2, 3), (3,), (2,), None, (3,), (3,), (3,), (4,)]
    pairs += [(4,), (3,), (3,), (3,), None]
    for p in pairs:
        scratch += [dma if p is None else dma(p)] * 2
    block_out, tile_grad, both = pl.pallas_call(
        functools.partial(block_kernel, rows, width),
        out_shape=[
            jax.ShapeDtypeStruct((channels, cells), B16),
            jax.ShapeDtypeStruct((channels, cells), B16),
            jax.ShapeDtypeStruct((2, 8, width), F32),
        ],
        in_specs=[vmem] * 8,
        out_specs=[vmem] * 3,
        scratch_shapes=scratch,
        compiler_params=pltpu.CompilerParams(
            collective_id=0, has_side_effects=True, vmem_limit_bytes=56 * 1024 * 1024
        ),
    )(tiles, cotangent, land_row, kernel, gain, scale, links, shard)
    return block_out, tile_grad, both[0, :rows], both[1, :rows]


def solution(mesh):
    return jax.shard_map(
        per_device,
        mesh=mesh,
        in_specs=(
            P("fsdp", "dp"),
            P(None, "fsdp"),
            P("fsdp"),
            P("dp", "fsdp"),
            P("dp", "fsdp"),
            P("fsdp"),
            P("dp", None, None),
            P("dp", None, None),
            P("dp", None),
            P("dp", None, None),
            P("fsdp", "dp"),
        ),
        out_specs=(P("fsdp", "dp"), P("fsdp", "dp"), P("dp", "fsdp"), P("dp", "fsdp")),
        check_vma=False,
    )
```

```python
import functools
import math

import jax
import jax.numpy as jnp
from jax import lax
from jax.experimental import pallas as pl
from jax.experimental.pallas import tpu as pltpu
from jax.sharding import PartitionSpec as P

root_half = 1.0 / math.sqrt(2.0)
root_tau = 1.0 / math.sqrt(2.0 * math.pi)

N_Z, N_Y, N_CORE, N_X = 16, 4, 2, 4
N_FAR, N_NEAR = 4, 4
N_DP = N_Z * N_Y * N_CORE
MESH = pl.DeviceIdType.MESH
F32, B16 = jnp.float32, jnp.bfloat16
SIDE, TILE, TAPS = 8, 8, 7
HALF_ROWS = 256


def dp_index(z, y, core):
    return (z * N_Y + y) * N_CORE + core


def dot(a, b):
    return jnp.dot(a, b, preferred_element_type=F32)


def dot_nt(a, b):
    return lax.dot_general(a, b, (((1,), (1,)), ((), ())), preferred_element_type=F32)


def dot_tn(a, b):
    return lax.dot_general(a, b, (((0,), (0,)), ((), ())), preferred_element_type=F32)


def block_kernel(
    rows, width,
    x_ref, cot_ref, land_ref, taps_ref, gain_ref, scale_ref, owner_ref, shift_ref, depth_ref, up_ref, down_ref,
    block_ref, grad_ref, up_grad_ref, down_grad_ref,
    perm, order, picks, taps, xt, go, east_in, west_in, pad, gains,
    gma, gmb, cva, cvb, cen, inv, nrm, gmx, hid, gpre,
    pga, pgb, pgin_a, pgin_b, mxa, mxb, mxin_a, mxin_b, sums, sums_in, sum_cols,
    gcv, gpad, ret_w, ret_e, ret_w_in, ret_e_in, tg,
    unit_in, wfar, wone_a, wone_b, wtwo_a, wtwo_b, dense,
    st_a, st_b, st_in_a, st_in_b, one_a, one_b, one_in_a, one_in_b, two_a, two_b, two_in_a, two_in_b,
    fsum, f_in, last, last_in,
    halo_s, halo_r, gain_s, gain_r, gm_s, gm_r, cv_s, cv_r, pg_s, pg_r, mx_s, mx_r, sum_s, sum_r,
    ret_s, ret_r, wsib_s, wsib_r, wfar_s, wfar_r, wone_s, wone_r, wtwo_s, wtwo_r, wsh_s, wsh_r,
    gsib_s, gsib_r, gone_s, gone_r, gtwo_s, gtwo_r, gfar_s, gfar_r, gend_s, gend_r,
):
    channels = x_ref.shape[0]
    low, high = 128, channels - 128
    cells = x_ref.shape[1]
    me = lax.axis_index("dp")
    x = lax.axis_index("fsdp")
    z, y, core = me // (N_Y * N_CORE), (me // N_CORE) % N_Y, me % N_CORE
    far, near = z // N_NEAR, z % N_NEAR
    east, west = (me + 1) % N_DP, (me + N_DP - 1) % N_DP
    sibling = dp_index(z, y, 1 - core)

    def at_z(step):
        return dp_index((z + step + N_Z) % N_Z, y, core)

    def at_y(k):
        return dp_index(z, (y + k) % N_Y, core)

    def copy(src, dst, send, recv, dp, fs=None):
        return pltpu.make_async_remote_copy(
            src_ref=src, dst_ref=dst, send_sem=send, recv_sem=recv,
            device_id=(dp, x if fs is None else fs), device_id_type=MESH,
        )

    barrier = pltpu.get_barrier_semaphore()
    greeted = [(east, x), (west, x), (sibling, x)]
    greeted += [(me, (x + k) % N_X) for k in range(1, N_X)]
    greeted += [(at_z(s), x) for s in (4, 8, 12, 1, -1, 2, -2)]
    greeted += [(at_y(k), x) for k in range(1, N_Y)]
    for other in greeted:
        pl.semaphore_signal(barrier, inc=1, device_id=other, device_id_type=MESH)

    out_cell = lax.broadcasted_iota(jnp.int32, (cells, cells), 0)
    in_cell = lax.broadcasted_iota(jnp.int32, (cells, cells), 1)
    wanted = (out_cell % 8) * 64 + ((out_cell // 8) % 8) * 8 + out_cell // 64
    perm[...] = jnp.where(in_cell == wanted, 1.0, 0.0).astype(B16)
    xt[...] = dot_nt(perm[...], x_ref[...]).astype(B16)
    j_row = lax.broadcasted_iota(jnp.int32, (SIDE, cells), 0)
    j_col = lax.broadcasted_iota(jnp.int32, (SIDE, cells), 1)
    spread_j = jnp.where(j_row == j_col % SIDE, 1.0, 0.0).astype(B16)
    land = land_ref[...].astype(F32).reshape(TILE * SIDE, SIDE).astype(B16)
    ti_row = lax.broadcasted_iota(jnp.int32, (TILE * SIDE, cells), 0)
    ti_col = lax.broadcasted_iota(jnp.int32, (TILE * SIDE, cells), 1)
    land_row = jnp.sum(
        jnp.where(ti_row == ti_col // SIDE, dot(land, spread_j), 0.0), axis=0, keepdims=True
    ).astype(B16)
    go[...] = dot_nt(perm[...], cot_ref[...] * land_row).astype(B16)
    scale_row = scale_ref[...].astype(F32)
    grad_mixed = (go[...].astype(F32) * scale_row).astype(B16)
    gma[x] = grad_mixed[:, :low]
    gmb[x] = jnp.concatenate([grad_mixed[:HALF_ROWS, low:], grad_mixed[HALF_ROWS:, low:]], axis=1)
    gains[x] = jnp.broadcast_to(gain_ref[...].astype(F32), (8, channels))
    s_row = lax.broadcasted_iota(jnp.int32, (16, rows), 0)
    s_col = lax.broadcasted_iota(jnp.int32, (16, rows), 1)
    unit_in[core] = (
        dot(jnp.where(s_row == s_col, 1.0, 0.0).astype(B16), up_ref[...])
        + dot(jnp.where(s_row == s_col + 8, 1.0, 0.0).astype(B16), down_ref[...])
    ).astype(B16)

    pl.semaphore_wait(barrier, len(greeted))

    halo_west = copy(xt.at[pl.ds(0, 192)], east_in, halo_s.at[0], halo_r.at[0], west)
    halo_east = copy(xt.at[pl.ds(cells - 192, 192)], west_in, halo_s.at[1], halo_r.at[1], east)
    halo_west.start()
    halo_east.start()
    wsib = copy(unit_in.at[core], unit_in.at[core], wsib_s, wsib_r, sibling)
    wsib.start()

    def x_copies(src, dst, send, recv, scatter):
        made = []
        for k in range(1, N_X):
            other = (x + k) % N_X
            if scatter:
                pair = (src.at[other], dst.at[k - 1])
            else:
                pair = (src.at[x], dst.at[x])
            made.append(copy(*pair, send.at[k - 1], recv.at[k - 1], me, other))
        return made

    gain_copies = x_copies(gains, gains, gain_s, gain_r, False)
    gm_copies = x_copies(gma, gma, gm_s.at[0], gm_r.at[0], False)
    gm_copies += x_copies(gmb, gmb, gm_s.at[1], gm_r.at[1], False)
    for c in gain_copies + gm_copies:
        c.start()

    edge_row = lax.broadcasted_iota(jnp.int32, (64, 64), 0)
    edge_col = lax.broadcasted_iota(jnp.int32, (64, 64), 1)
    owners = jnp.concatenate([owner_ref[...]] * 8, axis=0)
    moves = jnp.concatenate([shift_ref[...]] * 8, axis=0)
    depths = jnp.concatenate([depth_ref[...]] * 8, axis=0)
    for face in range(4):
        chosen = jnp.zeros((64, 64), F32)
        for entry in range(2):
            c = face * 2 + entry
            owner = owners[:, c : c + 1]
            shift = moves[:, c : c + 1]
            target = jnp.where(owner >= 0, owner % TILE + TILE * shift, -4096)
            target = target + (edge_row // 8) * 8
            chosen = chosen + jnp.where(target == edge_col, 1.0, 0.0)
        for layer in range(3):
            depth = 3 - layer if face in (0, 2) else layer + 1
            keep = depths[:, face : face + 1] >= depth
            picks[face * 3 + layer] = jnp.where(keep, chosen, 0.0).astype(B16)

    kernel_taps = taps_ref[...].astype(F32)
    for a in range(TAPS):
        for b in range(TAPS):
            k = a * TAPS + b
            taps[b, a] = jnp.broadcast_to(kernel_taps[k : k + 1], (8, channels))

    pad[...] = jnp.zeros_like(pad)
    cells_f = xt[...].astype(F32).reshape(SIDE, SIDE, TILE, channels)
    pad[3 : 3 + SIDE, 3 : 3 + SIDE] = cells_f
    for layer in range(3):
        north = cells_f[:, 5 + layer].reshape(64, channels).astype(B16)
        south = cells_f[:, layer].reshape(64, channels).astype(B16)
        pad[3 : 3 + SIDE, layer] = dot(picks[layer], north).astype(B16).astype(F32).reshape(SIDE, TILE, channels)
        pad[3 : 3 + SIDE, 11 + layer] = (
            dot(picks[3 + layer], south).astype(B16).astype(F32).reshape(SIDE, TILE, channels)
        )

    wsib.wait_recv()
    both = unit_in[...].reshape(N_CORE * 16, width)
    u_row = lax.broadcasted_iota(jnp.int32, (16, N_CORE * 16), 0)
    u_col = lax.broadcasted_iota(jnp.int32, (16, N_CORE * 16), 1)
    first = (u_row < rows) & (u_col == u_row + 8 * core)
    second = (u_row >= rows) & (u_row < 2 * rows) & (u_col == 16 + u_row - rows + 8 * core)
    joined = dot(jnp.where(first | second, 1.0, 0.0).astype(B16), both).astype(B16)
    wfar[far] = joined

    def far_copy(k):
        place = wfar.at[far]
        return copy(place, place, wfar_s.at[k - 1], wfar_r.at[k - 1], at_z(4 * k))

    for k in range(1, N_FAR):
        far_copy(k).start()

    halo_west.wait_recv()
    halo_east.wait_recv()
    for layer in range(3):
        part = pl.ds(layer * 64, 64)
        pad[layer, 3 : 3 + SIDE] = (
            dot(picks[6 + layer], west_in[part]).astype(B16).astype(F32).reshape(SIDE, TILE, channels)
        )
        pad[11 + layer, 3 : 3 + SIDE] = (
            dot(picks[9 + layer], east_in[part]).astype(B16).astype(F32).reshape(SIDE, TILE, channels)
        )

    def conv_column(j, start, size):
        total = jnp.zeros((SIDE, TILE, size), F32)
        for b in range(TAPS):
            source = pad[j + b, :, :, start : start + size]
            for a in range(TAPS):
                total = total + source[a : a + SIDE] * taps[b, a, :, start : start + size][None]
        return total.reshape(64, size).astype(B16)

    def conv_low(j, carry):
        cva[x, pl.ds(pl.multiple_of(j * 64, 64), 64)] = conv_column(j, 0, low)
        return carry

    def conv_high(j, carry):
        cvb[x, pl.ds(pl.multiple_of(j * 64, 64), 64)] = jnp.concatenate(
            [conv_column(j, low, high), conv_column(j + 4, low, high)], axis=1
        )
        return carry

    lax.fori_loop(0, SIDE, conv_low, 0)
    cv_copies = x_copies(cva, cva, cv_s.at[0], cv_r.at[0], False)
    for c in cv_copies:
        c.start()

    for k in range(1, N_FAR):
        far_copy(k).wait_recv()

    near_steps = (1, -1, -2)

    def one_copies():
        made = []
        for k in range(3):
            made.append(
                copy(wone_a.at[near], wone_a.at[near], wone_s.at[0, k], wone_r.at[0, k], at_z(near_steps[k]))
            )
            made.append(copy(wone_b.at[y], wone_b.at[y], wone_s.at[1, k], wone_r.at[1, k], at_y(k + 1)))
        return made

    wone_a[near] = wfar[0:2]
    wone_b[y] = wfar[2:4]
    for c in one_copies():
        c.start()

    lax.fori_loop(0, 4, conv_high, 0)
    high_copies = x_copies(cvb, cvb, cv_s.at[1], cv_r.at[1], False)
    for c in high_copies:
        c.start()

    span = N_CORE * rows
    w_row = lax.broadcasted_iota(jnp.int32, (256, channels), 0)
    w_col = lax.broadcasted_iota(jnp.int32, (256, channels), 1)
    w_from = ((w_row // span) % N_Y) * (span * N_NEAR) + (w_row // (span * N_Y)) * span + w_row % span
    order[...] = jnp.where((w_col == w_from) & (w_row < channels), 1.0, 0.0).astype(B16)
    p_row = lax.broadcasted_iota(jnp.int32, (4 * span, 64), 0)
    p_col = lax.broadcasted_iota(jnp.int32, (4 * span, 64), 1)
    close = jnp.where(p_col == (p_row // span) * 16 + p_row % span, 1.0, 0.0).astype(B16)
    gap_row = lax.broadcasted_iota(jnp.int32, (64, 4 * span), 0)
    gap_col = lax.broadcasted_iota(jnp.int32, (64, 4 * span), 1)
    reopen = jnp.where(gap_row == (gap_col // span) * 16 + gap_col % span, 1.0, 0.0).astype(B16)

    for c in gain_copies + gm_copies:
        c.wait_recv()
    for b in range(N_X):
        gap = jnp.zeros((cells, 256 - channels), B16)
        nrm[:, b * 256 + channels : (b + 1) * 256] = gap
        gmx[:, b * 256 + channels : (b + 1) * 256] = gap
        gmx[:, b * 256 : b * 256 + low] = gma[b]
        packed = gmb[b]
        gmx[:HALF_ROWS, b * 256 + low : b * 256 + channels] = packed[:, :high]
        gmx[HALF_ROWS:, b * 256 + low : b * 256 + channels] = packed[:, high:]

    def two_copies():
        made = []
        for k in range(3):
            place = wtwo_a.at[core, y]
            made.append(copy(place, place, wtwo_s.at[0, k], wtwo_r.at[0, k], at_y(k + 1)))
            place = wtwo_b.at[core, near]
            made.append(copy(place, place, wtwo_s.at[1, k], wtwo_r.at[1, k], at_z(near_steps[k])))
        return made

    def share_a(k):
        place = wtwo_a.at[core, (y + N_Y - k) % N_Y]
        return copy(place, place, wsh_s.at[0, k], wsh_r.at[0, k], sibling)

    def share_b(k):
        step = 0 if k == 0 else near_steps[k - 1]
        place = wtwo_b.at[core, (near - step + N_NEAR) % N_NEAR]
        return copy(place, place, wsh_s.at[1, k], wsh_r.at[1, k], sibling)

    for c in one_copies():
        c.wait_recv()
    for f in range(2):
        rows_a = jnp.concatenate([wone_a[nn, f] for nn in range(N_NEAR)], axis=0)
        wtwo_a[core, y, f] = dot(close, rows_a).astype(B16)
        rows_b = jnp.concatenate([wone_b[yy, f] for yy in range(N_Y)], axis=0)
        wtwo_b[core, near, f] = dot(close, rows_b).astype(B16)
    for c in two_copies():
        c.start()
    share_a(0).start()
    share_b(0).start()

    for c in cv_copies + high_copies:
        c.wait_recv()

    wide = float(channels * N_X)
    for half in range(2):

        def norm_rows(i, carry, half=half):
            part = pl.ds(pl.multiple_of(i * 64, 64), 64)
            here = pl.ds(pl.multiple_of(half * HALF_ROWS + i * 64, 64), 64)
            lows = [cva[b, here].astype(F32) for b in range(N_X)]
            highs = [cvb[b, part, half * high : (half + 1) * high].astype(F32) for b in range(N_X)]
            total = jnp.sum(sum(lows), axis=1, keepdims=True) + jnp.sum(sum(highs), axis=1, keepdims=True)
            square = jnp.sum(sum(v * v for v in lows), axis=1, keepdims=True) + jnp.sum(
                sum(v * v for v in highs), axis=1, keepdims=True
            )
            mean = total / wide
            scale = lax.rsqrt(square / wide - mean * mean + 1e-06)
            inv[here] = jnp.broadcast_to(scale, (64, 128))
            for b in range(N_X):
                centered = (lows[b] - mean) * scale
                cen[b, here, 0:low] = centered
                nrm[here, b * 256 : b * 256 + low] = (centered * gains[b, 0:1, 0:low]).astype(B16)
                centered = (highs[b] - mean) * scale
                cen[b, here, low:channels] = centered
                nrm[here, b * 256 + low : b * 256 + channels] = (
                    centered * gains[b, 0:1, low:channels]
                ).astype(B16)
            return carry

        lax.fori_loop(0, 4, norm_rows, 0)
        if half == 0:
            arrived = two_copies()
            for k in range(1, 4):
                arrived[2 * k - 2].wait_recv()
                share_a(k).start()
                arrived[2 * k - 1].wait_recv()
                share_b(k).start()

    for k in range(4):
        share_a(k).wait_recv()
        share_b(k).wait_recv()
    for m in range(2):
        for f in range(2):
            rows_a = jnp.concatenate([wtwo_a[m, yy, f] for yy in range(N_Y)], axis=0)
            dense[m, f * 256 : (f + 1) * 256] = dot(order[...], rows_a).astype(B16)
            for nn in range(N_NEAR):
                r = (f + 2) * 256 + nn * 4 * span
                dense[m, r : r + 4 * span] = wtwo_b[m, nn, f]
            dense[m, (f + 2) * 256 + channels : (f + 3) * 256] = jnp.zeros((256 - channels, width), B16)

    pg_copies, sum_copies = [], []
    for half in range(2):
        for i in range(2):
            start = half * HALF_ROWS + i * 128
            here = slice(start, start + 128)
            part = slice(half * 128, half * 128 + 128)
            pre = dot(nrm[here], dense[0])
            edge = 0.5 * (1.0 + lax.erf(pre * root_half))
            hid[here] = (pre * edge).astype(B16)
            slope = edge + pre * jnp.exp(-0.5 * pre * pre) * root_tau
            grad_pre = (dot(gmx[here], dense[1]) * slope).astype(B16)
            gpre[here] = grad_pre
            back = dot_nt(grad_pre, dense[0]).astype(B16)
            first_sum = jnp.zeros((128, 128), F32)
            second_sum = jnp.zeros((128, 128), F32)
            first_high = jnp.zeros((128, high), F32)
            second_high = jnp.zeros((128, high), F32)
            for b in range(N_X):
                low_part = back[:, b * 256 : b * 256 + low]
                high_part = back[:, b * 256 + low : b * 256 + channels]
                pga[b, here] = low_part
                pgb[b, part, i * high : (i + 1) * high] = high_part
                g = low_part.astype(F32) * gains[b, 0:1, 0:low]
                first_sum += g
                second_sum += g * cen[b, here, 0:low]
                g = high_part.astype(F32) * gains[b, 0:1, low:channels]
                first_high += g
                second_high += g * cen[b, here, low:channels]
            one = jnp.sum(first_sum, axis=1, keepdims=True) + jnp.sum(first_high, axis=1, keepdims=True)
            two = jnp.sum(second_sum, axis=1, keepdims=True) + jnp.sum(second_high, axis=1, keepdims=True)
            lane = lax.broadcasted_iota(jnp.int32, (128, 128), 1)
            columns = jnp.where(lane == 0, one, jnp.where(lane == 1, two, 0.0))
            sums[half, i] = jnp.transpose(columns)[0:8]
        made = []
        for k in range(1, N_X):
            other = (x + k) % N_X
            part = pl.ds(half * HALF_ROWS, HALF_ROWS)
            made.append(
                copy(pga.at[other, part], pgin_a.at[k - 1, part], pg_s.at[half, 0, k - 1], pg_r.at[half, 0, k - 1], me, other)
            )
            part = pl.ds(half * 128, 128)
            made.append(
                copy(pgb.at[other, part], pgin_b.at[k - 1, part], pg_s.at[half, 1, k - 1], pg_r.at[half, 1, k - 1], me, other)
            )
            made.append(
                copy(sums.at[half], sums_in.at[k - 1, half], sum_s.at[half, k - 1], sum_r.at[half, k - 1], me, other)
            )
        for c in made:
            c.start()
        pg_copies.append(made)

    for b in range(N_X):
        for m, left, right in ((0, nrm, gpre), (1, gmx, hid)):
            local = dot_tn(left[:, b * 256 : (b + 1) * 256], right[...]).astype(B16)
            if b < 2:
                local = dot_tn(order[...], local).astype(B16)
            for q in range(4):
                r = q * 4 * span
                if b < 2:
                    st_a[m, q, b] = local[r : r + 4 * span]
                else:
                    st_b[m, q, b - 2] = local[r : r + 4 * span]

    back_steps = (-1, 1, 2)

    def one_place(k):
        step = 0 if k == 0 else back_steps[k - 1]
        return (y + k) % N_Y, (near + step + N_NEAR) % N_NEAR

    def gsib_copies(k):
        yy, nn = one_place(k)
        return (
            copy(st_a.at[1 - core, yy], st_in_a.at[yy], gsib_s.at[0, k], gsib_r.at[0, k], sibling),
            copy(st_b.at[1 - core, nn], st_in_b.at[nn], gsib_s.at[1, k], gsib_r.at[1, k], sibling),
        )

    for k in (1, 2, 3, 0):
        for c in gsib_copies(k):
            c.start()

    def gone_copies(k):
        return (
            copy(one_a.at[k], one_in_a.at[k - 1], gone_s.at[0, k - 1], gone_r.at[0, k - 1], at_y(k)),
            copy(
                one_b.at[k], one_in_b.at[k - 1], gone_s.at[1, k - 1], gone_r.at[1, k - 1], at_z(back_steps[k - 1])
            ),
        )

    for k in (1, 2, 3, 0):
        yy, nn = one_place(k)
        over_y, over_z = gsib_copies(k)
        over_y.wait_recv()
        one_a[k] = (st_a[core, yy].astype(F32) + st_in_a[yy].astype(F32)).astype(B16)
        if k > 0:
            gone_copies(k)[0].start()
        over_z.wait_recv()
        one_b[k] = (st_b[core, nn].astype(F32) + st_in_b[nn].astype(F32)).astype(B16)
        if k > 0:
            gone_copies(k)[1].start()

    for half in range(2):

        def out_rows(i, carry, half=half):
            part = pl.ds(pl.multiple_of(i * 128, 128), 128)
            here = pl.ds(pl.multiple_of(half * HALF_ROWS + i * 128, 128), 128)
            mixed = dot_nt(hid[here], dense[1]).astype(B16)
            for b in range(N_X):
                mxa[b, here] = mixed[:, b * 256 : b * 256 + low]
                mxb[b, part, half * high : (half + 1) * high] = mixed[:, b * 256 + low : b * 256 + channels]
            return carry

        lax.fori_loop(0, 2, out_rows, 0)

    mx_copies = x_copies(mxa, mxin_a, mx_s.at[0], mx_r.at[0], True)
    mx_copies += x_copies(mxb, mxin_b, mx_s.at[1], mx_r.at[1], True)
    for c in mx_copies:
        c.start()

    gcv[...] = jnp.zeros_like(gcv)
    for half in range(2):
        for c in pg_copies[half]:
            c.wait_recv()
        for i in range(2):
            total = sums[half, i]
            for k in range(N_X - 1):
                total = total + sums_in[k, half, i]
            spread = jnp.concatenate([total / wide, jnp.zeros((120, 128), F32)], axis=0)
            sum_cols[...] = jnp.transpose(spread)
            lanes = slice(i * high, (i + 1) * high)

            def back_rows(n, carry, half=half, i=i, lanes=lanes):
                column = half * 4 + i * 2 + n
                part = pl.ds(pl.multiple_of(half * 128 + n * 64, 64), 64)
                here = pl.ds(pl.multiple_of(column * 64, 64), 64)
                low_part = pga[x, here].astype(F32)
                high_part = pgb[x, part, lanes].astype(F32)
                for k in range(N_X - 1):
                    low_part = low_part + pgin_a[k, here].astype(F32)
                    high_part = high_part + pgin_b[k, part, lanes].astype(F32)
                local = pl.ds(pl.multiple_of(n * 64, 64), 64)
                e1 = sum_cols[local, 0:1]
                e2 = sum_cols[local, 1:2]
                scale = inv[here]
                g = low_part * gains[x, 0:1, 0:low]
                g = scale * (g - e1 - cen[x, here, 0:low] * e2)
                gcv[column, :, :, 0:low] = g.astype(B16).astype(F32).reshape(SIDE, TILE, low)
                g = high_part * gains[x, 0:1, low:channels]
                g = scale[:, :high] * (g - e1 - cen[x, here, low:channels] * e2)
                gcv[column, :, :, low:channels] = g.astype(B16).astype(F32).reshape(SIDE, TILE, high)
                return carry

            lax.fori_loop(0, 2, back_rows, 0)

    def spread_column(j, start, size):
        def add_tap(b, totals):
            totals = list(totals)
            source = gcv[j - b, :, :, start : start + size]
            for a in range(TAPS):
                tap = taps[b, a, :, start : start + size]
                for i in range(SIDE):
                    totals[i + a] = totals[i + a] + source[i] * tap
            return tuple(totals)

        empty = tuple(jnp.zeros((TILE, size), F32) for _ in range(SIDE + 6))
        first_tap = jnp.maximum(0, j - (SIDE - 1))
        end_tap = jnp.minimum(TAPS, j + 1)
        totals = lax.fori_loop(first_tap, end_tap, add_tap, empty)
        for i in range(SIDE + 6):
            gpad[j, i, :, start : start + size] = totals[i]

    def spread_edge(j, carry):
        for k in (j, j + 11):
            spread_column(k, 0, low)
            spread_column(k, low, high)
        return carry

    def spread_inner(j, carry):
        spread_column(j, 0, low)
        spread_column(j, low, high)
        return carry

    lax.fori_loop(0, 3, spread_edge, 0)
    for layer in range(3):
        part = pl.ds(layer * 64, 64)
        for face, column, held in ((2, layer, ret_w), (3, 11 + layer, ret_e)):
            edge = gpad[column, 3 : 3 + SIDE].reshape(64, channels).astype(B16)
            held[part] = dot_tn(picks[face * 3 + layer], edge).astype(B16)
    ret_west = copy(ret_w, ret_w_in, ret_s.at[0], ret_r.at[0], west)
    ret_east = copy(ret_e, ret_e_in, ret_s.at[1], ret_r.at[1], east)
    ret_west.start()
    ret_east.start()

    def gtwo_copies(k):
        yy, nn = one_place(k)
        return (
            copy(two_a.at[nn], two_in_a.at[k - 1], gtwo_s.at[0, k - 1], gtwo_r.at[0, k - 1], at_z(back_steps[k - 1])),
            copy(two_b.at[yy], two_in_b.at[k - 1], gtwo_s.at[1, k - 1], gtwo_r.at[1, k - 1], at_y(k)),
        )

    for k in range(1, 4):
        for c in gone_copies(k):
            c.wait_recv()
    for f in range(2):
        for mine, came, units in ((one_a, one_in_a, two_a), (one_b, one_in_b, two_b)):
            total = mine[0, f].astype(F32)
            for k in range(3):
                total = total + came[k, f].astype(F32)
            opened = dot(reopen, total.astype(B16)).astype(B16)
            for q in range(4):
                units[q, f] = opened[q * 16 : (q + 1) * 16]
    for k in range(1, 4):
        for c in gtwo_copies(k):
            c.start()

    lax.fori_loop(3, 11, spread_inner, 0)

    for k in range(1, 4):
        for c in gtwo_copies(k):
            c.wait_recv()
    total = two_a[near].astype(F32)
    other_total = two_b[y].astype(F32)
    for k in range(3):
        total = total + two_in_a[k].astype(F32)
        other_total = other_total + two_in_b[k].astype(F32)
    fsum[0:2] = total
    fsum[2:4] = other_total

    def gfar_copy(k):
        return copy(
            fsum.at[(far + k) % N_FAR], f_in.at[k - 1], gfar_s.at[k - 1], gfar_r.at[k - 1], at_z(4 * k)
        )

    for k in range(1, N_FAR):
        gfar_copy(k).start()

    tg[...] = go[...].astype(F32).reshape(SIDE, SIDE, TILE, channels) + gpad[3 : 3 + SIDE, 3 : 3 + SIDE]
    for layer in range(3):
        for face, row, target in ((0, layer, 5 + layer), (1, 11 + layer, layer)):
            edge = gpad[3 : 3 + SIDE, row].reshape(64, channels).astype(B16)
            back = dot_tn(picks[face * 3 + layer], edge)
            tg[:, target] = tg[:, target] + back.reshape(SIDE, TILE, channels)

    for c in mx_copies:
        c.wait_recv()
    low_part = mxa[x].astype(F32)
    packed = mxb[x].astype(F32)
    for k in range(N_X - 1):
        low_part = low_part + mxin_a[k].astype(F32)
        packed = packed + mxin_b[k].astype(F32)
    high_part = jnp.concatenate([packed[:, :high], packed[:, high:]], axis=0)
    mixed = jnp.concatenate([low_part, high_part], axis=1)
    out = (xt[...].astype(F32) + scale_row * mixed).astype(B16)
    block_ref[...] = dot_tn(out, perm[...]).astype(B16)

    for k in range(1, N_FAR):
        gfar_copy(k).wait_recv()
    total = fsum[far]
    for k in range(1, N_FAR):
        total = total + f_in[k - 1]
    last[0, 0:8] = total[0:8]
    last[1, 0:8] = total[rows : rows + 8]
    gend = copy(last.at[1 - core], last_in.at[core], gend_s, gend_r, sibling)
    gend.start()
    last_in[core] = last[core]

    ret_west.wait_recv()
    ret_east.wait_recv()
    for layer in range(3):
        part = pl.ds(layer * 64, 64)
        tg[5 + layer] = tg[5 + layer] + ret_w_in[part].astype(F32).reshape(SIDE, TILE, channels)
        tg[layer] = tg[layer] + ret_e_in[part].astype(F32).reshape(SIDE, TILE, channels)
    grad_ref[...] = dot_tn(tg[...].reshape(cells, channels).astype(B16), perm[...]).astype(B16)

    gend.wait_recv()
    up_grad_ref[...] = last_in[0, 0:rows]
    down_grad_ref[...] = last_in[1, 0:rows]

    sent = [halo_west, halo_east, wsib, ret_west, ret_east, gend]
    sent += gain_copies + gm_copies + cv_copies + high_copies + mx_copies + pg_copies[0] + pg_copies[1]
    sent += [far_copy(k) for k in range(1, N_FAR)] + one_copies() + two_copies()
    sent += [share_a(k) for k in range(4)] + [share_b(k) for k in range(4)]
    for k in range(4):
        sent += gsib_copies(k)
    for k in range(1, 4):
        sent += gone_copies(k) + gtwo_copies(k)
    sent += [gfar_copy(k) for k in range(1, N_FAR)]
    for c in sent:
        c.wait_send()


def per_device(
    tiles, kernel, norm_gain, w_up, w_down, layer_scale, neighbors, shifts, halo_widths, land, cotangent
):
    channels, cells = tiles.shape
    rows, width = w_up.shape
    vmem = pl.BlockSpec(memory_space=pltpu.VMEM)
    dma = pltpu.SemaphoreType.DMA

    def v(dtype, *shape):
        return pltpu.VMEM(shape, dtype)

    strip = (2, 8 * rows, width)
    units = (2, 16, width)
    scratch = [
        v(B16, cells, cells), v(B16, 256, channels), v(B16, 12, 64, 64), v(F32, TAPS, TAPS, 8, channels),
        v(B16, cells, channels), v(B16, cells, channels), v(B16, 192, channels), v(B16, 192, channels),
        v(F32, SIDE + 6, SIDE + 6, TILE, channels), v(F32, N_X, 8, channels),
        v(B16, N_X, cells, 128), v(B16, N_X, HALF_ROWS, 128), v(B16, N_X, cells, 128), v(B16, N_X, HALF_ROWS, 128),
        v(F32, N_X, cells, channels), v(F32, cells, 128), v(B16, cells, N_X * 256), v(B16, cells, N_X * 256),
        v(B16, cells, width), v(B16, cells, width),
        v(B16, N_X, cells, 128), v(B16, N_X, HALF_ROWS, 128), v(B16, 3, cells, 128), v(B16, 3, HALF_ROWS, 128),
        v(B16, N_X, cells, 128), v(B16, N_X, HALF_ROWS, 128), v(B16, 3, cells, 128), v(B16, 3, HALF_ROWS, 128),
        v(F32, 2, 2, 8, 128), v(F32, 3, 2, 2, 8, 128), v(F32, 128, 128),
        v(F32, SIDE, SIDE, TILE, channels), v(F32, SIDE + 6, SIDE + 6, TILE, channels),
        v(B16, 192, channels), v(B16, 192, channels), v(B16, 192, channels), v(B16, 192, channels),
        v(F32, SIDE, SIDE, TILE, channels),
        v(B16, 2, 16, width), v(B16, N_FAR, 16, width), v(B16, 4, *units), v(B16, 4, *units),
        v(B16, 2, 4, *strip), v(B16, 2, 4, *strip), v(B16, 2, N_X * 256, width),
        v(B16, 2, 4, *strip), v(B16, 2, 4, *strip), v(B16, 4, *strip), v(B16, 4, *strip),
        v(B16, 4, *strip), v(B16, 4, *strip), v(B16, 3, *strip), v(B16, 3, *strip),
        v(B16, 4, *units), v(B16, 4, *units), v(B16, 3, *units), v(B16, 3, *units),
        v(F32, N_FAR, 16, width), v(F32, 3, 16, width), v(F32, 2, 8, width), v(F32, 2, 8, width),
    ]
    pairs = [(2,), (3,), (2, 3), (2, 3), (2, 2, 3), (2, 3), (2, 3), (2,), None, (3,), (2, 3), (2, 3), (2, 4)]
    pairs += [(2, 4), (2, 3), (2, 3), (3,), None]
    for p in pairs:
        scratch += [dma if p is None else dma(p)] * 2
    return pl.pallas_call(
        functools.partial(block_kernel, rows, width),
        out_shape=[
            jax.ShapeDtypeStruct((channels, cells), B16),
            jax.ShapeDtypeStruct((channels, cells), B16),
            jax.ShapeDtypeStruct((rows, width), F32),
            jax.ShapeDtypeStruct((rows, width), F32),
        ],
        in_specs=[vmem] * 11,
        out_specs=[vmem] * 4,
        scratch_shapes=scratch,
        compiler_params=pltpu.CompilerParams(
            collective_id=0, has_side_effects=True, vmem_limit_bytes=56 * 1024 * 1024
        ),
    )(
        tiles, cotangent, land, kernel, norm_gain.reshape(1, channels), layer_scale.reshape(1, channels),
        neighbors.reshape(TILE, 8), shifts.reshape(TILE, 8), halo_widths, w_up, w_down,
    )


def solution(mesh):
    return jax.shard_map(
        per_device,
        mesh=mesh,
        in_specs=(
            P("fsdp", "dp"),
            P(None, "fsdp"),
            P("fsdp"),
            P("dp", "fsdp"),
            P("dp", "fsdp"),
            P("fsdp"),
            P("dp", None, None),
            P("dp", None, None),
            P("dp", None),
            P("dp", None, None),
            P("fsdp", "dp"),
        ),
        out_specs=(P("fsdp", "dp"), P("fsdp", "dp"), P("dp", "fsdp"), P("dp", "fsdp")),
        check_vma=False,
    )
```

```python
import functools
import math

import jax
import jax.numpy as jnp
from jax import lax
from jax.experimental import pallas as pl
from jax.experimental.pallas import tpu as pltpu
from jax.sharding import PartitionSpec as P

root_half = 1.0 / math.sqrt(2.0)
root_tau = 1.0 / math.sqrt(2.0 * math.pi)

N_Z, N_Y, N_CORE, N_X = 16, 4, 2, 4
N_FAR, N_NEAR = 4, 4
N_DP = N_Z * N_Y * N_CORE
MESH = pl.DeviceIdType.MESH
F32, B16 = jnp.float32, jnp.bfloat16
SIDE, TILE, TAPS = 8, 8, 7
HALF_ROWS = 256


def dp_index(z, y, core):
    return (z * N_Y + y) * N_CORE + core


def dot(a, b):
    return jnp.dot(a, b, preferred_element_type=F32)


def dot_nt(a, b):
    return lax.dot_general(a, b, (((1,), (1,)), ((), ())), preferred_element_type=F32)


def dot_tn(a, b):
    return lax.dot_general(a, b, (((0,), (0,)), ((), ())), preferred_element_type=F32)


def block_kernel(
    rows, width,
    x_ref, cot_ref, land_ref, taps_ref, gain_ref, scale_ref, owner_ref, shift_ref, depth_ref, up_ref, down_ref,
    block_ref, grad_ref, up_grad_ref, down_grad_ref,
    perm, order, picks, taps, xt, go, east_in, west_in, pad, gains,
    gma, gmb, cva, cvb, cen, inv, nrm, gmx, hid, gpre,
    pga, pgb, pgin_a, pgin_b, pgre_a, pgre_b, mxa, mxb, mxin_a, mxin_b, mxre_a, mxre_b, sums, sums_in, sum_cols,
    gcv, gpad, ret_w, ret_e, ret_w_in, ret_e_in, tg,
    unit_in, wfar, wone_a, wone_b, wtwo_a, wtwo_b, dense,
    st_a, st_b, st_in_a, st_in_b, one_a, one_b, one_in_a, one_in_b, two_a, two_b, two_in_a, two_in_b,
    fsum, f_in, last, last_in,
    x_in, cot_in, in_sem, halo_s, halo_r, gain_s, gain_r, gm_s, gm_r, cv_s, cv_r, pg_s, pg_r, mx_s, mx_r, sum_s, sum_r,
    ret_s, ret_r, wsib_s, wsib_r, wfar_s, wfar_r, wone_s, wone_r, wtwo_s, wtwo_r, wsh_s, wsh_r,
    gsib_s, gsib_r, gone_s, gone_r, gtwo_s, gtwo_r, gfar_s, gfar_r, gend_s, gend_r,
):
    channels = x_ref.shape[0]
    low, high = 128, channels - 128
    cells = x_ref.shape[1]
    me = lax.axis_index("dp")
    x = lax.axis_index("fsdp")
    z, y, core = me // (N_Y * N_CORE), (me // N_CORE) % N_Y, me % N_CORE
    far, near = z // N_NEAR, z % N_NEAR
    east, west = (me + 1) % N_DP, (me + N_DP - 1) % N_DP
    sibling = dp_index(z, y, 1 - core)

    def at_z(step):
        return dp_index((z + step + N_Z) % N_Z, y, core)

    def at_y(k):
        return dp_index(z, (y + k) % N_Y, core)

    def copy(src, dst, send, recv, dp, fs=None):
        return pltpu.make_async_remote_copy(
            src_ref=src, dst_ref=dst, send_sem=send, recv_sem=recv,
            device_id=(dp, x if fs is None else fs), device_id_type=MESH,
        )

    barrier = pltpu.get_barrier_semaphore()
    greeted = [(east, x), (west, x), (sibling, x)]
    greeted += [(me, (x + k) % N_X) for k in range(1, N_X)]
    greeted += [(at_z(s), x) for s in (4, 8, 12, 1, -1, 2, -2)]
    greeted += [(at_y(k), x) for k in range(1, N_Y)]
    for other in greeted:
        pl.semaphore_signal(barrier, inc=1, device_id=other, device_id_type=MESH)
    x_load = pltpu.make_async_copy(x_ref, x_in, in_sem.at[0])
    cot_load = pltpu.make_async_copy(cot_ref, cot_in, in_sem.at[1])
    x_load.start()
    cot_load.start()

    out_cell = lax.broadcasted_iota(jnp.int32, (cells, cells), 0)
    in_cell = lax.broadcasted_iota(jnp.int32, (cells, cells), 1)
    wanted = (out_cell % 8) * 64 + ((out_cell // 8) % 8) * 8 + out_cell // 64
    perm[...] = jnp.where(in_cell == wanted, 1.0, 0.0).astype(B16)
    x_load.wait()
    xt[...] = dot_nt(perm[...], x_in[...]).astype(B16)
    cot_load.wait()
    j_row = lax.broadcasted_iota(jnp.int32, (SIDE, cells), 0)
    j_col = lax.broadcasted_iota(jnp.int32, (SIDE, cells), 1)
    spread_j = jnp.where(j_row == j_col % SIDE, 1.0, 0.0).astype(B16)
    land = land_ref[...].astype(F32).reshape(TILE * SIDE, SIDE).astype(B16)
    ti_row = lax.broadcasted_iota(jnp.int32, (TILE * SIDE, cells), 0)
    ti_col = lax.broadcasted_iota(jnp.int32, (TILE * SIDE, cells), 1)
    land_row = jnp.sum(
        jnp.where(ti_row == ti_col // SIDE, dot(land, spread_j), 0.0), axis=0, keepdims=True
    ).astype(B16)
    go[...] = dot_nt(perm[...], cot_in[...] * land_row).astype(B16)
    scale_row = scale_ref[...].astype(F32).reshape(1, channels)
    grad_mixed = (go[...].astype(F32) * scale_row).astype(B16)
    gma[x] = grad_mixed[:, :low]
    gmb[x] = jnp.concatenate([grad_mixed[:HALF_ROWS, low:], grad_mixed[HALF_ROWS:, low:]], axis=1)
    gains[x] = jnp.broadcast_to(gain_ref[...].astype(F32).reshape(1, channels), (8, channels))
    s_row = lax.broadcasted_iota(jnp.int32, (16, rows), 0)
    s_col = lax.broadcasted_iota(jnp.int32, (16, rows), 1)
    unit_in[core] = (
        dot(jnp.where(s_row == s_col, 1.0, 0.0).astype(B16), up_ref[...])
        + dot(jnp.where(s_row == s_col + 8, 1.0, 0.0).astype(B16), down_ref[...])
    ).astype(B16)

    pl.semaphore_wait(barrier, len(greeted))

    halo_west = copy(xt.at[pl.ds(0, 192)], east_in, halo_s.at[0], halo_r.at[0], west)
    halo_east = copy(xt.at[pl.ds(cells - 192, 192)], west_in, halo_s.at[1], halo_r.at[1], east)
    halo_west.start()
    halo_east.start()
    wsib = copy(unit_in.at[core], unit_in.at[core], wsib_s, wsib_r, sibling)
    wsib.start()

    right, left, across = (x + 1) % N_X, (x + N_X - 1) % N_X, (x + 2) % N_X

    def gather_first(buffer, send, recv):
        return [
            copy(buffer.at[x], buffer.at[x], send.at[0], recv.at[0], me, right),
            copy(buffer.at[x], buffer.at[x], send.at[1], recv.at[1], me, left),
        ]

    def gather_next(buffer, send, recv):
        count = buffer.shape[1] // 2
        head, tail = pl.ds(0, count), pl.ds(count, count)
        return [
            copy(buffer.at[left, head], buffer.at[left, head], send.at[2], recv.at[2], me, right),
            copy(buffer.at[right, tail], buffer.at[right, tail], send.at[3], recv.at[3], me, left),
        ]

    def forward(first, later):
        for c, n in zip(first, later):
            c.wait_recv()
            n.start()

    gain_copies = []
    for k in range(1, N_X):
        gain_copies.append(
            copy(gains.at[x], gains.at[x], gain_s.at[k - 1], gain_r.at[k - 1], me, (x + k) % N_X)
        )
    gm_first = gather_first(gma, gm_s.at[0], gm_r.at[0]), gather_first(gmb, gm_s.at[1], gm_r.at[1])
    gm_next = gather_next(gma, gm_s.at[0], gm_r.at[0]), gather_next(gmb, gm_s.at[1], gm_r.at[1])
    for c in gm_first[0] + gm_first[1] + gain_copies:
        c.start()

    def scatter_copies(held, came, relay, send, recv, half):
        toward, away = (right, left) if half == 0 else (left, right)
        made = []
        for p in range(2):
            count = held[p].shape[1] // 2
            part = pl.ds(half * count, count)
            made.append((
                copy(held[p].at[across, part], relay[p].at[half], send.at[half, 0, p], recv.at[half, 0, p], me, toward),
                copy(
                    held[p].at[away, part], came[p].at[1 - half, part], send.at[half, 1, p], recv.at[half, 1, p], me, away
                ),
                copy(
                    held[p].at[toward, part], came[p].at[half, part], send.at[half, 2, p], recv.at[half, 2, p], me, toward
                ),
            ))
        return made

    def relay_on(held, relay, made, half):
        toward = right if half == 0 else left
        for p in range(2):
            count = held[p].shape[1] // 2
            part = pl.ds(half * count, count)
            made[p][0].wait_recv()
            held[p][toward, part] = (held[p][toward, part].astype(F32) + relay[p][half].astype(F32)).astype(B16)
            made[p][2].start()

    pg_made = [scatter_copies((pga, pgb), (pgin_a, pgin_b), (pgre_a, pgre_b), pg_s, pg_r, h) for h in range(2)]
    mx_made = [scatter_copies((mxa, mxb), (mxin_a, mxin_b), (mxre_a, mxre_b), mx_s, mx_r, h) for h in range(2)]

    edge_row = lax.broadcasted_iota(jnp.int32, (64, 64), 0)
    for face in range(4):
        chosen = jnp.zeros((64, 64), F32)
        for entry in range(2):
            owner = owner_ref[face, entry : entry + 1, :]
            shift = shift_ref[face, entry : entry + 1, :]
            target = jnp.where(owner >= 0, owner % TILE + TILE * shift, -4096)
            target = jnp.concatenate([target + TILE * p for p in range(SIDE)], axis=1)
            chosen = chosen + jnp.where(target == edge_row, 1.0, 0.0)
        widths = jnp.concatenate([depth_ref[face : face + 1, :]] * SIDE, axis=1)
        for layer in range(3):
            depth = 3 - layer if face in (0, 2) else layer + 1
            picks[face * 3 + layer] = jnp.where(widths >= depth, chosen, 0.0).astype(B16)

    kernel_taps = taps_ref[...].astype(F32)
    for a in range(TAPS):
        for b in range(TAPS):
            k = a * TAPS + b
            taps[b, a] = jnp.broadcast_to(kernel_taps[k : k + 1], (8, channels))

    pad[...] = jnp.zeros_like(pad)
    cells_f = xt[...].astype(F32).reshape(SIDE, SIDE, TILE, channels)
    pad[3 : 3 + SIDE, 3 : 3 + SIDE] = cells_f
    for layer in range(3):
        north = cells_f[:, 5 + layer].reshape(64, channels).astype(B16)
        south = cells_f[:, layer].reshape(64, channels).astype(B16)
        pad[3 : 3 + SIDE, layer] = dot_tn(picks[layer], north).astype(B16).astype(F32).reshape(SIDE, TILE, channels)
        pad[3 : 3 + SIDE, 11 + layer] = (
            dot_tn(picks[3 + layer], south).astype(B16).astype(F32).reshape(SIDE, TILE, channels)
        )

    wsib.wait_recv()
    both = unit_in[...].reshape(N_CORE * 16, width)
    u_row = lax.broadcasted_iota(jnp.int32, (16, N_CORE * 16), 0)
    u_col = lax.broadcasted_iota(jnp.int32, (16, N_CORE * 16), 1)
    first = (u_row < rows) & (u_col == u_row + 8 * core)
    second = (u_row >= rows) & (u_row < 2 * rows) & (u_col == 16 + u_row - rows + 8 * core)
    joined = dot(jnp.where(first | second, 1.0, 0.0).astype(B16), both).astype(B16)
    wfar[far] = joined

    def far_copy(k):
        place = wfar.at[far]
        return copy(place, place, wfar_s.at[k - 1], wfar_r.at[k - 1], at_z(4 * k))

    for k in range(1, N_FAR):
        far_copy(k).start()

    halo_west.wait_recv()
    halo_east.wait_recv()
    for layer in range(3):
        part = pl.ds(layer * 64, 64)
        pad[layer, 3 : 3 + SIDE] = (
            dot_tn(picks[6 + layer], west_in[part]).astype(B16).astype(F32).reshape(SIDE, TILE, channels)
        )
        pad[11 + layer, 3 : 3 + SIDE] = (
            dot_tn(picks[9 + layer], east_in[part]).astype(B16).astype(F32).reshape(SIDE, TILE, channels)
        )

    def conv_column(j, start, size):
        total = jnp.zeros((SIDE, TILE, size), F32)
        for b in range(TAPS):
            source = pad[j + b, :, :, start : start + size]
            for a in range(TAPS):
                total = total + source[a : a + SIDE] * taps[b, a, :, start : start + size][None]
        return total.reshape(64, size).astype(B16)

    def conv_low(j, carry):
        cva[x, pl.ds(pl.multiple_of(j * 64, 64), 64)] = conv_column(j, 0, low)
        return carry

    def conv_high(j, carry):
        cvb[x, pl.ds(pl.multiple_of(j * 64, 64), 64)] = jnp.concatenate(
            [conv_column(j, low, high), conv_column(j + 4, low, high)], axis=1
        )
        return carry

    lax.fori_loop(0, SIDE, conv_low, 0)
    cv_first = gather_first(cva, cv_s.at[0], cv_r.at[0])
    cv_next = gather_next(cva, cv_s.at[0], cv_r.at[0])
    for c in cv_first:
        c.start()

    for k in range(1, N_FAR):
        far_copy(k).wait_recv()

    near_steps = (1, -1, -2)

    def one_copies():
        made = []
        for k in range(3):
            made.append(
                copy(wone_a.at[near], wone_a.at[near], wone_s.at[0, k], wone_r.at[0, k], at_z(near_steps[k]))
            )
            made.append(copy(wone_b.at[y], wone_b.at[y], wone_s.at[1, k], wone_r.at[1, k], at_y(k + 1)))
        return made

    wone_a[near] = wfar[0:2]
    wone_b[y] = wfar[2:4]
    for c in one_copies():
        c.start()

    lax.fori_loop(0, 4, conv_high, 0)
    high_first = gather_first(cvb, cv_s.at[1], cv_r.at[1])
    high_next = gather_next(cvb, cv_s.at[1], cv_r.at[1])
    for c in high_first:
        c.start()
    forward(gm_first[0], gm_next[0])
    forward(gm_first[1], gm_next[1])

    span = N_CORE * rows
    w_row = lax.broadcasted_iota(jnp.int32, (256, channels), 0)
    w_col = lax.broadcasted_iota(jnp.int32, (256, channels), 1)
    w_from = ((w_row // span) % N_Y) * (span * N_NEAR) + (w_row // (span * N_Y)) * span + w_row % span
    order[...] = jnp.where((w_col == w_from) & (w_row < channels), 1.0, 0.0).astype(B16)
    p_row = lax.broadcasted_iota(jnp.int32, (4 * span, 64), 0)
    p_col = lax.broadcasted_iota(jnp.int32, (4 * span, 64), 1)
    close = jnp.where(p_col == (p_row // span) * 16 + p_row % span, 1.0, 0.0).astype(B16)
    gap_row = lax.broadcasted_iota(jnp.int32, (64, 4 * span), 0)
    gap_col = lax.broadcasted_iota(jnp.int32, (64, 4 * span), 1)
    reopen = jnp.where(gap_row == (gap_col // span) * 16 + gap_col % span, 1.0, 0.0).astype(B16)

    def two_copies():
        made = []
        for k in range(3):
            place = wtwo_a.at[core, y]
            made.append(copy(place, place, wtwo_s.at[0, k], wtwo_r.at[0, k], at_y(k + 1)))
            place = wtwo_b.at[core, near]
            made.append(copy(place, place, wtwo_s.at[1, k], wtwo_r.at[1, k], at_z(near_steps[k])))
        return made

    def share_a(k):
        place = wtwo_a.at[core, (y + N_Y - k) % N_Y]
        return copy(place, place, wsh_s.at[0, k], wsh_r.at[0, k], sibling)

    def share_b(k):
        step = 0 if k == 0 else near_steps[k - 1]
        place = wtwo_b.at[core, (near - step + N_NEAR) % N_NEAR]
        return copy(place, place, wsh_s.at[1, k], wsh_r.at[1, k], sibling)

    for c in one_copies():
        c.wait_recv()
    for f in range(2):
        rows_a = jnp.concatenate([wone_a[nn, f] for nn in range(N_NEAR)], axis=0)
        wtwo_a[core, y, f] = dot(close, rows_a).astype(B16)
        rows_b = jnp.concatenate([wone_b[yy, f] for yy in range(N_Y)], axis=0)
        wtwo_b[core, near, f] = dot(close, rows_b).astype(B16)
    for c in two_copies():
        c.start()
    share_a(0).start()
    share_b(0).start()

    forward(cv_first, cv_next)
    forward(high_first, high_next)
    for c in gm_next[0] + gm_next[1]:
        c.wait_recv()
    for b in range(N_X):
        gap = jnp.zeros((cells, 256 - channels), B16)
        nrm[:, b * 256 + channels : (b + 1) * 256] = gap
        gmx[:, b * 256 + channels : (b + 1) * 256] = gap
        gmx[:, b * 256 : b * 256 + low] = gma[b]
        packed = gmb[b]
        gmx[:HALF_ROWS, b * 256 + low : b * 256 + channels] = packed[:, :high]
        gmx[HALF_ROWS:, b * 256 + low : b * 256 + channels] = packed[:, high:]

    for c in gain_copies + cv_next + high_next:
        c.wait_recv()

    wide = float(channels * N_X)
    for half in range(2):

        def norm_rows(i, carry, half=half):
            part = pl.ds(pl.multiple_of(i * 64, 64), 64)
            here = pl.ds(pl.multiple_of(half * HALF_ROWS + i * 64, 64), 64)
            lows = [cva[b, here].astype(F32) for b in range(N_X)]
            highs = [cvb[b, part, half * high : (half + 1) * high].astype(F32) for b in range(N_X)]
            total = jnp.sum(sum(lows), axis=1, keepdims=True) + jnp.sum(sum(highs), axis=1, keepdims=True)
            square = jnp.sum(sum(v * v for v in lows), axis=1, keepdims=True) + jnp.sum(
                sum(v * v for v in highs), axis=1, keepdims=True
            )
            mean = total / wide
            scale = lax.rsqrt(square / wide - mean * mean + 1e-06)
            inv[here] = jnp.broadcast_to(scale, (64, 128))
            for b in range(N_X):
                centered = (lows[b] - mean) * scale
                cen[b, here, 0:low] = centered
                nrm[here, b * 256 : b * 256 + low] = (centered * gains[b, 0:1, 0:low]).astype(B16)
                centered = (highs[b] - mean) * scale
                cen[b, here, low:channels] = centered
                nrm[here, b * 256 + low : b * 256 + channels] = (
                    centered * gains[b, 0:1, low:channels]
                ).astype(B16)
            return carry

        lax.fori_loop(0, 4, norm_rows, 0)
        if half == 0:
            arrived = two_copies()
            for k in range(1, 4):
                arrived[2 * k - 2].wait_recv()
                share_a(k).start()
                arrived[2 * k - 1].wait_recv()
                share_b(k).start()

    for k in range(4):
        share_a(k).wait_recv()
        share_b(k).wait_recv()
    for m in range(2):
        for f in range(2):
            rows_a = jnp.concatenate([wtwo_a[m, yy, f] for yy in range(N_Y)], axis=0)
            dense[m, f * 256 : (f + 1) * 256] = dot(order[...], rows_a).astype(B16)
            for nn in range(N_NEAR):
                r = (f + 2) * 256 + nn * 4 * span
                dense[m, r : r + 4 * span] = wtwo_b[m, nn, f]
            dense[m, (f + 2) * 256 + channels : (f + 3) * 256] = jnp.zeros((256 - channels, width), B16)

    sum_copies = []
    for half in range(2):
        for i in range(2):
            start = half * HALF_ROWS + i * 128
            here = slice(start, start + 128)
            part = slice(half * 128, half * 128 + 128)
            pre = dot(nrm[here], dense[0])
            edge = 0.5 * (1.0 + lax.erf(pre * root_half))
            hid[here] = (pre * edge).astype(B16)
            slope = edge + pre * jnp.exp(-0.5 * pre * pre) * root_tau
            grad_pre = (dot(gmx[here], dense[1]) * slope).astype(B16)
            gpre[here] = grad_pre
            back = dot_nt(grad_pre, dense[0]).astype(B16)
            first_sum = jnp.zeros((128, 128), F32)
            second_sum = jnp.zeros((128, 128), F32)
            first_high = jnp.zeros((128, high), F32)
            second_high = jnp.zeros((128, high), F32)
            for b in range(N_X):
                low_part = back[:, b * 256 : b * 256 + low]
                high_part = back[:, b * 256 + low : b * 256 + channels]
                pga[b, here] = low_part
                pgb[b, part, i * high : (i + 1) * high] = high_part
                g = low_part.astype(F32) * gains[b, 0:1, 0:low]
                first_sum += g
                second_sum += g * cen[b, here, 0:low]
                g = high_part.astype(F32) * gains[b, 0:1, low:channels]
                first_high += g
                second_high += g * cen[b, here, low:channels]
            one = jnp.sum(first_sum, axis=1, keepdims=True) + jnp.sum(first_high, axis=1, keepdims=True)
            two = jnp.sum(second_sum, axis=1, keepdims=True) + jnp.sum(second_high, axis=1, keepdims=True)
            lane = lax.broadcasted_iota(jnp.int32, (128, 128), 1)
            columns = jnp.where(lane == 0, one, jnp.where(lane == 1, two, 0.0))
            sums[half, i] = jnp.transpose(columns)[0:8]
        made = []
        for k in range(1, N_X):
            other = (x + k) % N_X
            made.append(
                copy(sums.at[half], sums_in.at[k - 1, half], sum_s.at[half, k - 1], sum_r.at[half, k - 1], me, other)
            )
        for p in range(2):
            pg_made[half][p][0].start()
        for p in range(2):
            pg_made[half][p][1].start()
        for c in made:
            c.start()
        sum_copies.append(made)
    relay_on((pga, pgb), (pgre_a, pgre_b), pg_made[0], 0)

    for b in range(N_X):
        for m, inner, outer in ((0, nrm, gpre), (1, gmx, hid)):
            local = dot_tn(inner[:, b * 256 : (b + 1) * 256], outer[...]).astype(B16)
            if b < 2:
                local = dot_tn(order[...], local).astype(B16)
            for q in range(4):
                r = q * 4 * span
                if b < 2:
                    st_a[m, q, b] = local[r : r + 4 * span]
                else:
                    st_b[m, q, b - 2] = local[r : r + 4 * span]

    back_steps = (-1, 1, 2)

    def one_place(k):
        step = 0 if k == 0 else back_steps[k - 1]
        return (y + k) % N_Y, (near + step + N_NEAR) % N_NEAR

    def gsib_copies(k):
        yy, nn = one_place(k)
        return (
            copy(st_a.at[1 - core, yy], st_in_a.at[yy], gsib_s.at[0, k], gsib_r.at[0, k], sibling),
            copy(st_b.at[1 - core, nn], st_in_b.at[nn], gsib_s.at[1, k], gsib_r.at[1, k], sibling),
        )

    for k in (1, 2, 3, 0):
        for c in gsib_copies(k):
            c.start()

    relay_on((pga, pgb), (pgre_a, pgre_b), pg_made[1], 1)

    def gone_copies(k):
        return (
            copy(one_a.at[k], one_in_a.at[k - 1], gone_s.at[0, k - 1], gone_r.at[0, k - 1], at_y(k)),
            copy(
                one_b.at[k], one_in_b.at[k - 1], gone_s.at[1, k - 1], gone_r.at[1, k - 1], at_z(back_steps[k - 1])
            ),
        )

    for k in (1, 2, 3, 0):
        yy, nn = one_place(k)
        over_y, over_z = gsib_copies(k)
        over_y.wait_recv()
        one_a[k] = (st_a[core, yy].astype(F32) + st_in_a[yy].astype(F32)).astype(B16)
        if k > 0:
            to_y, to_z = gone_copies(k)
            to_y.start()
        over_z.wait_recv()
        one_b[k] = (st_b[core, nn].astype(F32) + st_in_b[nn].astype(F32)).astype(B16)
        if k > 0:
            to_z.start()

    for half in range(2):
        for i in range(2):
            start = half * HALF_ROWS + i * 128
            mixed = dot_nt(hid[start : start + 128], dense[1]).astype(B16)
            for b in range(N_X):
                mxa[b, start : start + 128] = mixed[:, b * 256 : b * 256 + low]
                mxb[b, half * 128 : half * 128 + 128, i * high : (i + 1) * high] = mixed[
                    :, b * 256 + low : b * 256 + channels
                ]
        for p in range(2):
            mx_made[half][p][0].start()
            mx_made[half][p][1].start()

    gcv[...] = jnp.zeros_like(gcv)
    for half in range(2):
        for c in sum_copies[half]:
            c.wait_recv()
        for p in range(2):
            pg_made[half][p][1].wait_recv()
            pg_made[half][p][2].wait_recv()
        for i in range(2):
            total = sums[half, i]
            for k in range(N_X - 1):
                total = total + sums_in[k, half, i]
            spread = jnp.concatenate([total / wide, jnp.zeros((120, 128), F32)], axis=0)
            sum_cols[...] = jnp.transpose(spread)
            lanes = slice(i * high, (i + 1) * high)

            def back_rows(n, carry, half=half, i=i, lanes=lanes):
                column = half * 4 + i * 2 + n
                part = pl.ds(pl.multiple_of(half * 128 + n * 64, 64), 64)
                here = pl.ds(pl.multiple_of(column * 64, 64), 64)
                low_part = pga[x, here].astype(F32)
                high_part = pgb[x, part, lanes].astype(F32)
                for k in range(2):
                    low_part = low_part + pgin_a[k, here].astype(F32)
                    high_part = high_part + pgin_b[k, part, lanes].astype(F32)
                local = pl.ds(pl.multiple_of(n * 64, 64), 64)
                e1 = sum_cols[local, 0:1]
                e2 = sum_cols[local, 1:2]
                scale = inv[here]
                g = low_part * gains[x, 0:1, 0:low]
                g = scale * (g - e1 - cen[x, here, 0:low] * e2)
                gcv[column, :, :, 0:low] = g.astype(B16).astype(F32).reshape(SIDE, TILE, low)
                g = high_part * gains[x, 0:1, low:channels]
                g = scale[:, :high] * (g - e1 - cen[x, here, low:channels] * e2)
                gcv[column, :, :, low:channels] = g.astype(B16).astype(F32).reshape(SIDE, TILE, high)
                return carry

            lax.fori_loop(0, 2, back_rows, 0)

    def spread_column(j, start, size):
        def add_tap(b, totals):
            totals = list(totals)
            source = gcv[j - b, :, :, start : start + size]
            for a in range(TAPS):
                tap = taps[b, a, :, start : start + size]
                for i in range(SIDE):
                    totals[i + a] = totals[i + a] + source[i] * tap
            return tuple(totals)

        empty = tuple(jnp.zeros((TILE, size), F32) for _ in range(SIDE + 6))
        first_tap = jnp.maximum(0, j - (SIDE - 1))
        end_tap = jnp.minimum(TAPS, j + 1)
        totals = lax.fori_loop(first_tap, end_tap, add_tap, empty)
        for i in range(SIDE + 6):
            gpad[j, i, :, start : start + size] = totals[i]

    def spread_edge(j, carry):
        for k in (j, j + 11):
            spread_column(k, 0, low)
            spread_column(k, low, high)
        return carry

    def spread_inner(j, carry):
        spread_column(j, 0, low)
        spread_column(j, low, high)
        return carry

    for half in range(2):
        relay_on((mxa, mxb), (mxre_a, mxre_b), mx_made[half], half)
    lax.fori_loop(0, 3, spread_edge, 0)
    for layer in range(3):
        part = pl.ds(layer * 64, 64)
        for face, column, held in ((2, layer, ret_w), (3, 11 + layer, ret_e)):
            edge = gpad[column, 3 : 3 + SIDE].reshape(64, channels).astype(B16)
            held[part] = dot(picks[face * 3 + layer], edge).astype(B16)
    ret_west = copy(ret_w, ret_w_in, ret_s.at[0], ret_r.at[0], west)
    ret_east = copy(ret_e, ret_e_in, ret_s.at[1], ret_r.at[1], east)
    ret_west.start()
    ret_east.start()

    def gtwo_copies(k):
        yy, nn = one_place(k)
        return (
            copy(two_a.at[nn], two_in_a.at[k - 1], gtwo_s.at[0, k - 1], gtwo_r.at[0, k - 1], at_z(back_steps[k - 1])),
            copy(two_b.at[yy], two_in_b.at[k - 1], gtwo_s.at[1, k - 1], gtwo_r.at[1, k - 1], at_y(k)),
        )

    for k in range(1, 4):
        for c in gone_copies(k):
            c.wait_recv()
    for f in range(2):
        for mine, came, units in ((one_a, one_in_a, two_a), (one_b, one_in_b, two_b)):
            total = mine[0, f].astype(F32)
            for k in range(3):
                total = total + came[k, f].astype(F32)
            opened = dot(reopen, total.astype(B16)).astype(B16)
            for q in range(4):
                units[q, f] = opened[q * 16 : (q + 1) * 16]
    for k in range(1, 4):
        for c in gtwo_copies(k):
            c.start()

    lax.fori_loop(3, 11, spread_inner, 0)

    for k in range(1, 4):
        for c in gtwo_copies(k):
            c.wait_recv()
    total = two_a[near].astype(F32)
    other_total = two_b[y].astype(F32)
    for k in range(3):
        total = total + two_in_a[k].astype(F32)
        other_total = other_total + two_in_b[k].astype(F32)
    fsum[0:2] = total
    fsum[2:4] = other_total

    def gfar_copy(k):
        return copy(
            fsum.at[(far + k) % N_FAR], f_in.at[k - 1], gfar_s.at[k - 1], gfar_r.at[k - 1], at_z(4 * k)
        )

    for k in range(1, N_FAR):
        gfar_copy(k).start()

    tg[...] = go[...].astype(F32).reshape(SIDE, SIDE, TILE, channels) + gpad[3 : 3 + SIDE, 3 : 3 + SIDE]
    for layer in range(3):
        for face, row, target in ((0, layer, 5 + layer), (1, 11 + layer, layer)):
            edge = gpad[3 : 3 + SIDE, row].reshape(64, channels).astype(B16)
            back = dot(picks[face * 3 + layer], edge)
            tg[:, target] = tg[:, target] + back.reshape(SIDE, TILE, channels)

    for half in range(2):
        for p in range(2):
            mx_made[half][p][1].wait_recv()
            mx_made[half][p][2].wait_recv()
    low_part = mxa[x].astype(F32)
    packed = mxb[x].astype(F32)
    for k in range(2):
        low_part = low_part + mxin_a[k].astype(F32)
        packed = packed + mxin_b[k].astype(F32)
    tops, ends = packed[:128], packed[128:]
    high_part = jnp.concatenate([tops[:, :high], tops[:, high:], ends[:, :high], ends[:, high:]], axis=0)
    mixed = jnp.concatenate([low_part, high_part], axis=1)
    out = (xt[...].astype(F32) + scale_row * mixed).astype(B16)
    block_ref[...] = dot_tn(out, perm[...]).astype(B16)

    for k in range(1, N_FAR):
        gfar_copy(k).wait_recv()
    total = fsum[far]
    for k in range(1, N_FAR):
        total = total + f_in[k - 1]
    last[0, 0:8] = total[0:8]
    last[1, 0:8] = total[rows : rows + 8]
    gend = copy(last.at[1 - core], last_in.at[core], gend_s, gend_r, sibling)
    gend.start()
    last_in[core] = last[core]

    ret_west.wait_recv()
    ret_east.wait_recv()
    for layer in range(3):
        part = pl.ds(layer * 64, 64)
        tg[5 + layer] = tg[5 + layer] + ret_w_in[part].astype(F32).reshape(SIDE, TILE, channels)
        tg[layer] = tg[layer] + ret_e_in[part].astype(F32).reshape(SIDE, TILE, channels)
    grad_ref[...] = dot_tn(tg[...].reshape(cells, channels).astype(B16), perm[...]).astype(B16)

    gend.wait_recv()
    up_grad_ref[...] = last_in[0, 0:rows]
    down_grad_ref[...] = last_in[1, 0:rows]

    sent = [halo_west, halo_east, wsib, ret_west, ret_east, gend]
    sent += gain_copies + gm_first[0] + gm_first[1] + gm_next[0] + gm_next[1]
    sent += cv_first + cv_next + high_first + high_next + sum_copies[0] + sum_copies[1]
    for made in pg_made + mx_made:
        sent += made[0] + made[1]
    sent += [far_copy(k) for k in range(1, N_FAR)] + one_copies() + two_copies()
    sent += [share_a(k) for k in range(4)] + [share_b(k) for k in range(4)]
    for k in range(4):
        sent += gsib_copies(k)
    for k in range(1, 4):
        sent += gone_copies(k) + gtwo_copies(k)
    sent += [gfar_copy(k) for k in range(1, N_FAR)]
    for c in sent:
        c.wait_send()


def hand_over(*refs):
    for i in range(4):
        refs[4 + i][...] = refs[i][...]


def per_device(
    tiles, kernel, norm_gain, w_up, w_down, layer_scale, neighbors, shifts, halo_widths, land, cotangent
):
    channels, cells = tiles.shape
    rows, width = w_up.shape
    vmem = pl.BlockSpec(memory_space=pltpu.VMEM)
    dma = pltpu.SemaphoreType.DMA

    def v(dtype, *shape):
        return pltpu.VMEM(shape, dtype)

    strip = (2, 8 * rows, width)
    units = (2, 16, width)
    scratch = [
        v(B16, cells, cells), v(B16, 256, channels), v(B16, 12, 64, 64), v(F32, TAPS, TAPS, 8, channels),
        v(B16, cells, channels), v(B16, cells, channels), v(B16, 192, channels), v(B16, 192, channels),
        v(F32, SIDE + 6, SIDE + 6, TILE, channels), v(F32, N_X, 8, channels),
        v(B16, N_X, cells, 128), v(B16, N_X, HALF_ROWS, 128), v(B16, N_X, cells, 128), v(B16, N_X, HALF_ROWS, 128),
        v(F32, N_X, cells, channels), v(F32, cells, 128), v(B16, cells, N_X * 256), v(B16, cells, N_X * 256),
        v(B16, cells, width), v(B16, cells, width),
        v(B16, N_X, cells, 128), v(B16, N_X, HALF_ROWS, 128), v(B16, 2, cells, 128), v(B16, 2, HALF_ROWS, 128),
        v(B16, 2, HALF_ROWS, 128), v(B16, 2, 128, 128),
        v(B16, N_X, cells, 128), v(B16, N_X, HALF_ROWS, 128), v(B16, 2, cells, 128), v(B16, 2, HALF_ROWS, 128),
        v(B16, 2, HALF_ROWS, 128), v(B16, 2, 128, 128),
        v(F32, 2, 2, 8, 128), v(F32, 3, 2, 2, 8, 128), v(F32, 128, 128),
        v(F32, SIDE, SIDE, TILE, channels), v(F32, SIDE + 6, SIDE + 6, TILE, channels),
        v(B16, 192, channels), v(B16, 192, channels), v(B16, 192, channels), v(B16, 192, channels),
        v(F32, SIDE, SIDE, TILE, channels),
        v(B16, 2, 16, width), v(B16, N_FAR, 16, width), v(B16, 4, *units), v(B16, 4, *units),
        v(B16, 2, 4, *strip), v(B16, 2, 4, *strip), v(B16, 2, N_X * 256, width),
        v(B16, 2, 4, *strip), v(B16, 2, 4, *strip), v(B16, 4, *strip), v(B16, 4, *strip),
        v(B16, 4, *strip), v(B16, 4, *strip), v(B16, 3, *strip), v(B16, 3, *strip),
        v(B16, 4, *units), v(B16, 4, *units), v(B16, 3, *units), v(B16, 3, *units),
        v(F32, N_FAR, 16, width), v(F32, 3, 16, width), v(F32, 2, 8, width), v(F32, 2, 8, width),
    ]
    scratch += [v(B16, channels, cells), v(B16, channels, cells), dma((2,))]
    pairs = [(2,), (3,), (2, 4), (2, 4), (2, 3, 2), (2, 3, 2), (2, 3), (2,), None, (3,), (2, 3), (2, 3), (2, 4)]
    pairs += [(2, 4), (2, 3), (2, 3), (3,), None]
    for p in pairs:
        scratch += [dma if p is None else dma(p)] * 2
    shapes = [
        jax.ShapeDtypeStruct((channels, cells), B16),
        jax.ShapeDtypeStruct((channels, cells), B16),
        jax.ShapeDtypeStruct((rows, width), F32),
        jax.ShapeDtypeStruct((rows, width), F32),
    ]
    made = pl.pallas_call(
        functools.partial(block_kernel, rows, width),
        out_shape=shapes,
        in_specs=[pl.BlockSpec(memory_space=pl.ANY)] * 2 + [vmem] * 9,
        out_specs=[vmem] * 4,
        scratch_shapes=scratch,
        compiler_params=pltpu.CompilerParams(
            collective_id=0, has_side_effects=True, vmem_limit_bytes=56 * 1024 * 1024
        ),
    )(
        tiles, cotangent, land, kernel, norm_gain, layer_scale,
        jnp.transpose(neighbors, (1, 2, 0)), jnp.transpose(shifts, (1, 2, 0)), halo_widths.T, w_up, w_down,
    )
    return pl.pallas_call(
        hand_over,
        out_shape=shapes,
        in_specs=[vmem] * 4,
        out_specs=[vmem] * 4,
    )(*made)


def solution(mesh):
    return jax.shard_map(
        per_device,
        mesh=mesh,
        in_specs=(
            P("fsdp", "dp"),
            P(None, "fsdp"),
            P("fsdp"),
            P("dp", "fsdp"),
            P("dp", "fsdp"),
            P("fsdp"),
            P("dp", None, None),
            P("dp", None, None),
            P("dp", None),
            P("dp", None, None),
            P("fsdp", "dp"),
        ),
        out_specs=(P("fsdp", "dp"), P("fsdp", "dp"), P("dp", "fsdp"), P("dp", "fsdp")),
        check_vma=False,
    )
```

```python
import functools
import math

import jax
import jax.numpy as jnp
from jax import lax
from jax.experimental import pallas as pl
from jax.experimental.pallas import tpu as pltpu
from jax.sharding import PartitionSpec as P

root_half = 1.0 / math.sqrt(2.0)
root_tau = 1.0 / math.sqrt(2.0 * math.pi)

N_Z, N_Y, N_CORE, N_X = 16, 4, 2, 4
N_FAR, N_NEAR = 4, 4
N_DP = N_Z * N_Y * N_CORE
MESH = pl.DeviceIdType.MESH
F32, B16 = jnp.float32, jnp.bfloat16
SIDE, TILE, TAPS = 8, 8, 7
HALF_ROWS = 256


def dp_index(z, y, core):
    return (z * N_Y + y) * N_CORE + core


def dot(a, b):
    return jnp.dot(a, b, preferred_element_type=F32)


def dot_nt(a, b):
    return lax.dot_general(a, b, (((1,), (1,)), ((), ())), preferred_element_type=F32)


def dot_tn(a, b):
    return lax.dot_general(a, b, (((0,), (0,)), ((), ())), preferred_element_type=F32)


def block_kernel(
    rows, width,
    x_ref, cot_ref, land_ref, taps_ref, gain_ref, scale_ref, owner_ref, shift_ref, depth_ref, up_ref, down_ref,
    block_ref, grad_ref, up_grad_ref, down_grad_ref,
    perm, order, picks, taps, xt, go, east_in, west_in, pad, gains,
    gma, gmb, cva, cvb, cen, inv, nrm, gmx, hid, gpre,
    pga, pgb, pgin_a, pgin_b, pgre_a, pgre_b, mxa, mxb, mxin_a, mxin_b, mxre_a, mxre_b, sums, sums_in, sum_cols,
    gcv, gpad, ret_w, ret_e, ret_w_in, ret_e_in, tg,
    unit_in, wfar, wone_a, wone_b, wtwo_a, wtwo_b, dense,
    st_a, st_b, st_in_a, st_in_b, one_a, one_b, one_in_a, one_in_b, two_a, two_b, two_in_a, two_in_b,
    fsum, f_in, last, last_in,
    x_in, cot_in, in_sem, halo_s, halo_r, gain_s, gain_r, gm_s, gm_r, cv_s, cv_r, pg_s, pg_r, mx_s, mx_r, sum_s, sum_r,
    ret_s, ret_r, wsib_s, wsib_r, wfar_s, wfar_r, wone_s, wone_r, wtwo_s, wtwo_r, wsh_s, wsh_r,
    gsib_s, gsib_r, gone_s, gone_r, gtwo_s, gtwo_r, gfar_s, gfar_r, gend_s, gend_r,
):
    channels = x_ref.shape[0]
    low, high = 128, channels - 128
    cells = x_ref.shape[1]
    me = lax.axis_index("dp")
    x = lax.axis_index("fsdp")
    z, y, core = me // (N_Y * N_CORE), (me // N_CORE) % N_Y, me % N_CORE
    far, near = z // N_NEAR, z % N_NEAR
    east, west = (me + 1) % N_DP, (me + N_DP - 1) % N_DP
    sibling = dp_index(z, y, 1 - core)

    def at_z(step):
        return dp_index((z + step + N_Z) % N_Z, y, core)

    def at_y(k):
        return dp_index(z, (y + k) % N_Y, core)

    def copy(src, dst, send, recv, dp, fs=None):
        return pltpu.make_async_remote_copy(
            src_ref=src, dst_ref=dst, send_sem=send, recv_sem=recv,
            device_id=(dp, x if fs is None else fs), device_id_type=MESH,
        )

    barrier = pltpu.get_barrier_semaphore()
    greeted = [(east, x), (west, x), (sibling, x)]
    greeted += [(me, (x + k) % N_X) for k in range(1, N_X)]
    greeted += [(at_z(s), x) for s in (4, 8, 12, 1, -1, 2, -2)]
    greeted += [(at_y(k), x) for k in range(1, N_Y)]
    for other in greeted:
        pl.semaphore_signal(barrier, inc=1, device_id=other, device_id_type=MESH)
    x_load = pltpu.make_async_copy(x_ref, x_in, in_sem.at[0])
    cot_load = pltpu.make_async_copy(cot_ref, cot_in, in_sem.at[1])
    x_load.start()
    cot_load.start()

    out_cell = lax.broadcasted_iota(jnp.int32, (cells, 128), 0)
    in_cell = lax.broadcasted_iota(jnp.int32, (cells, 128), 1)
    wanted = ((out_cell & 7) << 6) + (((out_cell >> 3) & 7) << 3) + (out_cell >> 6)
    for start in range(0, cells, 128):
        perm[:, start : start + 128] = jnp.where(in_cell + start == wanted, 1.0, 0.0).astype(B16)
    x_load.wait()
    xt[...] = dot_nt(perm[...], x_in[...]).astype(B16)
    cot_load.wait()
    j_row = lax.broadcasted_iota(jnp.int32, (SIDE, cells), 0)
    j_col = lax.broadcasted_iota(jnp.int32, (SIDE, cells), 1)
    spread_j = jnp.where(j_row == (j_col & 7), 1.0, 0.0).astype(B16)
    land = land_ref[...].astype(F32).reshape(TILE * SIDE, SIDE).astype(B16)
    ti_row = lax.broadcasted_iota(jnp.int32, (TILE * SIDE, cells), 0)
    ti_col = lax.broadcasted_iota(jnp.int32, (TILE * SIDE, cells), 1)
    land_row = jnp.sum(
        jnp.where(ti_row == (ti_col >> 3), dot(land, spread_j), 0.0), axis=0, keepdims=True
    ).astype(B16)
    go[...] = dot_nt(perm[...], cot_in[...] * land_row).astype(B16)
    scale_row = scale_ref[...].astype(F32).reshape(1, channels)
    grad_mixed = (go[...].astype(F32) * scale_row).astype(B16)
    gma[x] = grad_mixed[:, :low]
    gmb[x] = jnp.concatenate([grad_mixed[:HALF_ROWS, low:], grad_mixed[HALF_ROWS:, low:]], axis=1)
    gains[x] = jnp.broadcast_to(gain_ref[...].astype(F32).reshape(1, channels), (8, channels))
    s_row = lax.broadcasted_iota(jnp.int32, (16, rows), 0)
    s_col = lax.broadcasted_iota(jnp.int32, (16, rows), 1)
    unit_in[core] = (
        dot(jnp.where(s_row == s_col, 1.0, 0.0).astype(B16), up_ref[...])
        + dot(jnp.where(s_row == s_col + 8, 1.0, 0.0).astype(B16), down_ref[...])
    ).astype(B16)

    pl.semaphore_wait(barrier, len(greeted))

    halo_west = copy(xt.at[pl.ds(0, 192)], east_in, halo_s.at[0], halo_r.at[0], west)
    halo_east = copy(xt.at[pl.ds(cells - 192, 192)], west_in, halo_s.at[1], halo_r.at[1], east)
    halo_west.start()
    halo_east.start()
    wsib = copy(unit_in.at[core], unit_in.at[core], wsib_s, wsib_r, sibling)
    wsib.start()

    right, left, across = (x + 1) % N_X, (x + N_X - 1) % N_X, (x + 2) % N_X

    def gather_first(buffer, send, recv):
        return [
            copy(buffer.at[x], buffer.at[x], send.at[0], recv.at[0], me, right),
            copy(buffer.at[x], buffer.at[x], send.at[1], recv.at[1], me, left),
        ]

    def gather_next(buffer, send, recv):
        count = buffer.shape[1] // 2
        head, tail = pl.ds(0, count), pl.ds(count, count)
        return [
            copy(buffer.at[left, head], buffer.at[left, head], send.at[2], recv.at[2], me, right),
            copy(buffer.at[right, tail], buffer.at[right, tail], send.at[3], recv.at[3], me, left),
        ]

    def forward(first, later):
        for c, n in zip(first, later):
            c.wait_recv()
            n.start()

    gain_copies = []
    for k in range(1, N_X):
        gain_copies.append(
            copy(gains.at[x], gains.at[x], gain_s.at[k - 1], gain_r.at[k - 1], me, (x + k) % N_X)
        )
    gm_first = gather_first(gma, gm_s.at[0], gm_r.at[0]), gather_first(gmb, gm_s.at[1], gm_r.at[1])
    gm_next = gather_next(gma, gm_s.at[0], gm_r.at[0]), gather_next(gmb, gm_s.at[1], gm_r.at[1])
    for c in gm_first[0] + gm_first[1] + gain_copies:
        c.start()

    def scatter_copies(held, came, relay, send, recv, half):
        toward, away = (right, left) if half == 0 else (left, right)
        made = []
        for p in range(2):
            count = held[p].shape[1] // 2
            part = pl.ds(half * count, count)
            made.append((
                copy(held[p].at[across, part], relay[p].at[half], send.at[half, 0, p], recv.at[half, 0, p], me, toward),
                copy(
                    held[p].at[away, part], came[p].at[1 - half, part], send.at[half, 1, p], recv.at[half, 1, p], me, away
                ),
                copy(
                    held[p].at[toward, part], came[p].at[half, part], send.at[half, 2, p], recv.at[half, 2, p], me, toward
                ),
            ))
        return made

    def relay_on(held, relay, made, half):
        toward = right if half == 0 else left
        for p in range(2):
            count = held[p].shape[1] // 2
            part = pl.ds(half * count, count)
            made[p][0].wait_recv()
            held[p][toward, part] = (held[p][toward, part].astype(F32) + relay[p][half].astype(F32)).astype(B16)
            made[p][2].start()

    pg_made = [scatter_copies((pga, pgb), (pgin_a, pgin_b), (pgre_a, pgre_b), pg_s, pg_r, h) for h in range(2)]
    mx_made = [scatter_copies((mxa, mxb), (mxin_a, mxin_b), (mxre_a, mxre_b), mx_s, mx_r, h) for h in range(2)]

    edge_row = lax.broadcasted_iota(jnp.int32, (64, 64), 0)
    for face in range(4):
        chosen = jnp.zeros((64, 64), F32)
        for entry in range(2):
            owner = owner_ref[face, entry : entry + 1, :]
            shift = shift_ref[face, entry : entry + 1, :]
            target = jnp.where(owner >= 0, (owner & 7) + TILE * shift, -4096)
            target = jnp.concatenate([target + TILE * p for p in range(SIDE)], axis=1)
            chosen = chosen + jnp.where(target == edge_row, 1.0, 0.0)
        widths = jnp.concatenate([depth_ref[face : face + 1, :]] * SIDE, axis=1)
        for layer in range(3):
            depth = 3 - layer if face in (0, 2) else layer + 1
            picks[face * 3 + layer] = jnp.where(widths >= depth, chosen, 0.0).astype(B16)

    span = N_CORE * rows
    w_row = lax.broadcasted_iota(jnp.int32, (256, channels), 0)
    w_col = lax.broadcasted_iota(jnp.int32, (256, channels), 1)
    w_strip = (w_row * 171) >> 11
    w_from = (w_strip & 3) * (span * N_NEAR) + (w_strip >> 2) * span + (w_row - w_strip * span)
    order[...] = jnp.where((w_col == w_from) & (w_row < channels), 1.0, 0.0).astype(B16)
    p_row = lax.broadcasted_iota(jnp.int32, (4 * span, 64), 0)
    p_col = lax.broadcasted_iota(jnp.int32, (4 * span, 64), 1)
    close = jnp.where(p_col == p_row + 4 * ((p_row * 171) >> 11), 1.0, 0.0).astype(B16)
    gap_row = lax.broadcasted_iota(jnp.int32, (64, 4 * span), 0)
    gap_col = lax.broadcasted_iota(jnp.int32, (64, 4 * span), 1)
    reopen = jnp.where(gap_row == gap_col + 4 * ((gap_col * 171) >> 11), 1.0, 0.0).astype(B16)

    kernel_taps = taps_ref[...].astype(F32)
    for a in range(TAPS):
        for b in range(TAPS):
            k = a * TAPS + b
            taps[b, a] = jnp.broadcast_to(kernel_taps[k : k + 1], (8, channels))

    pad[...] = jnp.zeros_like(pad)
    cells_f = xt[...].astype(F32).reshape(SIDE, SIDE, TILE, channels)
    pad[3 : 3 + SIDE, 3 : 3 + SIDE] = cells_f
    for layer in range(3):
        north = cells_f[:, 5 + layer].reshape(64, channels).astype(B16)
        south = cells_f[:, layer].reshape(64, channels).astype(B16)
        pad[3 : 3 + SIDE, layer] = dot_tn(picks[layer], north).astype(B16).astype(F32).reshape(SIDE, TILE, channels)
        pad[3 : 3 + SIDE, 11 + layer] = (
            dot_tn(picks[3 + layer], south).astype(B16).astype(F32).reshape(SIDE, TILE, channels)
        )

    wsib.wait_recv()
    both = unit_in[...].reshape(N_CORE * 16, width)
    u_row = lax.broadcasted_iota(jnp.int32, (16, N_CORE * 16), 0)
    u_col = lax.broadcasted_iota(jnp.int32, (16, N_CORE * 16), 1)
    first = (u_row < rows) & (u_col == u_row + 8 * core)
    second = (u_row >= rows) & (u_row < 2 * rows) & (u_col == 16 + u_row - rows + 8 * core)
    joined = dot(jnp.where(first | second, 1.0, 0.0).astype(B16), both).astype(B16)
    wfar[far] = joined

    def far_copy(k):
        place = wfar.at[far]
        return copy(place, place, wfar_s.at[k - 1], wfar_r.at[k - 1], at_z(4 * k))

    for k in range(1, N_FAR):
        far_copy(k).start()

    halo_west.wait_recv()
    halo_east.wait_recv()
    for layer in range(3):
        part = pl.ds(layer * 64, 64)
        pad[layer, 3 : 3 + SIDE] = (
            dot_tn(picks[6 + layer], west_in[part]).astype(B16).astype(F32).reshape(SIDE, TILE, channels)
        )
        pad[11 + layer, 3 : 3 + SIDE] = (
            dot_tn(picks[9 + layer], east_in[part]).astype(B16).astype(F32).reshape(SIDE, TILE, channels)
        )

    def conv_column(j, start, size):
        total = jnp.zeros((SIDE, TILE, size), F32)
        for b in range(TAPS):
            source = pad[j + b, :, :, start : start + size]
            for a in range(TAPS):
                total = total + source[a : a + SIDE] * taps[b, a, :, start : start + size][None]
        return total.reshape(64, size).astype(B16)

    def conv_low(j, carry):
        cva[x, pl.ds(pl.multiple_of(j * 64, 64), 64)] = conv_column(j, 0, low)
        return carry

    def conv_high(j, carry):
        cvb[x, pl.ds(pl.multiple_of(j * 64, 64), 64)] = jnp.concatenate(
            [conv_column(j, low, high), conv_column(j + 4, low, high)], axis=1
        )
        return carry

    lax.fori_loop(0, SIDE, conv_low, 0)
    cv_first = gather_first(cva, cv_s.at[0], cv_r.at[0])
    cv_next = gather_next(cva, cv_s.at[0], cv_r.at[0])
    for c in cv_first:
        c.start()

    for k in range(1, N_FAR):
        far_copy(k).wait_recv()

    near_steps = (1, -1, -2)

    def one_copies():
        made = []
        for k in range(3):
            made.append(
                copy(wone_a.at[near], wone_a.at[near], wone_s.at[0, k], wone_r.at[0, k], at_z(near_steps[k]))
            )
            made.append(copy(wone_b.at[y], wone_b.at[y], wone_s.at[1, k], wone_r.at[1, k], at_y(k + 1)))
        return made

    wone_a[near] = wfar[0:2]
    wone_b[y] = wfar[2:4]
    for c in one_copies():
        c.start()

    lax.fori_loop(0, 4, conv_high, 0)
    high_first = gather_first(cvb, cv_s.at[1], cv_r.at[1])
    high_next = gather_next(cvb, cv_s.at[1], cv_r.at[1])
    for c in high_first:
        c.start()
    forward(gm_first[0], gm_next[0])
    forward(gm_first[1], gm_next[1])

    def two_copies():
        made = []
        for k in range(3):
            place = wtwo_a.at[core, y]
            made.append(copy(place, place, wtwo_s.at[0, k], wtwo_r.at[0, k], at_y(k + 1)))
            place = wtwo_b.at[core, near]
            made.append(copy(place, place, wtwo_s.at[1, k], wtwo_r.at[1, k], at_z(near_steps[k])))
        return made

    def share_a(k):
        place = wtwo_a.at[core, (y + N_Y - k) % N_Y]
        return copy(place, place, wsh_s.at[0, k], wsh_r.at[0, k], sibling)

    def share_b(k):
        step = 0 if k == 0 else near_steps[k - 1]
        place = wtwo_b.at[core, (near - step + N_NEAR) % N_NEAR]
        return copy(place, place, wsh_s.at[1, k], wsh_r.at[1, k], sibling)

    for c in one_copies():
        c.wait_recv()
    for f in range(2):
        rows_a = jnp.concatenate([wone_a[nn, f] for nn in range(N_NEAR)], axis=0)
        wtwo_a[core, y, f] = dot(close, rows_a).astype(B16)
        rows_b = jnp.concatenate([wone_b[yy, f] for yy in range(N_Y)], axis=0)
        wtwo_b[core, near, f] = dot(close, rows_b).astype(B16)
    for c in two_copies():
        c.start()
    share_a(0).start()
    share_b(0).start()

    forward(cv_first, cv_next)
    forward(high_first, high_next)
    for c in gm_next[0] + gm_next[1]:
        c.wait_recv()
    for b in range(N_X):
        gap = jnp.zeros((cells, 256 - channels), B16)
        nrm[:, b * 256 + channels : (b + 1) * 256] = gap
        gmx[:, b * 256 + channels : (b + 1) * 256] = gap
        gmx[:, b * 256 : b * 256 + low] = gma[b]
        packed = gmb[b]
        gmx[:HALF_ROWS, b * 256 + low : b * 256 + channels] = packed[:, :high]
        gmx[HALF_ROWS:, b * 256 + low : b * 256 + channels] = packed[:, high:]

    for c in gain_copies + cv_next + high_next:
        c.wait_recv()

    wide = float(channels * N_X)
    for half in range(2):

        def norm_rows(i, carry, half=half):
            part = pl.ds(pl.multiple_of(i * 64, 64), 64)
            here = pl.ds(pl.multiple_of(half * HALF_ROWS + i * 64, 64), 64)
            lows = [cva[b, here].astype(F32) for b in range(N_X)]
            highs = [cvb[b, part, half * high : (half + 1) * high].astype(F32) for b in range(N_X)]
            total = jnp.sum(sum(lows), axis=1, keepdims=True) + jnp.sum(sum(highs), axis=1, keepdims=True)
            square = jnp.sum(sum(v * v for v in lows), axis=1, keepdims=True) + jnp.sum(
                sum(v * v for v in highs), axis=1, keepdims=True
            )
            mean = total / wide
            scale = lax.rsqrt(square / wide - mean * mean + 1e-06)
            inv[here] = jnp.broadcast_to(scale, (64, 128))
            for b in range(N_X):
                centered = (lows[b] - mean) * scale
                cen[b, here, 0:low] = centered
                nrm[here, b * 256 : b * 256 + low] = (centered * gains[b, 0:1, 0:low]).astype(B16)
                centered = (highs[b] - mean) * scale
                cen[b, here, low:channels] = centered
                nrm[here, b * 256 + low : b * 256 + channels] = (
                    centered * gains[b, 0:1, low:channels]
                ).astype(B16)
            return carry

        lax.fori_loop(0, 4, norm_rows, 0)
        if half == 0:
            arrived = two_copies()
            for k in range(1, 4):
                arrived[2 * k - 2].wait_recv()
                share_a(k).start()
                arrived[2 * k - 1].wait_recv()
                share_b(k).start()

    for k in range(4):
        share_a(k).wait_recv()
        share_b(k).wait_recv()
    for m in range(2):
        for f in range(2):
            rows_a = jnp.concatenate([wtwo_a[m, yy, f] for yy in range(N_Y)], axis=0)
            dense[m, f * 256 : (f + 1) * 256] = dot(order[...], rows_a).astype(B16)
            for nn in range(N_NEAR):
                r = (f + 2) * 256 + nn * 4 * span
                dense[m, r : r + 4 * span] = wtwo_b[m, nn, f]
            dense[m, (f + 2) * 256 + channels : (f + 3) * 256] = jnp.zeros((256 - channels, width), B16)

    sum_copies = []
    for half in range(2):
        for i in range(2):
            start = half * HALF_ROWS + i * 128
            here = slice(start, start + 128)
            part = slice(half * 128, half * 128 + 128)
            pre = dot(nrm[here], dense[0])
            edge = 0.5 * (1.0 + lax.erf(pre * root_half))
            hid[here] = (pre * edge).astype(B16)
            slope = edge + pre * jnp.exp(-0.5 * pre * pre) * root_tau
            grad_pre = (dot(gmx[here], dense[1]) * slope).astype(B16)
            gpre[here] = grad_pre
            back = dot_nt(grad_pre, dense[0]).astype(B16)
            first_sum = jnp.zeros((128, 128), F32)
            second_sum = jnp.zeros((128, 128), F32)
            first_high = jnp.zeros((128, high), F32)
            second_high = jnp.zeros((128, high), F32)
            for b in range(N_X):
                low_part = back[:, b * 256 : b * 256 + low]
                high_part = back[:, b * 256 + low : b * 256 + channels]
                pga[b, here] = low_part
                pgb[b, part, i * high : (i + 1) * high] = high_part
                g = low_part.astype(F32) * gains[b, 0:1, 0:low]
                first_sum += g
                second_sum += g * cen[b, here, 0:low]
                g = high_part.astype(F32) * gains[b, 0:1, low:channels]
                first_high += g
                second_high += g * cen[b, here, low:channels]
            one = jnp.sum(first_sum, axis=1, keepdims=True) + jnp.sum(first_high, axis=1, keepdims=True)
            two = jnp.sum(second_sum, axis=1, keepdims=True) + jnp.sum(second_high, axis=1, keepdims=True)
            lane = lax.broadcasted_iota(jnp.int32, (128, 128), 1)
            columns = jnp.where(lane == 0, one, jnp.where(lane == 1, two, 0.0))
            sums[half, i] = jnp.transpose(columns)[0:8]
        made = []
        for k in range(1, N_X):
            other = (x + k) % N_X
            made.append(
                copy(sums.at[half], sums_in.at[k - 1, half], sum_s.at[half, k - 1], sum_r.at[half, k - 1], me, other)
            )
        for p in range(2):
            pg_made[half][p][0].start()
        for p in range(2):
            pg_made[half][p][1].start()
        for c in made:
            c.start()
        sum_copies.append(made)
    relay_on((pga, pgb), (pgre_a, pgre_b), pg_made[0], 0)

    for b in range(N_X):
        for m, inner, outer in ((0, nrm, gpre), (1, gmx, hid)):
            local = dot_tn(inner[:, b * 256 : (b + 1) * 256], outer[...]).astype(B16)
            if b < 2:
                local = dot_tn(order[...], local).astype(B16)
            for q in range(4):
                r = q * 4 * span
                if b < 2:
                    st_a[m, q, b] = local[r : r + 4 * span]
                else:
                    st_b[m, q, b - 2] = local[r : r + 4 * span]

    back_steps = (-1, 1, 2)

    def one_place(k):
        step = 0 if k == 0 else back_steps[k - 1]
        return (y + k) % N_Y, (near + step + N_NEAR) % N_NEAR

    def gsib_copies(k):
        yy, nn = one_place(k)
        return (
            copy(st_a.at[1 - core, yy], st_in_a.at[yy], gsib_s.at[0, k], gsib_r.at[0, k], sibling),
            copy(st_b.at[1 - core, nn], st_in_b.at[nn], gsib_s.at[1, k], gsib_r.at[1, k], sibling),
        )

    for k in (1, 2, 3, 0):
        for c in gsib_copies(k):
            c.start()

    relay_on((pga, pgb), (pgre_a, pgre_b), pg_made[1], 1)

    def gone_copies(k):
        return (
            copy(one_a.at[k], one_in_a.at[k - 1], gone_s.at[0, k - 1], gone_r.at[0, k - 1], at_y(k)),
            copy(
                one_b.at[k], one_in_b.at[k - 1], gone_s.at[1, k - 1], gone_r.at[1, k - 1], at_z(back_steps[k - 1])
            ),
        )

    for k in (1, 2, 3, 0):
        yy, nn = one_place(k)
        over_y, over_z = gsib_copies(k)
        over_y.wait_recv()
        one_a[k] = (st_a[core, yy].astype(F32) + st_in_a[yy].astype(F32)).astype(B16)
        if k > 0:
            to_y, to_z = gone_copies(k)
            to_y.start()
        over_z.wait_recv()
        one_b[k] = (st_b[core, nn].astype(F32) + st_in_b[nn].astype(F32)).astype(B16)
        if k > 0:
            to_z.start()

    for half in range(2):
        for i in range(2):
            start = half * HALF_ROWS + i * 128
            mixed = dot_nt(hid[start : start + 128], dense[1]).astype(B16)
            for b in range(N_X):
                mxa[b, start : start + 128] = mixed[:, b * 256 : b * 256 + low]
                mxb[b, half * 128 : half * 128 + 128, i * high : (i + 1) * high] = mixed[
                    :, b * 256 + low : b * 256 + channels
                ]
        for p in range(2):
            mx_made[half][p][0].start()
            mx_made[half][p][1].start()

    gcv[...] = jnp.zeros_like(gcv)
    for half in range(2):
        for c in sum_copies[half]:
            c.wait_recv()
        for p in range(2):
            pg_made[half][p][1].wait_recv()
            pg_made[half][p][2].wait_recv()
        for i in range(2):
            total = sums[half, i]
            for k in range(N_X - 1):
                total = total + sums_in[k, half, i]
            spread = jnp.concatenate([total / wide, jnp.zeros((120, 128), F32)], axis=0)
            sum_cols[...] = jnp.transpose(spread)
            lanes = slice(i * high, (i + 1) * high)

            def back_rows(n, carry, half=half, i=i, lanes=lanes):
                column = half * 4 + i * 2 + n
                part = pl.ds(pl.multiple_of(half * 128 + n * 64, 64), 64)
                here = pl.ds(pl.multiple_of(column * 64, 64), 64)
                low_part = pga[x, here].astype(F32)
                high_part = pgb[x, part, lanes].astype(F32)
                for k in range(2):
                    low_part = low_part + pgin_a[k, here].astype(F32)
                    high_part = high_part + pgin_b[k, part, lanes].astype(F32)
                local = pl.ds(pl.multiple_of(n * 64, 64), 64)
                e1 = sum_cols[local, 0:1]
                e2 = sum_cols[local, 1:2]
                scale = inv[here]
                g = low_part * gains[x, 0:1, 0:low]
                g = scale * (g - e1 - cen[x, here, 0:low] * e2)
                gcv[column, :, :, 0:low] = g.astype(B16).astype(F32).reshape(SIDE, TILE, low)
                g = high_part * gains[x, 0:1, low:channels]
                g = scale[:, :high] * (g - e1 - cen[x, here, low:channels] * e2)
                gcv[column, :, :, low:channels] = g.astype(B16).astype(F32).reshape(SIDE, TILE, high)
                return carry

            lax.fori_loop(0, 2, back_rows, 0)

    def spread_column(j, start, size):
        def add_tap(b, totals):
            totals = list(totals)
            source = gcv[j - b, :, :, start : start + size]
            for a in range(TAPS):
                tap = taps[b, a, :, start : start + size]
                for i in range(SIDE):
                    totals[i + a] = totals[i + a] + source[i] * tap
            return tuple(totals)

        empty = tuple(jnp.zeros((TILE, size), F32) for _ in range(SIDE + 6))
        first_tap = jnp.maximum(0, j - (SIDE - 1))
        end_tap = jnp.minimum(TAPS, j + 1)
        totals = lax.fori_loop(first_tap, end_tap, add_tap, empty)
        for i in range(SIDE + 6):
            gpad[j, i, :, start : start + size] = totals[i]

    def spread_edge(j, carry):
        for k in (j, j + 11):
            spread_column(k, 0, low)
            spread_column(k, low, high)
        return carry

    def spread_inner(j, carry):
        spread_column(j, 0, low)
        spread_column(j, low, high)
        return carry

    for half in range(2):
        relay_on((mxa, mxb), (mxre_a, mxre_b), mx_made[half], half)
    lax.fori_loop(0, 3, spread_edge, 0)
    for layer in range(3):
        part = pl.ds(layer * 64, 64)
        for face, column, held in ((2, layer, ret_w), (3, 11 + layer, ret_e)):
            edge = gpad[column, 3 : 3 + SIDE].reshape(64, channels).astype(B16)
            held[part] = dot(picks[face * 3 + layer], edge).astype(B16)
    ret_west = copy(ret_w, ret_w_in, ret_s.at[0], ret_r.at[0], west)
    ret_east = copy(ret_e, ret_e_in, ret_s.at[1], ret_r.at[1], east)
    ret_west.start()
    ret_east.start()

    def gtwo_copies(k):
        yy, nn = one_place(k)
        return (
            copy(two_a.at[nn], two_in_a.at[k - 1], gtwo_s.at[0, k - 1], gtwo_r.at[0, k - 1], at_z(back_steps[k - 1])),
            copy(two_b.at[yy], two_in_b.at[k - 1], gtwo_s.at[1, k - 1], gtwo_r.at[1, k - 1], at_y(k)),
        )

    for k in range(1, 4):
        for c in gone_copies(k):
            c.wait_recv()
    for f in range(2):
        for mine, came, units in ((one_a, one_in_a, two_a), (one_b, one_in_b, two_b)):
            total = mine[0, f].astype(F32)
            for k in range(3):
                total = total + came[k, f].astype(F32)
            opened = dot(reopen, total.astype(B16)).astype(B16)
            for q in range(4):
                units[q, f] = opened[q * 16 : (q + 1) * 16]
    for k in range(1, 4):
        for c in gtwo_copies(k):
            c.start()

    lax.fori_loop(3, 11, spread_inner, 0)

    for k in range(1, 4):
        for c in gtwo_copies(k):
            c.wait_recv()
    total = two_a[near].astype(F32)
    other_total = two_b[y].astype(F32)
    for k in range(3):
        total = total + two_in_a[k].astype(F32)
        other_total = other_total + two_in_b[k].astype(F32)
    fsum[0:2] = total
    fsum[2:4] = other_total

    def gfar_copy(k):
        return copy(
            fsum.at[(far + k) % N_FAR], f_in.at[k - 1], gfar_s.at[k - 1], gfar_r.at[k - 1], at_z(4 * k)
        )

    for k in range(1, N_FAR):
        gfar_copy(k).start()

    tg[...] = go[...].astype(F32).reshape(SIDE, SIDE, TILE, channels) + gpad[3 : 3 + SIDE, 3 : 3 + SIDE]
    for layer in range(3):
        for face, row, target in ((0, layer, 5 + layer), (1, 11 + layer, layer)):
            edge = gpad[3 : 3 + SIDE, row].reshape(64, channels).astype(B16)
            back = dot(picks[face * 3 + layer], edge)
            tg[:, target] = tg[:, target] + back.reshape(SIDE, TILE, channels)

    for half in range(2):
        for p in range(2):
            mx_made[half][p][1].wait_recv()
            mx_made[half][p][2].wait_recv()
    low_part = mxa[x].astype(F32)
    packed = mxb[x].astype(F32)
    for k in range(2):
        low_part = low_part + mxin_a[k].astype(F32)
        packed = packed + mxin_b[k].astype(F32)
    tops, ends = packed[:128], packed[128:]
    high_part = jnp.concatenate([tops[:, :high], tops[:, high:], ends[:, :high], ends[:, high:]], axis=0)
    mixed = jnp.concatenate([low_part, high_part], axis=1)
    out = (xt[...].astype(F32) + scale_row * mixed).astype(B16)
    block_ref[...] = dot_tn(out, perm[...]).astype(B16)

    for k in range(1, N_FAR):
        gfar_copy(k).wait_recv()
    total = fsum[far]
    for k in range(1, N_FAR):
        total = total + f_in[k - 1]
    last[0, 0:8] = total[0:8]
    last[1, 0:8] = total[rows : rows + 8]
    gend = copy(last.at[1 - core], last_in.at[core], gend_s, gend_r, sibling)
    gend.start()
    last_in[core] = last[core]

    ret_west.wait_recv()
    ret_east.wait_recv()
    for layer in range(3):
        part = pl.ds(layer * 64, 64)
        tg[5 + layer] = tg[5 + layer] + ret_w_in[part].astype(F32).reshape(SIDE, TILE, channels)
        tg[layer] = tg[layer] + ret_e_in[part].astype(F32).reshape(SIDE, TILE, channels)
    grad_ref[...] = dot_tn(tg[...].reshape(cells, channels).astype(B16), perm[...]).astype(B16)

    gend.wait_recv()
    up_grad_ref[...] = last_in[0, 0:rows]
    down_grad_ref[...] = last_in[1, 0:rows]

    sent = [halo_west, halo_east, wsib, ret_west, ret_east, gend]
    sent += gain_copies + gm_first[0] + gm_first[1] + gm_next[0] + gm_next[1]
    sent += cv_first + cv_next + high_first + high_next + sum_copies[0] + sum_copies[1]
    for made in pg_made + mx_made:
        sent += made[0] + made[1]
    sent += [far_copy(k) for k in range(1, N_FAR)] + one_copies() + two_copies()
    sent += [share_a(k) for k in range(4)] + [share_b(k) for k in range(4)]
    for k in range(4):
        sent += gsib_copies(k)
    for k in range(1, 4):
        sent += gone_copies(k) + gtwo_copies(k)
    sent += [gfar_copy(k) for k in range(1, N_FAR)]
    for c in sent:
        c.wait_send()


def hand_over(*refs):
    for i in range(4):
        refs[4 + i][...] = refs[i][...]


def per_device(
    tiles, kernel, norm_gain, w_up, w_down, layer_scale, neighbors, shifts, halo_widths, land, cotangent
):
    channels, cells = tiles.shape
    rows, width = w_up.shape
    vmem = pl.BlockSpec(memory_space=pltpu.VMEM)
    dma = pltpu.SemaphoreType.DMA

    def v(dtype, *shape):
        return pltpu.VMEM(shape, dtype)

    strip = (2, 8 * rows, width)
    units = (2, 16, width)
    scratch = [
        v(B16, cells, cells), v(B16, 256, channels), v(B16, 12, 64, 64), v(F32, TAPS, TAPS, 8, channels),
        v(B16, cells, channels), v(B16, cells, channels), v(B16, 192, channels), v(B16, 192, channels),
        v(F32, SIDE + 6, SIDE + 6, TILE, channels), v(F32, N_X, 8, channels),
        v(B16, N_X, cells, 128), v(B16, N_X, HALF_ROWS, 128), v(B16, N_X, cells, 128), v(B16, N_X, HALF_ROWS, 128),
        v(F32, N_X, cells, channels), v(F32, cells, 128), v(B16, cells, N_X * 256), v(B16, cells, N_X * 256),
        v(B16, cells, width), v(B16, cells, width),
        v(B16, N_X, cells, 128), v(B16, N_X, HALF_ROWS, 128), v(B16, 2, cells, 128), v(B16, 2, HALF_ROWS, 128),
        v(B16, 2, HALF_ROWS, 128), v(B16, 2, 128, 128),
        v(B16, N_X, cells, 128), v(B16, N_X, HALF_ROWS, 128), v(B16, 2, cells, 128), v(B16, 2, HALF_ROWS, 128),
        v(B16, 2, HALF_ROWS, 128), v(B16, 2, 128, 128),
        v(F32, 2, 2, 8, 128), v(F32, 3, 2, 2, 8, 128), v(F32, 128, 128),
        v(F32, SIDE, SIDE, TILE, channels), v(F32, SIDE + 6, SIDE + 6, TILE, channels),
        v(B16, 192, channels), v(B16, 192, channels), v(B16, 192, channels), v(B16, 192, channels),
        v(F32, SIDE, SIDE, TILE, channels),
        v(B16, 2, 16, width), v(B16, N_FAR, 16, width), v(B16, 4, *units), v(B16, 4, *units),
        v(B16, 2, 4, *strip), v(B16, 2, 4, *strip), v(B16, 2, N_X * 256, width),
        v(B16, 2, 4, *strip), v(B16, 2, 4, *strip), v(B16, 4, *strip), v(B16, 4, *strip),
        v(B16, 4, *strip), v(B16, 4, *strip), v(B16, 3, *strip), v(B16, 3, *strip),
        v(B16, 4, *units), v(B16, 4, *units), v(B16, 3, *units), v(B16, 3, *units),
        v(F32, N_FAR, 16, width), v(F32, 3, 16, width), v(F32, 2, 8, width), v(F32, 2, 8, width),
    ]
    scratch += [v(B16, channels, cells), v(B16, channels, cells), dma((2,))]
    pairs = [(2,), (3,), (2, 4), (2, 4), (2, 3, 2), (2, 3, 2), (2, 3), (2,), None, (3,), (2, 3), (2, 3), (2, 4)]
    pairs += [(2, 4), (2, 3), (2, 3), (3,), None]
    for p in pairs:
        scratch += [dma if p is None else dma(p)] * 2
    shapes = [
        jax.ShapeDtypeStruct((channels, cells), B16),
        jax.ShapeDtypeStruct((channels, cells), B16),
        jax.ShapeDtypeStruct((rows, width), F32),
        jax.ShapeDtypeStruct((rows, width), F32),
    ]
    made = pl.pallas_call(
        functools.partial(block_kernel, rows, width),
        out_shape=shapes,
        in_specs=[pl.BlockSpec(memory_space=pl.ANY)] * 2 + [vmem] * 9,
        out_specs=[vmem] * 4,
        scratch_shapes=scratch,
        compiler_params=pltpu.CompilerParams(
            collective_id=0, has_side_effects=True, vmem_limit_bytes=56 * 1024 * 1024
        ),
    )(
        tiles, cotangent, land, kernel, norm_gain, layer_scale,
        jnp.transpose(neighbors, (1, 2, 0)), jnp.transpose(shifts, (1, 2, 0)), halo_widths.T, w_up, w_down,
    )
    return pl.pallas_call(
        hand_over,
        out_shape=shapes,
        in_specs=[vmem] * 4,
        out_specs=[vmem] * 4,
    )(*made)


def solution(mesh):
    return jax.shard_map(
        per_device,
        mesh=mesh,
        in_specs=(
            P("fsdp", "dp"),
            P(None, "fsdp"),
            P("fsdp"),
            P("dp", "fsdp"),
            P("dp", "fsdp"),
            P("fsdp"),
            P("dp", None, None),
            P("dp", None, None),
            P("dp", None),
            P("dp", None, None),
            P("fsdp", "dp"),
        ),
        out_specs=(P("fsdp", "dp"), P("fsdp", "dp"), P("dp", "fsdp"), P("dp", "fsdp")),
        check_vma=False,
    )
```

```python
import functools
import math

import jax
import jax.numpy as jnp
from jax import lax
from jax.experimental import pallas as pl
from jax.experimental.pallas import tpu as pltpu
from jax.sharding import PartitionSpec as P

root_half = 1.0 / math.sqrt(2.0)
root_tau = 1.0 / math.sqrt(2.0 * math.pi)

N_Z, N_Y, N_CORE, N_X = 16, 4, 2, 4
N_FAR, N_NEAR = 4, 4
N_DP = N_Z * N_Y * N_CORE
MESH = pl.DeviceIdType.MESH
F32, B16 = jnp.float32, jnp.bfloat16
SIDE, TILE, TAPS = 8, 8, 7
HALF_ROWS = 256


def dp_index(z, y, core):
    return (z * N_Y + y) * N_CORE + core


def dot(a, b):
    return jnp.dot(a, b, preferred_element_type=F32)


def dot_nt(a, b):
    return lax.dot_general(a, b, (((1,), (1,)), ((), ())), preferred_element_type=F32)


def dot_tn(a, b):
    return lax.dot_general(a, b, (((0,), (0,)), ((), ())), preferred_element_type=F32)


def block_kernel(
    rows, width,
    x_ref, cot_ref, land_ref, taps_ref, gain_ref, scale_ref, owner_ref, shift_ref, depth_ref, up_ref, down_ref,
    block_ref, grad_ref, up_grad_ref, down_grad_ref,
    perm, order, picks, taps, xt, go, east_in, west_in, pad, gains,
    gma, gmb, cva, cvb, cen, inv, nrm, gmx, hid, gpre,
    pga, pgb, pgin_a, pgin_b, pgre_a, pgre_b, mxa, mxb, mxin_a, mxin_b, mxre_a, mxre_b, sums, sums_in, sum_cols,
    gcv, gpad, ret_w, ret_e, ret_w_in, ret_e_in, tg,
    unit_in, wfar, wone_a, wone_b, wtwo_a, wtwo_b, dense,
    st_a, st_b, st_in_a, st_in_b, one_a, one_b, one_in_a, one_in_b, two_a, two_b, two_in_a, two_in_b,
    fsum, f_in, last, last_in,
    x_in, cot_in, in_sem, halo_s, halo_r, gain_s, gain_r, gm_s, gm_r, cv_s, cv_r, pg_s, pg_r, mx_s, mx_r, sum_s, sum_r,
    ret_s, ret_r, wsib_s, wsib_r, wfar_s, wfar_r, wone_s, wone_r, wtwo_s, wtwo_r, wsh_s, wsh_r,
    gsib_s, gsib_r, gone_s, gone_r, gtwo_s, gtwo_r, gfar_s, gfar_r, gend_s, gend_r,
):
    channels = x_ref.shape[0]
    low, high = 128, channels - 128
    cells = x_ref.shape[1]
    me = lax.axis_index("dp")
    x = lax.axis_index("fsdp")
    z, y, core = me // (N_Y * N_CORE), (me // N_CORE) % N_Y, me % N_CORE
    far, near = z // N_NEAR, z % N_NEAR
    east, west = (me + 1) % N_DP, (me + N_DP - 1) % N_DP
    sibling = dp_index(z, y, 1 - core)

    def at_z(step):
        return dp_index((z + step + N_Z) % N_Z, y, core)

    def at_y(k):
        return dp_index(z, (y + k) % N_Y, core)

    def copy(src, dst, send, recv, dp, fs=None):
        return pltpu.make_async_remote_copy(
            src_ref=src, dst_ref=dst, send_sem=send, recv_sem=recv,
            device_id=(dp, x if fs is None else fs), device_id_type=MESH,
        )

    barrier = pltpu.get_barrier_semaphore()
    greeted = [(east, x), (west, x), (sibling, x)]
    greeted += [(me, (x + k) % N_X) for k in range(1, N_X)]
    greeted += [(at_z(s), x) for s in (4, 8, 12, 1, -1, 2, -2)]
    greeted += [(at_y(k), x) for k in range(1, N_Y)]
    for other in greeted:
        pl.semaphore_signal(barrier, inc=1, device_id=other, device_id_type=MESH)
    x_load = pltpu.make_async_copy(x_ref, x_in, in_sem.at[0])
    cot_load = pltpu.make_async_copy(cot_ref, cot_in, in_sem.at[1])
    x_load.start()
    cot_load.start()

    out_cell = lax.broadcasted_iota(jnp.int32, (cells, cells), 0)
    in_cell = lax.broadcasted_iota(jnp.int32, (cells, cells), 1)
    wanted = (out_cell % 8) * 64 + ((out_cell // 8) % 8) * 8 + out_cell // 64
    perm[...] = jnp.where(in_cell == wanted, 1.0, 0.0).astype(B16)
    x_load.wait()
    xt[...] = dot_nt(perm[...], x_in[...]).astype(B16)
    cot_load.wait()
    j_row = lax.broadcasted_iota(jnp.int32, (SIDE, cells), 0)
    j_col = lax.broadcasted_iota(jnp.int32, (SIDE, cells), 1)
    spread_j = jnp.where(j_row == j_col % SIDE, 1.0, 0.0).astype(B16)
    land = land_ref[...].astype(F32).reshape(TILE * SIDE, SIDE).astype(B16)
    ti_row = lax.broadcasted_iota(jnp.int32, (TILE * SIDE, cells), 0)
    ti_col = lax.broadcasted_iota(jnp.int32, (TILE * SIDE, cells), 1)
    land_row = jnp.sum(
        jnp.where(ti_row == ti_col // SIDE, dot(land, spread_j), 0.0), axis=0, keepdims=True
    ).astype(B16)
    go[...] = dot_nt(perm[...], cot_in[...] * land_row).astype(B16)
    scale_row = scale_ref[...].astype(F32).reshape(1, channels)
    grad_mixed = (go[...].astype(F32) * scale_row).astype(B16)
    gma[x] = grad_mixed[:, :low]
    gmb[x] = jnp.concatenate([grad_mixed[:HALF_ROWS, low:], grad_mixed[HALF_ROWS:, low:]], axis=1)
    gains[x] = jnp.broadcast_to(gain_ref[...].astype(F32).reshape(1, channels), (8, channels))
    s_row = lax.broadcasted_iota(jnp.int32, (16, rows), 0)
    s_col = lax.broadcasted_iota(jnp.int32, (16, rows), 1)
    unit_in[core] = (
        dot(jnp.where(s_row == s_col, 1.0, 0.0).astype(B16), up_ref[...])
        + dot(jnp.where(s_row == s_col + 8, 1.0, 0.0).astype(B16), down_ref[...])
    ).astype(B16)

    pl.semaphore_wait(barrier, len(greeted))

    halo_west = copy(xt.at[pl.ds(0, 192)], east_in, halo_s.at[0], halo_r.at[0], west)
    halo_east = copy(xt.at[pl.ds(cells - 192, 192)], west_in, halo_s.at[1], halo_r.at[1], east)
    halo_west.start()
    halo_east.start()
    wsib = copy(unit_in.at[core], unit_in.at[core], wsib_s, wsib_r, sibling)
    wsib.start()

    right, left, across = (x + 1) % N_X, (x + N_X - 1) % N_X, (x + 2) % N_X

    def gather_first(buffer, send, recv):
        return [
            copy(buffer.at[x], buffer.at[x], send.at[0], recv.at[0], me, right),
            copy(buffer.at[x], buffer.at[x], send.at[1], recv.at[1], me, left),
        ]

    def gather_next(buffer, send, recv):
        count = buffer.shape[1] // 2
        head, tail = pl.ds(0, count), pl.ds(count, count)
        return [
            copy(buffer.at[left, head], buffer.at[left, head], send.at[2], recv.at[2], me, right),
            copy(buffer.at[right, tail], buffer.at[right, tail], send.at[3], recv.at[3], me, left),
        ]

    def forward(first, later):
        for c, n in zip(first, later):
            c.wait_recv()
            n.start()

    gain_copies = []
    for k in range(1, N_X):
        gain_copies.append(
            copy(gains.at[x], gains.at[x], gain_s.at[k - 1], gain_r.at[k - 1], me, (x + k) % N_X)
        )
    gm_first = gather_first(gma, gm_s.at[0], gm_r.at[0]), gather_first(gmb, gm_s.at[1], gm_r.at[1])
    gm_next = gather_next(gma, gm_s.at[0], gm_r.at[0]), gather_next(gmb, gm_s.at[1], gm_r.at[1])
    for c in gm_first[0] + gm_first[1] + gain_copies:
        c.start()

    def scatter_copies(held, came, relay, send, recv, half):
        toward, away = (right, left) if half == 0 else (left, right)
        made = []
        for p in range(2):
            count = held[p].shape[1] // 2
            part = pl.ds(half * count, count)
            made.append((
                copy(held[p].at[across, part], relay[p].at[half], send.at[half, 0, p], recv.at[half, 0, p], me, toward),
                copy(
                    held[p].at[away, part], came[p].at[1 - half, part], send.at[half, 1, p], recv.at[half, 1, p], me, away
                ),
                copy(
                    held[p].at[toward, part], came[p].at[half, part], send.at[half, 2, p], recv.at[half, 2, p], me, toward
                ),
            ))
        return made

    def relay_on(held, relay, made, half):
        toward = right if half == 0 else left
        for p in range(2):
            count = held[p].shape[1] // 2
            part = pl.ds(half * count, count)
            made[p][0].wait_recv()
            held[p][toward, part] = (held[p][toward, part].astype(F32) + relay[p][half].astype(F32)).astype(B16)
            made[p][2].start()

    pg_made = [scatter_copies((pga, pgb), (pgin_a, pgin_b), (pgre_a, pgre_b), pg_s, pg_r, h) for h in range(2)]
    mx_made = [scatter_copies((mxa, mxb), (mxin_a, mxin_b), (mxre_a, mxre_b), mx_s, mx_r, h) for h in range(2)]

    edge_row = lax.broadcasted_iota(jnp.int32, (64, 64), 0)
    for face in range(4):
        chosen = jnp.zeros((64, 64), F32)
        for entry in range(2):
            owner = owner_ref[face, entry : entry + 1, :]
            shift = shift_ref[face, entry : entry + 1, :]
            target = jnp.where(owner >= 0, owner % TILE + TILE * shift, -4096)
            target = jnp.concatenate([target + TILE * p for p in range(SIDE)], axis=1)
            chosen = chosen + jnp.where(target == edge_row, 1.0, 0.0)
        widths = jnp.concatenate([depth_ref[face : face + 1, :]] * SIDE, axis=1)
        for layer in range(3):
            depth = 3 - layer if face in (0, 2) else layer + 1
            picks[face * 3 + layer] = jnp.where(widths >= depth, chosen, 0.0).astype(B16)

    kernel_taps = taps_ref[...].astype(F32)
    for a in range(TAPS):
        for b in range(TAPS):
            k = a * TAPS + b
            taps[b, a] = jnp.broadcast_to(kernel_taps[k : k + 1], (8, channels))

    pad[...] = jnp.zeros_like(pad)
    cells_f = xt[...].astype(F32).reshape(SIDE, SIDE, TILE, channels)
    pad[3 : 3 + SIDE, 3 : 3 + SIDE] = cells_f
    for layer in range(3):
        north = cells_f[:, 5 + layer].reshape(64, channels).astype(B16)
        south = cells_f[:, layer].reshape(64, channels).astype(B16)
        pad[3 : 3 + SIDE, layer] = dot_tn(picks[layer], north).astype(B16).astype(F32).reshape(SIDE, TILE, channels)
        pad[3 : 3 + SIDE, 11 + layer] = (
            dot_tn(picks[3 + layer], south).astype(B16).astype(F32).reshape(SIDE, TILE, channels)
        )

    wsib.wait_recv()
    both = unit_in[...].reshape(N_CORE * 16, width)
    u_row = lax.broadcasted_iota(jnp.int32, (16, N_CORE * 16), 0)
    u_col = lax.broadcasted_iota(jnp.int32, (16, N_CORE * 16), 1)
    first = (u_row < rows) & (u_col == u_row + 8 * core)
    second = (u_row >= rows) & (u_row < 2 * rows) & (u_col == 16 + u_row - rows + 8 * core)
    joined = dot(jnp.where(first | second, 1.0, 0.0).astype(B16), both).astype(B16)
    wfar[far] = joined

    def far_copy(k):
        place = wfar.at[far]
        return copy(place, place, wfar_s.at[k - 1], wfar_r.at[k - 1], at_z(4 * k))

    for k in range(1, N_FAR):
        far_copy(k).start()

    halo_west.wait_recv()
    halo_east.wait_recv()
    for layer in range(3):
        part = pl.ds(layer * 64, 64)
        pad[layer, 3 : 3 + SIDE] = (
            dot_tn(picks[6 + layer], west_in[part]).astype(B16).astype(F32).reshape(SIDE, TILE, channels)
        )
        pad[11 + layer, 3 : 3 + SIDE] = (
            dot_tn(picks[9 + layer], east_in[part]).astype(B16).astype(F32).reshape(SIDE, TILE, channels)
        )

    def conv_column(j, start, size):
        total = jnp.zeros((SIDE, TILE, size), F32)
        for b in range(TAPS):
            source = pad[j + b, :, :, start : start + size]
            for a in range(TAPS):
                total = total + source[a : a + SIDE] * taps[b, a, :, start : start + size][None]
        return total.reshape(64, size).astype(B16)

    def conv_low(j, carry):
        cva[x, pl.ds(pl.multiple_of(j * 64, 64), 64)] = conv_column(j, 0, low)
        return carry

    def conv_high(j, carry):
        cvb[x, pl.ds(pl.multiple_of(j * 64, 64), 64)] = jnp.concatenate(
            [conv_column(j, low, high), conv_column(j + 4, low, high)], axis=1
        )
        return carry

    lax.fori_loop(0, SIDE, conv_low, 0)
    cv_first = gather_first(cva, cv_s.at[0], cv_r.at[0])
    cv_next = gather_next(cva, cv_s.at[0], cv_r.at[0])
    for c in cv_first:
        c.start()

    for k in range(1, N_FAR):
        far_copy(k).wait_recv()

    near_steps = (1, -1, -2)

    def one_copies():
        made = []
        for k in range(3):
            made.append(
                copy(wone_a.at[near], wone_a.at[near], wone_s.at[0, k], wone_r.at[0, k], at_z(near_steps[k]))
            )
            made.append(copy(wone_b.at[y], wone_b.at[y], wone_s.at[1, k], wone_r.at[1, k], at_y(k + 1)))
        return made

    wone_a[near] = wfar[0:2]
    wone_b[y] = wfar[2:4]
    for c in one_copies():
        c.start()

    lax.fori_loop(0, 4, conv_high, 0)
    high_first = gather_first(cvb, cv_s.at[1], cv_r.at[1])
    high_next = gather_next(cvb, cv_s.at[1], cv_r.at[1])
    for c in high_first:
        c.start()
    forward(gm_first[0], gm_next[0])
    forward(gm_first[1], gm_next[1])

    span = N_CORE * rows
    w_row = lax.broadcasted_iota(jnp.int32, (256, channels), 0)
    w_col = lax.broadcasted_iota(jnp.int32, (256, channels), 1)
    w_from = ((w_row // span) % N_Y) * (span * N_NEAR) + (w_row // (span * N_Y)) * span + w_row % span
    order[...] = jnp.where((w_col == w_from) & (w_row < channels), 1.0, 0.0).astype(B16)
    p_row = lax.broadcasted_iota(jnp.int32, (4 * span, 64), 0)
    p_col = lax.broadcasted_iota(jnp.int32, (4 * span, 64), 1)
    close = jnp.where(p_col == (p_row // span) * 16 + p_row % span, 1.0, 0.0).astype(B16)
    gap_row = lax.broadcasted_iota(jnp.int32, (64, 4 * span), 0)
    gap_col = lax.broadcasted_iota(jnp.int32, (64, 4 * span), 1)
    reopen = jnp.where(gap_row == (gap_col // span) * 16 + gap_col % span, 1.0, 0.0).astype(B16)

    def two_copies():
        made = []
        for k in range(3):
            place = wtwo_a.at[core, y]
            made.append(copy(place, place, wtwo_s.at[0, k], wtwo_r.at[0, k], at_y(k + 1)))
            place = wtwo_b.at[core, near]
            made.append(copy(place, place, wtwo_s.at[1, k], wtwo_r.at[1, k], at_z(near_steps[k])))
        return made

    def share_a(k):
        place = wtwo_a.at[core, (y + N_Y - k) % N_Y]
        return copy(place, place, wsh_s.at[0, k], wsh_r.at[0, k], sibling)

    def share_b(k):
        step = 0 if k == 0 else near_steps[k - 1]
        place = wtwo_b.at[core, (near - step + N_NEAR) % N_NEAR]
        return copy(place, place, wsh_s.at[1, k], wsh_r.at[1, k], sibling)

    for c in one_copies():
        c.wait_recv()
    for f in range(2):
        rows_a = jnp.concatenate([wone_a[nn, f] for nn in range(N_NEAR)], axis=0)
        wtwo_a[core, y, f] = dot(close, rows_a).astype(B16)
        rows_b = jnp.concatenate([wone_b[yy, f] for yy in range(N_Y)], axis=0)
        wtwo_b[core, near, f] = dot(close, rows_b).astype(B16)
    for c in two_copies():
        c.start()
    share_a(0).start()
    share_b(0).start()

    forward(cv_first, cv_next)
    forward(high_first, high_next)
    for c in gm_next[0] + gm_next[1]:
        c.wait_recv()
    for b in range(N_X):
        gap = jnp.zeros((cells, 256 - channels), B16)
        nrm[:, b * 256 + channels : (b + 1) * 256] = gap
        gmx[:, b * 256 + channels : (b + 1) * 256] = gap
        gmx[:, b * 256 : b * 256 + low] = gma[b]
        packed = gmb[b]
        gmx[:HALF_ROWS, b * 256 + low : b * 256 + channels] = packed[:, :high]
        gmx[HALF_ROWS:, b * 256 + low : b * 256 + channels] = packed[:, high:]

    for c in gain_copies + cv_next + high_next:
        c.wait_recv()

    wide = float(channels * N_X)
    for half in range(2):

        def norm_rows(i, carry, half=half):
            part = pl.ds(pl.multiple_of(i * 64, 64), 64)
            here = pl.ds(pl.multiple_of(half * HALF_ROWS + i * 64, 64), 64)
            lows = [cva[b, here].astype(F32) for b in range(N_X)]
            highs = [cvb[b, part, half * high : (half + 1) * high].astype(F32) for b in range(N_X)]
            total = jnp.sum(sum(lows), axis=1, keepdims=True) + jnp.sum(sum(highs), axis=1, keepdims=True)
            square = jnp.sum(sum(v * v for v in lows), axis=1, keepdims=True) + jnp.sum(
                sum(v * v for v in highs), axis=1, keepdims=True
            )
            mean = total / wide
            scale = lax.rsqrt(square / wide - mean * mean + 1e-06)
            inv[here] = jnp.broadcast_to(scale, (64, 128))
            for b in range(N_X):
                centered = (lows[b] - mean) * scale
                cen[b, here, 0:low] = centered
                nrm[here, b * 256 : b * 256 + low] = (centered * gains[b, 0:1, 0:low]).astype(B16)
                centered = (highs[b] - mean) * scale
                cen[b, here, low:channels] = centered
                nrm[here, b * 256 + low : b * 256 + channels] = (
                    centered * gains[b, 0:1, low:channels]
                ).astype(B16)
            return carry

        lax.fori_loop(0, 4, norm_rows, 0)
        if half == 0:
            arrived = two_copies()
            for k in range(1, 4):
                arrived[2 * k - 2].wait_recv()
                share_a(k).start()
                arrived[2 * k - 1].wait_recv()
                share_b(k).start()

    for k in range(4):
        share_a(k).wait_recv()
        share_b(k).wait_recv()
    for m in range(2):
        for f in range(2):
            rows_a = jnp.concatenate([wtwo_a[m, yy, f] for yy in range(N_Y)], axis=0)
            dense[m, f * 256 : (f + 1) * 256] = dot(order[...], rows_a).astype(B16)
            for nn in range(N_NEAR):
                r = (f + 2) * 256 + nn * 4 * span
                dense[m, r : r + 4 * span] = wtwo_b[m, nn, f]
            dense[m, (f + 2) * 256 + channels : (f + 3) * 256] = jnp.zeros((256 - channels, width), B16)

    sum_copies = []
    for half in range(2):
        for i in range(2):
            start = half * HALF_ROWS + i * 128
            here = slice(start, start + 128)
            part = slice(half * 128, half * 128 + 128)
            pre = dot(nrm[here], dense[0])
            edge = 0.5 * (1.0 + lax.erf(pre * root_half))
            hid[here] = (pre * edge).astype(B16)
            slope = edge + pre * jnp.exp(-0.5 * pre * pre) * root_tau
            grad_pre = (dot(gmx[here], dense[1]) * slope).astype(B16)
            gpre[here] = grad_pre
            back = dot_nt(grad_pre, dense[0]).astype(B16)
            first_sum = jnp.zeros((128, 128), F32)
            second_sum = jnp.zeros((128, 128), F32)
            first_high = jnp.zeros((128, high), F32)
            second_high = jnp.zeros((128, high), F32)
            for b in range(N_X):
                low_part = back[:, b * 256 : b * 256 + low]
                high_part = back[:, b * 256 + low : b * 256 + channels]
                pga[b, here] = low_part
                pgb[b, part, i * high : (i + 1) * high] = high_part
                g = low_part.astype(F32) * gains[b, 0:1, 0:low]
                first_sum += g
                second_sum += g * cen[b, here, 0:low]
                g = high_part.astype(F32) * gains[b, 0:1, low:channels]
                first_high += g
                second_high += g * cen[b, here, low:channels]
            one = jnp.sum(first_sum, axis=1, keepdims=True) + jnp.sum(first_high, axis=1, keepdims=True)
            two = jnp.sum(second_sum, axis=1, keepdims=True) + jnp.sum(second_high, axis=1, keepdims=True)
            lane = lax.broadcasted_iota(jnp.int32, (128, 128), 1)
            columns = jnp.where(lane == 0, one, jnp.where(lane == 1, two, 0.0))
            sums[half, i] = jnp.transpose(columns)[0:8]
        made = []
        for k in range(1, N_X):
            other = (x + k) % N_X
            made.append(
                copy(sums.at[half], sums_in.at[k - 1, half], sum_s.at[half, k - 1], sum_r.at[half, k - 1], me, other)
            )
        for p in range(2):
            pg_made[half][p][0].start()
        for p in range(2):
            pg_made[half][p][1].start()
        for c in made:
            c.start()
        sum_copies.append(made)
    relay_on((pga, pgb), (pgre_a, pgre_b), pg_made[0], 0)

    for b in range(N_X):
        for m, inner, outer in ((0, nrm, gpre), (1, gmx, hid)):
            local = dot_tn(inner[:, b * 256 : (b + 1) * 256], outer[...]).astype(B16)
            if b < 2:
                local = dot_tn(order[...], local).astype(B16)
            for q in range(4):
                r = q * 4 * span
                if b < 2:
                    st_a[m, q, b] = local[r : r + 4 * span]
                else:
                    st_b[m, q, b - 2] = local[r : r + 4 * span]

    back_steps = (-1, 1, 2)

    def one_place(k):
        step = 0 if k == 0 else back_steps[k - 1]
        return (y + k) % N_Y, (near + step + N_NEAR) % N_NEAR

    def gsib_copies(k):
        yy, nn = one_place(k)
        return (
            copy(st_a.at[1 - core, yy], st_in_a.at[yy], gsib_s.at[0, k], gsib_r.at[0, k], sibling),
            copy(st_b.at[1 - core, nn], st_in_b.at[nn], gsib_s.at[1, k], gsib_r.at[1, k], sibling),
        )

    for k in (1, 2, 3, 0):
        for c in gsib_copies(k):
            c.start()

    relay_on((pga, pgb), (pgre_a, pgre_b), pg_made[1], 1)

    def gone_copies(k):
        return (
            copy(one_a.at[k], one_in_a.at[k - 1], gone_s.at[0, k - 1], gone_r.at[0, k - 1], at_y(k)),
            copy(
                one_b.at[k], one_in_b.at[k - 1], gone_s.at[1, k - 1], gone_r.at[1, k - 1], at_z(back_steps[k - 1])
            ),
        )

    for k in (1, 2, 3, 0):
        yy, nn = one_place(k)
        over_y, over_z = gsib_copies(k)
        over_y.wait_recv()
        one_a[k] = (st_a[core, yy].astype(F32) + st_in_a[yy].astype(F32)).astype(B16)
        if k > 0:
            to_y, to_z = gone_copies(k)
            to_y.start()
        over_z.wait_recv()
        one_b[k] = (st_b[core, nn].astype(F32) + st_in_b[nn].astype(F32)).astype(B16)
        if k > 0:
            to_z.start()

    for half in range(2):
        for i in range(2):
            start = half * HALF_ROWS + i * 128
            mixed = dot_nt(hid[start : start + 128], dense[1]).astype(B16)
            for b in range(N_X):
                mxa[b, start : start + 128] = mixed[:, b * 256 : b * 256 + low]
                mxb[b, half * 128 : half * 128 + 128, i * high : (i + 1) * high] = mixed[
                    :, b * 256 + low : b * 256 + channels
                ]
        for p in range(2):
            mx_made[half][p][0].start()
            mx_made[half][p][1].start()

    gcv[...] = jnp.zeros_like(gcv)
    for half in range(2):
        for c in sum_copies[half]:
            c.wait_recv()
        for p in range(2):
            pg_made[half][p][1].wait_recv()
            pg_made[half][p][2].wait_recv()
        for i in range(2):
            total = sums[half, i]
            for k in range(N_X - 1):
                total = total + sums_in[k, half, i]
            spread = jnp.concatenate([total / wide, jnp.zeros((120, 128), F32)], axis=0)
            sum_cols[...] = jnp.transpose(spread)
            lanes = slice(i * high, (i + 1) * high)

            def back_rows(n, carry, half=half, i=i, lanes=lanes):
                column = half * 4 + i * 2 + n
                part = pl.ds(pl.multiple_of(half * 128 + n * 64, 64), 64)
                here = pl.ds(pl.multiple_of(column * 64, 64), 64)
                low_part = pga[x, here].astype(F32)
                high_part = pgb[x, part, lanes].astype(F32)
                for k in range(2):
                    low_part = low_part + pgin_a[k, here].astype(F32)
                    high_part = high_part + pgin_b[k, part, lanes].astype(F32)
                local = pl.ds(pl.multiple_of(n * 64, 64), 64)
                e1 = sum_cols[local, 0:1]
                e2 = sum_cols[local, 1:2]
                scale = inv[here]
                g = low_part * gains[x, 0:1, 0:low]
                g = scale * (g - e1 - cen[x, here, 0:low] * e2)
                gcv[column, :, :, 0:low] = g.astype(B16).astype(F32).reshape(SIDE, TILE, low)
                g = high_part * gains[x, 0:1, low:channels]
                g = scale[:, :high] * (g - e1 - cen[x, here, low:channels] * e2)
                gcv[column, :, :, low:channels] = g.astype(B16).astype(F32).reshape(SIDE, TILE, high)
                return carry

            lax.fori_loop(0, 2, back_rows, 0)

    def spread_column(j, start, size):
        def add_tap(b, totals):
            totals = list(totals)
            source = gcv[j - b, :, :, start : start + size]
            for a in range(TAPS):
                tap = taps[b, a, :, start : start + size]
                for i in range(SIDE):
                    totals[i + a] = totals[i + a] + source[i] * tap
            return tuple(totals)

        empty = tuple(jnp.zeros((TILE, size), F32) for _ in range(SIDE + 6))
        first_tap = jnp.maximum(0, j - (SIDE - 1))
        end_tap = jnp.minimum(TAPS, j + 1)
        totals = lax.fori_loop(first_tap, end_tap, add_tap, empty)
        for i in range(SIDE + 6):
            gpad[j, i, :, start : start + size] = totals[i]

    def spread_edge(j, carry):
        for k in (j, j + 11):
            spread_column(k, 0, low)
            spread_column(k, low, high)
        return carry

    def spread_inner(j, carry):
        spread_column(j, 0, low)
        spread_column(j, low, high)
        return carry

    def gtwo_copies(k):
        yy, nn = one_place(k)
        return (
            copy(two_a.at[nn], two_in_a.at[k - 1], gtwo_s.at[0, k - 1], gtwo_r.at[0, k - 1], at_z(back_steps[k - 1])),
            copy(two_b.at[yy], two_in_b.at[k - 1], gtwo_s.at[1, k - 1], gtwo_r.at[1, k - 1], at_y(k)),
        )

    for k in range(1, 4):
        for c in gone_copies(k):
            c.wait_recv()
    for f in range(2):
        for mine, came, units in ((one_a, one_in_a, two_a), (one_b, one_in_b, two_b)):
            total = mine[0, f].astype(F32)
            for k in range(3):
                total = total + came[k, f].astype(F32)
            opened = dot(reopen, total.astype(B16)).astype(B16)
            for q in range(4):
                units[q, f] = opened[q * 16 : (q + 1) * 16]
    for k in range(1, 4):
        for c in gtwo_copies(k):
            c.start()

    lax.fori_loop(0, 3, spread_edge, 0)
    for layer in range(3):
        part = pl.ds(layer * 64, 64)
        for face, column, held in ((2, layer, ret_w), (3, 11 + layer, ret_e)):
            edge = gpad[column, 3 : 3 + SIDE].reshape(64, channels).astype(B16)
            held[part] = dot(picks[face * 3 + layer], edge).astype(B16)
    ret_west = copy(ret_w, ret_w_in, ret_s.at[0], ret_r.at[0], west)
    ret_east = copy(ret_e, ret_e_in, ret_s.at[1], ret_r.at[1], east)
    ret_west.start()
    ret_east.start()

    for half in range(2):
        relay_on((mxa, mxb), (mxre_a, mxre_b), mx_made[half], half)
    lax.fori_loop(3, 11, spread_inner, 0)

    for k in range(1, 4):
        for c in gtwo_copies(k):
            c.wait_recv()
    total = two_a[near].astype(F32)
    other_total = two_b[y].astype(F32)
    for k in range(3):
        total = total + two_in_a[k].astype(F32)
        other_total = other_total + two_in_b[k].astype(F32)
    fsum[0:2] = total
    fsum[2:4] = other_total

    def gfar_copy(k):
        return copy(
            fsum.at[(far + k) % N_FAR], f_in.at[k - 1], gfar_s.at[k - 1], gfar_r.at[k - 1], at_z(4 * k)
        )

    for k in range(1, N_FAR):
        gfar_copy(k).start()

    tg[...] = go[...].astype(F32).reshape(SIDE, SIDE, TILE, channels) + gpad[3 : 3 + SIDE, 3 : 3 + SIDE]
    for layer in range(3):
        for face, row, target in ((0, layer, 5 + layer), (1, 11 + layer, layer)):
            edge = gpad[3 : 3 + SIDE, row].reshape(64, channels).astype(B16)
            back = dot(picks[face * 3 + layer], edge)
            tg[:, target] = tg[:, target] + back.reshape(SIDE, TILE, channels)

    ret_west.wait_recv()
    ret_east.wait_recv()
    for layer in range(3):
        part = pl.ds(layer * 64, 64)
        tg[5 + layer] = tg[5 + layer] + ret_w_in[part].astype(F32).reshape(SIDE, TILE, channels)
        tg[layer] = tg[layer] + ret_e_in[part].astype(F32).reshape(SIDE, TILE, channels)
    grad_ref[...] = dot_tn(tg[...].reshape(cells, channels).astype(B16), perm[...]).astype(B16)

    for half in range(2):
        for p in range(2):
            mx_made[half][p][1].wait_recv()
            mx_made[half][p][2].wait_recv()
    low_part = mxa[x].astype(F32)
    packed = mxb[x].astype(F32)
    for k in range(2):
        low_part = low_part + mxin_a[k].astype(F32)
        packed = packed + mxin_b[k].astype(F32)
    tops, ends = packed[:128], packed[128:]
    high_part = jnp.concatenate([tops[:, :high], tops[:, high:], ends[:, :high], ends[:, high:]], axis=0)
    mixed = jnp.concatenate([low_part, high_part], axis=1)
    out = (xt[...].astype(F32) + scale_row * mixed).astype(B16)
    block_ref[...] = dot_tn(out, perm[...]).astype(B16)

    for k in range(1, N_FAR):
        gfar_copy(k).wait_recv()
    total = fsum[far]
    for k in range(1, N_FAR):
        total = total + f_in[k - 1]
    last[0, 0:8] = total[0:8]
    last[1, 0:8] = total[rows : rows + 8]
    gend = copy(last.at[1 - core], last_in.at[core], gend_s, gend_r, sibling)
    gend.start()
    last_in[core] = last[core]

    gend.wait_recv()
    up_grad_ref[...] = last_in[0, 0:rows]
    down_grad_ref[...] = last_in[1, 0:rows]

    sent = [halo_west, halo_east, wsib, ret_west, ret_east, gend]
    sent += gain_copies + gm_first[0] + gm_first[1] + gm_next[0] + gm_next[1]
    sent += cv_first + cv_next + high_first + high_next + sum_copies[0] + sum_copies[1]
    for made in pg_made + mx_made:
        sent += made[0] + made[1]
    sent += [far_copy(k) for k in range(1, N_FAR)] + one_copies() + two_copies()
    sent += [share_a(k) for k in range(4)] + [share_b(k) for k in range(4)]
    for k in range(4):
        sent += gsib_copies(k)
    for k in range(1, 4):
        sent += gone_copies(k) + gtwo_copies(k)
    sent += [gfar_copy(k) for k in range(1, N_FAR)]
    for c in sent:
        c.wait_send()


def hand_over(*refs):
    for i in range(4):
        refs[4 + i][...] = refs[i][...]


def per_device(
    tiles, kernel, norm_gain, w_up, w_down, layer_scale, neighbors, shifts, halo_widths, land, cotangent
):
    channels, cells = tiles.shape
    rows, width = w_up.shape
    vmem = pl.BlockSpec(memory_space=pltpu.VMEM)
    dma = pltpu.SemaphoreType.DMA

    def v(dtype, *shape):
        return pltpu.VMEM(shape, dtype)

    strip = (2, 8 * rows, width)
    units = (2, 16, width)
    scratch = [
        v(B16, cells, cells), v(B16, 256, channels), v(B16, 12, 64, 64), v(F32, TAPS, TAPS, 8, channels),
        v(B16, cells, channels), v(B16, cells, channels), v(B16, 192, channels), v(B16, 192, channels),
        v(F32, SIDE + 6, SIDE + 6, TILE, channels), v(F32, N_X, 8, channels),
        v(B16, N_X, cells, 128), v(B16, N_X, HALF_ROWS, 128), v(B16, N_X, cells, 128), v(B16, N_X, HALF_ROWS, 128),
        v(F32, N_X, cells, channels), v(F32, cells, 128), v(B16, cells, N_X * 256), v(B16, cells, N_X * 256),
        v(B16, cells, width), v(B16, cells, width),
        v(B16, N_X, cells, 128), v(B16, N_X, HALF_ROWS, 128), v(B16, 2, cells, 128), v(B16, 2, HALF_ROWS, 128),
        v(B16, 2, HALF_ROWS, 128), v(B16, 2, 128, 128),
        v(B16, N_X, cells, 128), v(B16, N_X, HALF_ROWS, 128), v(B16, 2, cells, 128), v(B16, 2, HALF_ROWS, 128),
        v(B16, 2, HALF_ROWS, 128), v(B16, 2, 128, 128),
        v(F32, 2, 2, 8, 128), v(F32, 3, 2, 2, 8, 128), v(F32, 128, 128),
        v(F32, SIDE, SIDE, TILE, channels), v(F32, SIDE + 6, SIDE + 6, TILE, channels),
        v(B16, 192, channels), v(B16, 192, channels), v(B16, 192, channels), v(B16, 192, channels),
        v(F32, SIDE, SIDE, TILE, channels),
        v(B16, 2, 16, width), v(B16, N_FAR, 16, width), v(B16, 4, *units), v(B16, 4, *units),
        v(B16, 2, 4, *strip), v(B16, 2, 4, *strip), v(B16, 2, N_X * 256, width),
        v(B16, 2, 4, *strip), v(B16, 2, 4, *strip), v(B16, 4, *strip), v(B16, 4, *strip),
        v(B16, 4, *strip), v(B16, 4, *strip), v(B16, 3, *strip), v(B16, 3, *strip),
        v(B16, 4, *units), v(B16, 4, *units), v(B16, 3, *units), v(B16, 3, *units),
        v(F32, N_FAR, 16, width), v(F32, 3, 16, width), v(F32, 2, 8, width), v(F32, 2, 8, width),
    ]
    scratch += [v(B16, channels, cells), v(B16, channels, cells), dma((2,))]
    pairs = [(2,), (3,), (2, 4), (2, 4), (2, 3, 2), (2, 3, 2), (2, 3), (2,), None, (3,), (2, 3), (2, 3), (2, 4)]
    pairs += [(2, 4), (2, 3), (2, 3), (3,), None]
    for p in pairs:
        scratch += [dma if p is None else dma(p)] * 2
    shapes = [
        jax.ShapeDtypeStruct((channels, cells), B16),
        jax.ShapeDtypeStruct((channels, cells), B16),
        jax.ShapeDtypeStruct((rows, width), F32),
        jax.ShapeDtypeStruct((rows, width), F32),
    ]
    made = pl.pallas_call(
        functools.partial(block_kernel, rows, width),
        out_shape=shapes,
        in_specs=[pl.BlockSpec(memory_space=pl.ANY)] * 2 + [vmem] * 9,
        out_specs=[vmem] * 4,
        scratch_shapes=scratch,
        compiler_params=pltpu.CompilerParams(
            collective_id=0, has_side_effects=True, vmem_limit_bytes=56 * 1024 * 1024
        ),
    )(
        tiles, cotangent, land, kernel, norm_gain, layer_scale,
        jnp.transpose(neighbors, (1, 2, 0)), jnp.transpose(shifts, (1, 2, 0)), halo_widths.T, w_up, w_down,
    )
    return pl.pallas_call(
        hand_over,
        out_shape=shapes,
        in_specs=[vmem] * 4,
        out_specs=[vmem] * 4,
    )(*made)


def solution(mesh):
    return jax.shard_map(
        per_device,
        mesh=mesh,
        in_specs=(
            P("fsdp", "dp"),
            P(None, "fsdp"),
            P("fsdp"),
            P("dp", "fsdp"),
            P("dp", "fsdp"),
            P("fsdp"),
            P("dp", None, None),
            P("dp", None, None),
            P("dp", None),
            P("dp", None, None),
            P("fsdp", "dp"),
        ),
        out_specs=(P("fsdp", "dp"), P("fsdp", "dp"), P("dp", "fsdp"), P("dp", "fsdp")),
        check_vma=False,
    )
```

```python
import functools
import math

import jax
import jax.numpy as jnp
from jax import lax
from jax.experimental import pallas as pl
from jax.experimental.pallas import tpu as pltpu
from jax.sharding import PartitionSpec as P

root_half = 1.0 / math.sqrt(2.0)
root_tau = 1.0 / math.sqrt(2.0 * math.pi)

N_Z, N_Y, N_CORE, N_X = 16, 4, 2, 4
N_FAR, N_NEAR = 4, 4
N_DP = N_Z * N_Y * N_CORE
MESH = pl.DeviceIdType.MESH
F32, B16 = jnp.float32, jnp.bfloat16
SIDE, TILE, TAPS = 8, 8, 7
HALF_ROWS = 256


def dp_index(z, y, core):
    return (z * N_Y + y) * N_CORE + core


def dot(a, b):
    return jnp.dot(a, b, preferred_element_type=F32)


def dot_nt(a, b):
    return lax.dot_general(a, b, (((1,), (1,)), ((), ())), preferred_element_type=F32)


def dot_tn(a, b):
    return lax.dot_general(a, b, (((0,), (0,)), ((), ())), preferred_element_type=F32)


def block_kernel(
    rows, width,
    x_ref, cot_ref, land_ref, taps_ref, gain_ref, scale_ref, owner_ref, shift_ref, depth_ref, up_ref, down_ref,
    block_ref, grad_ref, up_grad_ref, down_grad_ref,
    perm, order, picks, taps, xt, go, east_in, west_in, pad, gains,
    gma, gmb, cva, cvb, cen, inv, nrm, gmx, hid, gpre,
    pga, pgb, pgin_a, pgin_b, pgre_a, pgre_b, mxa, mxb, mxin_a, mxin_b, mxre_a, mxre_b, sums, sums_in, sum_cols,
    gcv, gpad, ret_w, ret_e, ret_w_in, ret_e_in, tg,
    unit_in, wfar, wone_a, wone_b, wtwo_a, wtwo_b, dense,
    st_a, st_b, st_in_a, st_in_b, one_a, one_b, one_in_a, one_in_b, two_a, two_b, two_in_a, two_in_b,
    fsum, f_in, last, last_in,
    x_in, cot_in, in_sem, halo_s, halo_r, gain_s, gain_r, gm_s, gm_r, cv_s, cv_r, pg_s, pg_r, mx_s, mx_r, sum_s, sum_r,
    ret_s, ret_r, wsib_s, wsib_r, wfar_s, wfar_r, wone_s, wone_r, wtwo_s, wtwo_r, wsh_s, wsh_r,
    gsib_s, gsib_r, gone_s, gone_r, gtwo_s, gtwo_r, gfar_s, gfar_r, gend_s, gend_r,
):
    channels = x_ref.shape[0]
    low, high = 128, channels - 128
    cells = x_ref.shape[1]
    me = lax.axis_index("dp")
    x = lax.axis_index("fsdp")
    z, y, core = me // (N_Y * N_CORE), (me // N_CORE) % N_Y, me % N_CORE
    far, near = z // N_NEAR, z % N_NEAR
    east, west = (me + 1) % N_DP, (me + N_DP - 1) % N_DP
    sibling = dp_index(z, y, 1 - core)

    def at_z(step):
        return dp_index((z + step + N_Z) % N_Z, y, core)

    def at_y(k):
        return dp_index(z, (y + k) % N_Y, core)

    def copy(src, dst, send, recv, dp, fs=None):
        return pltpu.make_async_remote_copy(
            src_ref=src, dst_ref=dst, send_sem=send, recv_sem=recv,
            device_id=(dp, x if fs is None else fs), device_id_type=MESH,
        )

    barrier = pltpu.get_barrier_semaphore()
    greeted = [(east, x), (west, x), (sibling, x)]
    greeted += [(me, (x + k) % N_X) for k in range(1, N_X)]
    greeted += [(at_z(s), x) for s in (4, 8, 12, 1, -1, 2, -2)]
    greeted += [(at_y(k), x) for k in range(1, N_Y)]
    for other in greeted:
        pl.semaphore_signal(barrier, inc=1, device_id=other, device_id_type=MESH)
    x_load = pltpu.make_async_copy(x_ref, x_in, in_sem.at[0])
    cot_load = pltpu.make_async_copy(cot_ref, cot_in, in_sem.at[1])
    x_load.start()
    cot_load.start()

    out_cell = lax.broadcasted_iota(jnp.int32, (cells, cells), 0)
    in_cell = lax.broadcasted_iota(jnp.int32, (cells, cells), 1)
    wanted = (out_cell % 8) * 64 + ((out_cell // 8) % 8) * 8 + out_cell // 64
    perm[...] = jnp.where(in_cell == wanted, 1.0, 0.0).astype(B16)
    x_load.wait()
    xt[...] = dot_nt(perm[...], x_in[...]).astype(B16)
    cot_load.wait()
    j_row = lax.broadcasted_iota(jnp.int32, (SIDE, cells), 0)
    j_col = lax.broadcasted_iota(jnp.int32, (SIDE, cells), 1)
    spread_j = jnp.where(j_row == j_col % SIDE, 1.0, 0.0).astype(B16)
    land = land_ref[...].astype(F32).reshape(TILE * SIDE, SIDE).astype(B16)
    ti_row = lax.broadcasted_iota(jnp.int32, (TILE * SIDE, cells), 0)
    ti_col = lax.broadcasted_iota(jnp.int32, (TILE * SIDE, cells), 1)
    land_row = jnp.sum(
        jnp.where(ti_row == ti_col // SIDE, dot(land, spread_j), 0.0), axis=0, keepdims=True
    ).astype(B16)
    go[...] = dot_nt(perm[...], cot_in[...] * land_row).astype(B16)
    scale_row = scale_ref[...].astype(F32).reshape(1, channels)
    grad_mixed = (go[...].astype(F32) * scale_row).astype(B16)
    gma[x] = grad_mixed[:, :low]
    gmb[x] = jnp.concatenate([grad_mixed[:HALF_ROWS, low:], grad_mixed[HALF_ROWS:, low:]], axis=1)
    gains[x] = jnp.broadcast_to(gain_ref[...].astype(F32).reshape(1, channels), (8, channels))
    s_row = lax.broadcasted_iota(jnp.int32, (16, rows), 0)
    s_col = lax.broadcasted_iota(jnp.int32, (16, rows), 1)
    unit_in[core] = (
        dot(jnp.where(s_row == s_col, 1.0, 0.0).astype(B16), up_ref[...])
        + dot(jnp.where(s_row == s_col + 8, 1.0, 0.0).astype(B16), down_ref[...])
    ).astype(B16)

    pl.semaphore_wait(barrier, len(greeted))

    halo_west = copy(xt.at[pl.ds(0, 192)], east_in, halo_s.at[0], halo_r.at[0], west)
    halo_east = copy(xt.at[pl.ds(cells - 192, 192)], west_in, halo_s.at[1], halo_r.at[1], east)
    halo_west.start()
    halo_east.start()
    wsib = copy(unit_in.at[core], unit_in.at[core], wsib_s, wsib_r, sibling)
    wsib.start()

    right, left, across = (x + 1) % N_X, (x + N_X - 1) % N_X, (x + 2) % N_X

    def gather_first(buffer, send, recv):
        return [
            copy(buffer.at[x], buffer.at[x], send.at[0], recv.at[0], me, right),
            copy(buffer.at[x], buffer.at[x], send.at[1], recv.at[1], me, left),
        ]

    def gather_next(buffer, send, recv):
        count = buffer.shape[1] // 2
        head, tail = pl.ds(0, count), pl.ds(count, count)
        return [
            copy(buffer.at[left, head], buffer.at[left, head], send.at[2], recv.at[2], me, right),
            copy(buffer.at[right, tail], buffer.at[right, tail], send.at[3], recv.at[3], me, left),
        ]

    def forward(first, later):
        for c, n in zip(first, later):
            c.wait_recv()
            n.start()

    gain_copies = []
    for k in range(1, N_X):
        gain_copies.append(
            copy(gains.at[x], gains.at[x], gain_s.at[k - 1], gain_r.at[k - 1], me, (x + k) % N_X)
        )
    gm_first = gather_first(gma, gm_s.at[0], gm_r.at[0]), gather_first(gmb, gm_s.at[1], gm_r.at[1])
    gm_next = gather_next(gma, gm_s.at[0], gm_r.at[0]), gather_next(gmb, gm_s.at[1], gm_r.at[1])
    for c in gm_first[0] + gm_first[1] + gain_copies:
        c.start()

    def scatter_copies(held, came, relay, send, recv, half):
        toward, away = (right, left) if half == 0 else (left, right)
        made = []
        for p in range(2):
            count = held[p].shape[1] // 2
            part = pl.ds(half * count, count)
            made.append((
                copy(held[p].at[across, part], relay[p].at[half], send.at[half, 0, p], recv.at[half, 0, p], me, toward),
                copy(
                    held[p].at[away, part], came[p].at[1 - half, part], send.at[half, 1, p], recv.at[half, 1, p], me, away
                ),
                copy(
                    held[p].at[toward, part], came[p].at[half, part], send.at[half, 2, p], recv.at[half, 2, p], me, toward
                ),
            ))
        return made

    def relay_on(held, relay, made, half):
        toward = right if half == 0 else left
        for p in range(2):
            count = held[p].shape[1] // 2
            part = pl.ds(half * count, count)
            made[p][0].wait_recv()
            held[p][toward, part] = (held[p][toward, part].astype(F32) + relay[p][half].astype(F32)).astype(B16)
            made[p][2].start()

    pg_made = [scatter_copies((pga, pgb), (pgin_a, pgin_b), (pgre_a, pgre_b), pg_s, pg_r, h) for h in range(2)]
    mx_made = [scatter_copies((mxa, mxb), (mxin_a, mxin_b), (mxre_a, mxre_b), mx_s, mx_r, h) for h in range(2)]

    edge_row = lax.broadcasted_iota(jnp.int32, (64, 64), 0)
    for face in range(4):
        chosen = jnp.zeros((64, 64), F32)
        for entry in range(2):
            owner = owner_ref[face, entry : entry + 1, :]
            shift = shift_ref[face, entry : entry + 1, :]
            target = jnp.where(owner >= 0, owner % TILE + TILE * shift, -4096)
            target = jnp.concatenate([target + TILE * p for p in range(SIDE)], axis=1)
            chosen = chosen + jnp.where(target == edge_row, 1.0, 0.0)
        widths = jnp.concatenate([depth_ref[face : face + 1, :]] * SIDE, axis=1)
        for layer in range(3):
            depth = 3 - layer if face in (0, 2) else layer + 1
            picks[face * 3 + layer] = jnp.where(widths >= depth, chosen, 0.0).astype(B16)

    kernel_taps = taps_ref[...].astype(F32)
    for a in range(TAPS):
        for b in range(TAPS):
            k = a * TAPS + b
            taps[b, a] = jnp.broadcast_to(kernel_taps[k : k + 1], (8, channels))

    pad[...] = jnp.zeros_like(pad)
    cells_f = xt[...].astype(F32).reshape(SIDE, SIDE, TILE, channels)
    pad[3 : 3 + SIDE, 3 : 3 + SIDE] = cells_f
    for layer in range(3):
        north = cells_f[:, 5 + layer].reshape(64, channels).astype(B16)
        south = cells_f[:, layer].reshape(64, channels).astype(B16)
        pad[3 : 3 + SIDE, layer] = dot_tn(picks[layer], north).astype(B16).astype(F32).reshape(SIDE, TILE, channels)
        pad[3 : 3 + SIDE, 11 + layer] = (
            dot_tn(picks[3 + layer], south).astype(B16).astype(F32).reshape(SIDE, TILE, channels)
        )

    wsib.wait_recv()
    both = unit_in[...].reshape(N_CORE * 16, width)
    u_row = lax.broadcasted_iota(jnp.int32, (16, N_CORE * 16), 0)
    u_col = lax.broadcasted_iota(jnp.int32, (16, N_CORE * 16), 1)
    first = (u_row < rows) & (u_col == u_row + 8 * core)
    second = (u_row >= rows) & (u_row < 2 * rows) & (u_col == 16 + u_row - rows + 8 * core)
    joined = dot(jnp.where(first | second, 1.0, 0.0).astype(B16), both).astype(B16)
    wfar[far] = joined

    def far_copy(k):
        place = wfar.at[far]
        return copy(place, place, wfar_s.at[k - 1], wfar_r.at[k - 1], at_z(4 * k))

    for k in range(1, N_FAR):
        far_copy(k).start()

    halo_west.wait_recv()
    halo_east.wait_recv()
    for layer in range(3):
        part = pl.ds(layer * 64, 64)
        pad[layer, 3 : 3 + SIDE] = (
            dot_tn(picks[6 + layer], west_in[part]).astype(B16).astype(F32).reshape(SIDE, TILE, channels)
        )
        pad[11 + layer, 3 : 3 + SIDE] = (
            dot_tn(picks[9 + layer], east_in[part]).astype(B16).astype(F32).reshape(SIDE, TILE, channels)
        )

    def conv_column(j, start, size):
        total = jnp.zeros((SIDE, TILE, size), F32)
        for b in range(TAPS):
            source = pad[j + b, :, :, start : start + size]
            for a in range(TAPS):
                total = total + source[a : a + SIDE] * taps[b, a, :, start : start + size][None]
        return total.reshape(64, size).astype(B16)

    def conv_low(j, carry):
        cva[x, pl.ds(pl.multiple_of(j * 64, 64), 64)] = conv_column(j, 0, low)
        return carry

    def conv_high(j, carry):
        cvb[x, pl.ds(pl.multiple_of(j * 64, 64), 64)] = jnp.concatenate(
            [conv_column(j, low, high), conv_column(j + 4, low, high)], axis=1
        )
        return carry

    lax.fori_loop(0, SIDE, conv_low, 0)
    cv_first = gather_first(cva, cv_s.at[0], cv_r.at[0])
    cv_next = gather_next(cva, cv_s.at[0], cv_r.at[0])
    for c in cv_first:
        c.start()

    for k in range(1, N_FAR):
        far_copy(k).wait_recv()

    near_steps = (1, -1, -2)

    def one_copies():
        made = []
        for k in range(3):
            made.append(
                copy(wone_a.at[near], wone_a.at[near], wone_s.at[0, k], wone_r.at[0, k], at_z(near_steps[k]))
            )
            made.append(copy(wone_b.at[y], wone_b.at[y], wone_s.at[1, k], wone_r.at[1, k], at_y(k + 1)))
        return made

    wone_a[near] = wfar[0:2]
    wone_b[y] = wfar[2:4]
    for c in one_copies():
        c.start()

    lax.fori_loop(0, 4, conv_high, 0)
    high_first = gather_first(cvb, cv_s.at[1], cv_r.at[1])
    high_next = gather_next(cvb, cv_s.at[1], cv_r.at[1])
    for c in high_first:
        c.start()
    forward(gm_first[0], gm_next[0])
    forward(gm_first[1], gm_next[1])

    span = N_CORE * rows
    w_row = lax.broadcasted_iota(jnp.int32, (256, channels), 0)
    w_col = lax.broadcasted_iota(jnp.int32, (256, channels), 1)
    w_from = ((w_row // span) % N_Y) * (span * N_NEAR) + (w_row // (span * N_Y)) * span + w_row % span
    order[...] = jnp.where((w_col == w_from) & (w_row < channels), 1.0, 0.0).astype(B16)
    p_row = lax.broadcasted_iota(jnp.int32, (4 * span, 64), 0)
    p_col = lax.broadcasted_iota(jnp.int32, (4 * span, 64), 1)
    close = jnp.where(p_col == (p_row // span) * 16 + p_row % span, 1.0, 0.0).astype(B16)
    gap_row = lax.broadcasted_iota(jnp.int32, (64, 4 * span), 0)
    gap_col = lax.broadcasted_iota(jnp.int32, (64, 4 * span), 1)
    reopen = jnp.where(gap_row == (gap_col // span) * 16 + gap_col % span, 1.0, 0.0).astype(B16)

    def two_copies():
        made = []
        for k in range(3):
            place = wtwo_a.at[core, y]
            made.append(copy(place, place, wtwo_s.at[0, k], wtwo_r.at[0, k], at_y(k + 1)))
            place = wtwo_b.at[core, near]
            made.append(copy(place, place, wtwo_s.at[1, k], wtwo_r.at[1, k], at_z(near_steps[k])))
        return made

    def share_a(k):
        place = wtwo_a.at[core, (y + N_Y - k) % N_Y]
        return copy(place, place, wsh_s.at[0, k], wsh_r.at[0, k], sibling)

    def share_b(k):
        step = 0 if k == 0 else near_steps[k - 1]
        place = wtwo_b.at[core, (near - step + N_NEAR) % N_NEAR]
        return copy(place, place, wsh_s.at[1, k], wsh_r.at[1, k], sibling)

    for c in one_copies():
        c.wait_recv()
    for f in range(2):
        rows_a = jnp.concatenate([wone_a[nn, f] for nn in range(N_NEAR)], axis=0)
        wtwo_a[core, y, f] = dot(close, rows_a).astype(B16)
        rows_b = jnp.concatenate([wone_b[yy, f] for yy in range(N_Y)], axis=0)
        wtwo_b[core, near, f] = dot(close, rows_b).astype(B16)
    for c in two_copies():
        c.start()
    share_a(0).start()
    share_b(0).start()

    forward(cv_first, cv_next)
    forward(high_first, high_next)
    for c in gm_next[0] + gm_next[1]:
        c.wait_recv()
    for b in range(N_X):
        gap = jnp.zeros((cells, 256 - channels), B16)
        nrm[:, b * 256 + channels : (b + 1) * 256] = gap
        gmx[:, b * 256 + channels : (b + 1) * 256] = gap
        gmx[:, b * 256 : b * 256 + low] = gma[b]
        packed = gmb[b]
        gmx[:HALF_ROWS, b * 256 + low : b * 256 + channels] = packed[:, :high]
        gmx[HALF_ROWS:, b * 256 + low : b * 256 + channels] = packed[:, high:]

    for c in gain_copies + cv_next + high_next:
        c.wait_recv()

    wide = float(channels * N_X)
    for half in range(2):

        def norm_rows(i, carry, half=half):
            part = pl.ds(pl.multiple_of(i * 64, 64), 64)
            here = pl.ds(pl.multiple_of(half * HALF_ROWS + i * 64, 64), 64)
            lows = [cva[b, here].astype(F32) for b in range(N_X)]
            highs = [cvb[b, part, half * high : (half + 1) * high].astype(F32) for b in range(N_X)]
            total = jnp.sum(sum(lows), axis=1, keepdims=True) + jnp.sum(sum(highs), axis=1, keepdims=True)
            square = jnp.sum(sum(v * v for v in lows), axis=1, keepdims=True) + jnp.sum(
                sum(v * v for v in highs), axis=1, keepdims=True
            )
            mean = total / wide
            scale = lax.rsqrt(square / wide - mean * mean + 1e-06)
            inv[here] = jnp.broadcast_to(scale, (64, 128))
            for b in range(N_X):
                centered = (lows[b] - mean) * scale
                cen[b, here, 0:low] = centered
                nrm[here, b * 256 : b * 256 + low] = (centered * gains[b, 0:1, 0:low]).astype(B16)
                centered = (highs[b] - mean) * scale
                cen[b, here, low:channels] = centered
                nrm[here, b * 256 + low : b * 256 + channels] = (
                    centered * gains[b, 0:1, low:channels]
                ).astype(B16)
            return carry

        lax.fori_loop(0, 4, norm_rows, 0)
        if half == 0:
            arrived = two_copies()
            for k in range(1, 4):
                arrived[2 * k - 2].wait_recv()
                share_a(k).start()
                arrived[2 * k - 1].wait_recv()
                share_b(k).start()

    for k in range(4):
        share_a(k).wait_recv()
        share_b(k).wait_recv()
    for m in range(2):
        for f in range(2):
            rows_a = jnp.concatenate([wtwo_a[m, yy, f] for yy in range(N_Y)], axis=0)
            dense[m, f * 256 : (f + 1) * 256] = dot(order[...], rows_a).astype(B16)
            for nn in range(N_NEAR):
                r = (f + 2) * 256 + nn * 4 * span
                dense[m, r : r + 4 * span] = wtwo_b[m, nn, f]
            dense[m, (f + 2) * 256 + channels : (f + 3) * 256] = jnp.zeros((256 - channels, width), B16)

    sum_copies = []
    for half in range(2):
        for i in range(2):
            start = half * HALF_ROWS + i * 128
            here = slice(start, start + 128)
            part = slice(half * 128, half * 128 + 128)
            pre = dot(nrm[here], dense[0])
            edge = 0.5 * (1.0 + lax.erf(pre * root_half))
            hid[here] = (pre * edge).astype(B16)
            slope = edge + pre * jnp.exp(-0.5 * pre * pre) * root_tau
            grad_pre = (dot(gmx[here], dense[1]) * slope).astype(B16)
            gpre[here] = grad_pre
            back = dot_nt(grad_pre, dense[0]).astype(B16)
            first_sum = jnp.zeros((128, 128), F32)
            second_sum = jnp.zeros((128, 128), F32)
            first_high = jnp.zeros((128, high), F32)
            second_high = jnp.zeros((128, high), F32)
            for b in range(N_X):
                low_part = back[:, b * 256 : b * 256 + low]
                high_part = back[:, b * 256 + low : b * 256 + channels]
                pga[b, here] = low_part
                pgb[b, part, i * high : (i + 1) * high] = high_part
                g = low_part.astype(F32) * gains[b, 0:1, 0:low]
                first_sum += g
                second_sum += g * cen[b, here, 0:low]
                g = high_part.astype(F32) * gains[b, 0:1, low:channels]
                first_high += g
                second_high += g * cen[b, here, low:channels]
            one = jnp.sum(first_sum, axis=1, keepdims=True) + jnp.sum(first_high, axis=1, keepdims=True)
            two = jnp.sum(second_sum, axis=1, keepdims=True) + jnp.sum(second_high, axis=1, keepdims=True)
            lane = lax.broadcasted_iota(jnp.int32, (128, 128), 1)
            columns = jnp.where(lane == 0, one, jnp.where(lane == 1, two, 0.0))
            sums[half, i] = jnp.transpose(columns)[0:8]
        made = []
        for k in range(1, N_X):
            other = (x + k) % N_X
            made.append(
                copy(sums.at[half], sums_in.at[k - 1, half], sum_s.at[half, k - 1], sum_r.at[half, k - 1], me, other)
            )
        for p in range(2):
            pg_made[half][p][0].start()
        for p in range(2):
            pg_made[half][p][1].start()
        for c in made:
            c.start()
        sum_copies.append(made)

    back_steps = (-1, 1, 2)

    def one_place(k):
        step = 0 if k == 0 else back_steps[k - 1]
        return (y + k) % N_Y, (near + step + N_NEAR) % N_NEAR

    def gsib_copies(k):
        yy, nn = one_place(k)
        return (
            copy(st_a.at[1 - core, yy], st_in_a.at[yy], gsib_s.at[0, k], gsib_r.at[0, k], sibling),
            copy(st_b.at[1 - core, nn], st_in_b.at[nn], gsib_s.at[1, k], gsib_r.at[1, k], sibling),
        )

    for b in range(N_X):
        for m, inner, outer in ((0, nrm, gpre), (1, gmx, hid)):
            local = dot_tn(inner[:, b * 256 : (b + 1) * 256], outer[...]).astype(B16)
            if b < 2:
                local = dot_tn(order[...], local).astype(B16)
            for q in range(4):
                r = q * 4 * span
                if b < 2:
                    st_a[m, q, b] = local[r : r + 4 * span]
                else:
                    st_b[m, q, b - 2] = local[r : r + 4 * span]

        if b % 2 == 1:
            for k in (1, 2, 3, 0):
                gsib_copies(k)[b // 2].start()
        if b == 1:
            relay_on((pga, pgb), (pgre_a, pgre_b), pg_made[0], 0)

    relay_on((pga, pgb), (pgre_a, pgre_b), pg_made[1], 1)

    def gone_copies(k):
        return (
            copy(one_a.at[k], one_in_a.at[k - 1], gone_s.at[0, k - 1], gone_r.at[0, k - 1], at_y(k)),
            copy(
                one_b.at[k], one_in_b.at[k - 1], gone_s.at[1, k - 1], gone_r.at[1, k - 1], at_z(back_steps[k - 1])
            ),
        )

    for k in (1, 2, 3, 0):
        yy, nn = one_place(k)
        over_y, over_z = gsib_copies(k)
        over_y.wait_recv()
        one_a[k] = (st_a[core, yy].astype(F32) + st_in_a[yy].astype(F32)).astype(B16)
        if k > 0:
            to_y, to_z = gone_copies(k)
            to_y.start()
        over_z.wait_recv()
        one_b[k] = (st_b[core, nn].astype(F32) + st_in_b[nn].astype(F32)).astype(B16)
        if k > 0:
            to_z.start()

    for half in range(2):
        for i in range(2):
            start = half * HALF_ROWS + i * 128
            mixed = dot_nt(hid[start : start + 128], dense[1]).astype(B16)
            for b in range(N_X):
                mxa[b, start : start + 128] = mixed[:, b * 256 : b * 256 + low]
                mxb[b, half * 128 : half * 128 + 128, i * high : (i + 1) * high] = mixed[
                    :, b * 256 + low : b * 256 + channels
                ]
        for p in range(2):
            mx_made[half][p][0].start()
            mx_made[half][p][1].start()

    gcv[...] = jnp.zeros_like(gcv)
    for half in range(2):
        for c in sum_copies[half]:
            c.wait_recv()
        for p in range(2):
            pg_made[half][p][1].wait_recv()
            pg_made[half][p][2].wait_recv()
        for i in range(2):
            total = sums[half, i]
            for k in range(N_X - 1):
                total = total + sums_in[k, half, i]
            spread = jnp.concatenate([total / wide, jnp.zeros((120, 128), F32)], axis=0)
            sum_cols[...] = jnp.transpose(spread)
            lanes = slice(i * high, (i + 1) * high)

            def back_rows(n, carry, half=half, i=i, lanes=lanes):
                column = half * 4 + i * 2 + n
                part = pl.ds(pl.multiple_of(half * 128 + n * 64, 64), 64)
                here = pl.ds(pl.multiple_of(column * 64, 64), 64)
                low_part = pga[x, here].astype(F32)
                high_part = pgb[x, part, lanes].astype(F32)
                for k in range(2):
                    low_part = low_part + pgin_a[k, here].astype(F32)
                    high_part = high_part + pgin_b[k, part, lanes].astype(F32)
                local = pl.ds(pl.multiple_of(n * 64, 64), 64)
                e1 = sum_cols[local, 0:1]
                e2 = sum_cols[local, 1:2]
                scale = inv[here]
                g = low_part * gains[x, 0:1, 0:low]
                g = scale * (g - e1 - cen[x, here, 0:low] * e2)
                gcv[column, :, :, 0:low] = g.astype(B16).astype(F32).reshape(SIDE, TILE, low)
                g = high_part * gains[x, 0:1, low:channels]
                g = scale[:, :high] * (g - e1 - cen[x, here, low:channels] * e2)
                gcv[column, :, :, low:channels] = g.astype(B16).astype(F32).reshape(SIDE, TILE, high)
                return carry

            lax.fori_loop(0, 2, back_rows, 0)

    def spread_column(j, start, size):
        def add_tap(b, totals):
            totals = list(totals)
            source = gcv[j - b, :, :, start : start + size]
            for a in range(TAPS):
                tap = taps[b, a, :, start : start + size]
                for i in range(SIDE):
                    totals[i + a] = totals[i + a] + source[i] * tap
            return tuple(totals)

        empty = tuple(jnp.zeros((TILE, size), F32) for _ in range(SIDE + 6))
        first_tap = jnp.maximum(0, j - (SIDE - 1))
        end_tap = jnp.minimum(TAPS, j + 1)
        totals = lax.fori_loop(first_tap, end_tap, add_tap, empty)
        for i in range(SIDE + 6):
            gpad[j, i, :, start : start + size] = totals[i]

    def spread_edge(j, carry):
        for k in (j, j + 11):
            spread_column(k, 0, low)
            spread_column(k, low, high)
        return carry

    def spread_inner(j, carry):
        spread_column(j, 0, low)
        spread_column(j, low, high)
        return carry

    def gtwo_copies(k):
        yy, nn = one_place(k)
        return (
            copy(two_a.at[nn], two_in_a.at[k - 1], gtwo_s.at[0, k - 1], gtwo_r.at[0, k - 1], at_z(back_steps[k - 1])),
            copy(two_b.at[yy], two_in_b.at[k - 1], gtwo_s.at[1, k - 1], gtwo_r.at[1, k - 1], at_y(k)),
        )

    for k in range(1, 4):
        for c in gone_copies(k):
            c.wait_recv()
    for f in range(2):
        for mine, came, units in ((one_a, one_in_a, two_a), (one_b, one_in_b, two_b)):
            total = mine[0, f].astype(F32)
            for k in range(3):
                total = total + came[k, f].astype(F32)
            opened = dot(reopen, total.astype(B16)).astype(B16)
            for q in range(4):
                units[q, f] = opened[q * 16 : (q + 1) * 16]
    for k in range(1, 4):
        for c in gtwo_copies(k):
            c.start()

    lax.fori_loop(0, 3, spread_edge, 0)
    for layer in range(3):
        part = pl.ds(layer * 64, 64)
        for face, column, held in ((2, layer, ret_w), (3, 11 + layer, ret_e)):
            edge = gpad[column, 3 : 3 + SIDE].reshape(64, channels).astype(B16)
            held[part] = dot(picks[face * 3 + layer], edge).astype(B16)
    ret_west = copy(ret_w, ret_w_in, ret_s.at[0], ret_r.at[0], west)
    ret_east = copy(ret_e, ret_e_in, ret_s.at[1], ret_r.at[1], east)
    ret_west.start()
    ret_east.start()

    for half in range(2):
        relay_on((mxa, mxb), (mxre_a, mxre_b), mx_made[half], half)
    lax.fori_loop(3, 11, spread_inner, 0)

    for k in range(1, 4):
        for c in gtwo_copies(k):
            c.wait_recv()
    total = two_a[near].astype(F32)
    other_total = two_b[y].astype(F32)
    for k in range(3):
        total = total + two_in_a[k].astype(F32)
        other_total = other_total + two_in_b[k].astype(F32)
    fsum[0:2] = total
    fsum[2:4] = other_total

    def gfar_copy(k):
        return copy(
            fsum.at[(far + k) % N_FAR], f_in.at[k - 1], gfar_s.at[k - 1], gfar_r.at[k - 1], at_z(4 * k)
        )

    for k in range(1, N_FAR):
        gfar_copy(k).start()

    tg[...] = go[...].astype(F32).reshape(SIDE, SIDE, TILE, channels) + gpad[3 : 3 + SIDE, 3 : 3 + SIDE]
    for layer in range(3):
        for face, row, target in ((0, layer, 5 + layer), (1, 11 + layer, layer)):
            edge = gpad[3 : 3 + SIDE, row].reshape(64, channels).astype(B16)
            back = dot(picks[face * 3 + layer], edge)
            tg[:, target] = tg[:, target] + back.reshape(SIDE, TILE, channels)

    ret_west.wait_recv()
    ret_east.wait_recv()
    for layer in range(3):
        part = pl.ds(layer * 64, 64)
        tg[5 + layer] = tg[5 + layer] + ret_w_in[part].astype(F32).reshape(SIDE, TILE, channels)
        tg[layer] = tg[layer] + ret_e_in[part].astype(F32).reshape(SIDE, TILE, channels)
    grad_ref[...] = dot_tn(tg[...].reshape(cells, channels).astype(B16), perm[...]).astype(B16)

    for half in range(2):
        for p in range(2):
            mx_made[half][p][1].wait_recv()
            mx_made[half][p][2].wait_recv()
    low_part = mxa[x].astype(F32)
    packed = mxb[x].astype(F32)
    for k in range(2):
        low_part = low_part + mxin_a[k].astype(F32)
        packed = packed + mxin_b[k].astype(F32)
    tops, ends = packed[:128], packed[128:]
    high_part = jnp.concatenate([tops[:, :high], tops[:, high:], ends[:, :high], ends[:, high:]], axis=0)
    mixed = jnp.concatenate([low_part, high_part], axis=1)
    out = (xt[...].astype(F32) + scale_row * mixed).astype(B16)
    block_ref[...] = dot_tn(out, perm[...]).astype(B16)

    for k in range(1, N_FAR):
        gfar_copy(k).wait_recv()
    total = fsum[far]
    for k in range(1, N_FAR):
        total = total + f_in[k - 1]
    last[0, 0:8] = total[0:8]
    last[1, 0:8] = total[rows : rows + 8]
    gend = copy(last.at[1 - core], last_in.at[core], gend_s, gend_r, sibling)
    gend.start()
    last_in[core] = last[core]

    gend.wait_recv()
    up_grad_ref[...] = last_in[0, 0:rows]
    down_grad_ref[...] = last_in[1, 0:rows]

    sent = [halo_west, halo_east, wsib, ret_west, ret_east, gend]
    sent += gain_copies + gm_first[0] + gm_first[1] + gm_next[0] + gm_next[1]
    sent += cv_first + cv_next + high_first + high_next + sum_copies[0] + sum_copies[1]
    for made in pg_made + mx_made:
        sent += made[0] + made[1]
    sent += [far_copy(k) for k in range(1, N_FAR)] + one_copies() + two_copies()
    sent += [share_a(k) for k in range(4)] + [share_b(k) for k in range(4)]
    for k in range(4):
        sent += gsib_copies(k)
    for k in range(1, 4):
        sent += gone_copies(k) + gtwo_copies(k)
    sent += [gfar_copy(k) for k in range(1, N_FAR)]
    for c in sent:
        c.wait_send()


def hand_over(*refs):
    for i in range(4):
        refs[4 + i][...] = refs[i][...]


def per_device(
    tiles, kernel, norm_gain, w_up, w_down, layer_scale, neighbors, shifts, halo_widths, land, cotangent
):
    channels, cells = tiles.shape
    rows, width = w_up.shape
    vmem = pl.BlockSpec(memory_space=pltpu.VMEM)
    dma = pltpu.SemaphoreType.DMA

    def v(dtype, *shape):
        return pltpu.VMEM(shape, dtype)

    strip = (2, 8 * rows, width)
    units = (2, 16, width)
    scratch = [
        v(B16, cells, cells), v(B16, 256, channels), v(B16, 12, 64, 64), v(F32, TAPS, TAPS, 8, channels),
        v(B16, cells, channels), v(B16, cells, channels), v(B16, 192, channels), v(B16, 192, channels),
        v(F32, SIDE + 6, SIDE + 6, TILE, channels), v(F32, N_X, 8, channels),
        v(B16, N_X, cells, 128), v(B16, N_X, HALF_ROWS, 128), v(B16, N_X, cells, 128), v(B16, N_X, HALF_ROWS, 128),
        v(F32, N_X, cells, channels), v(F32, cells, 128), v(B16, cells, N_X * 256), v(B16, cells, N_X * 256),
        v(B16, cells, width), v(B16, cells, width),
        v(B16, N_X, cells, 128), v(B16, N_X, HALF_ROWS, 128), v(B16, 2, cells, 128), v(B16, 2, HALF_ROWS, 128),
        v(B16, 2, HALF_ROWS, 128), v(B16, 2, 128, 128),
        v(B16, N_X, cells, 128), v(B16, N_X, HALF_ROWS, 128), v(B16, 2, cells, 128), v(B16, 2, HALF_ROWS, 128),
        v(B16, 2, HALF_ROWS, 128), v(B16, 2, 128, 128),
        v(F32, 2, 2, 8, 128), v(F32, 3, 2, 2, 8, 128), v(F32, 128, 128),
        v(F32, SIDE, SIDE, TILE, channels), v(F32, SIDE + 6, SIDE + 6, TILE, channels),
        v(B16, 192, channels), v(B16, 192, channels), v(B16, 192, channels), v(B16, 192, channels),
        v(F32, SIDE, SIDE, TILE, channels),
        v(B16, 2, 16, width), v(B16, N_FAR, 16, width), v(B16, 4, *units), v(B16, 4, *units),
        v(B16, 2, 4, *strip), v(B16, 2, 4, *strip), v(B16, 2, N_X * 256, width),
        v(B16, 2, 4, *strip), v(B16, 2, 4, *strip), v(B16, 4, *strip), v(B16, 4, *strip),
        v(B16, 4, *strip), v(B16, 4, *strip), v(B16, 3, *strip), v(B16, 3, *strip),
        v(B16, 4, *units), v(B16, 4, *units), v(B16, 3, *units), v(B16, 3, *units),
        v(F32, N_FAR, 16, width), v(F32, 3, 16, width), v(F32, 2, 8, width), v(F32, 2, 8, width),
    ]
    scratch += [v(B16, channels, cells), v(B16, channels, cells), dma((2,))]
    pairs = [(2,), (3,), (2, 4), (2, 4), (2, 3, 2), (2, 3, 2), (2, 3), (2,), None, (3,), (2, 3), (2, 3), (2, 4)]
    pairs += [(2, 4), (2, 3), (2, 3), (3,), None]
    for p in pairs:
        scratch += [dma if p is None else dma(p)] * 2
    shapes = [
        jax.ShapeDtypeStruct((channels, cells), B16),
        jax.ShapeDtypeStruct((channels, cells), B16),
        jax.ShapeDtypeStruct((rows, width), F32),
        jax.ShapeDtypeStruct((rows, width), F32),
    ]
    made = pl.pallas_call(
        functools.partial(block_kernel, rows, width),
        out_shape=shapes,
        in_specs=[pl.BlockSpec(memory_space=pl.ANY)] * 2 + [vmem] * 9,
        out_specs=[vmem] * 4,
        scratch_shapes=scratch,
        compiler_params=pltpu.CompilerParams(
            collective_id=0, has_side_effects=True, vmem_limit_bytes=56 * 1024 * 1024
        ),
    )(
        tiles, cotangent, land, kernel, norm_gain, layer_scale,
        jnp.transpose(neighbors, (1, 2, 0)), jnp.transpose(shifts, (1, 2, 0)), halo_widths.T, w_up, w_down,
    )
    return pl.pallas_call(
        hand_over,
        out_shape=shapes,
        in_specs=[vmem] * 4,
        out_specs=[vmem] * 4,
    )(*made)


def solution(mesh):
    return jax.shard_map(
        per_device,
        mesh=mesh,
        in_specs=(
            P("fsdp", "dp"),
            P(None, "fsdp"),
            P("fsdp"),
            P("dp", "fsdp"),
            P("dp", "fsdp"),
            P("fsdp"),
            P("dp", None, None),
            P("dp", None, None),
            P("dp", None),
            P("dp", None, None),
            P("fsdp", "dp"),
        ),
        out_specs=(P("fsdp", "dp"), P("fsdp", "dp"), P("dp", "fsdp"), P("dp", "fsdp")),
        check_vma=False,
    )
```
